256 devices in a mesh: seq: 16 (over z, y_lo), head: 16 (over y_hi, x, core).
Axes of the slice: x: 4, y: 4 (y_hi: 2, y_lo: 2; y = y_hi * 2 + y_lo), z: 8, core: 2. Of those that a mesh axis runs over, the one named last changes fastest.
Arguments:
- normed: bfloat16 [8192, 8192], P('seq', 'head'), may hold values from -6 to 6
- output_gradient: bfloat16 [8192, 8192], P('seq', 'head'), may hold values from -6 to 6
- query_weight: bfloat16 [8192, 4096], P(None, 'head'), may hold values from -0.0625 to 0.0625
- key_value_weight: bfloat16 [8192, 2, 512], P(None, None, 'head'), may hold values from -0.0625 to 0.0625
- output_weight: bfloat16 [4096, 8192], P('head'), may hold values from -0.09375 to 0.09375
- adapter_down: bfloat16 [3, 8, 8192], replicated, may hold values from -0.0625 to 0.0625
- query_up: bfloat16 [8, 4096], P(None, 'head'), may hold values from -0.5 to 0.5
- key_value_up: bfloat16 [8, 2, 512], P(None, None, 'head'), may hold values from -0.5 to 0.5
- output_down: bfloat16 [8, 4096], P(None, 'head'), may hold values from -0.09375 to 0.09375
- output_up: bfloat16 [8, 8192], P(None, 'head'), may hold values from -0.5 to 0.5
Outputs:
- normalized_gradient: bfloat16 [8192, 8192], P('seq', 'head')
- adapter_down_gradient: float32 [3, 8, 8192], replicated
- query_up_gradient: float32 [8, 4096], P(None, 'head')
- key_value_up_gradient: float32 [8, 2, 512], P(None, None, 'head')
- output_down_gradient: float32 [8, 4096], P(None, 'head')
- output_up_gradient: float32 [8, 8192], P(None, 'head')
The draws below stay inside these ranges and needn't reach their ends.
All inputs are finite; a program needn't handle non-finite values.
Results may differ from the reference program's by a relative error of at most 0.035.
Values may be sent and summed in bfloat16 or wider, within the bound.
A program may use at most 128 MiB of HBM per device.

```python
import math
import jax
import jax.numpy as jnp
from jax import lax

MODEL_WIDTH = 8192
QUERY_HEADS = 32
KEY_VALUE_HEADS = 4
HEAD_SIZE = 128
ADAPTER_RANK = 8
TOKENS_PER_PART = 512
TOKENS = 8192


def block_levels(key, extent, split, smallest, high):
    def one(position, shards_of):
        heights = jax.random.uniform(jax.random.fold_in(jax.random.fold_in(key, 6), position), (shards_of,), jnp.float32, smallest / len(split), high / len(split))
        return jnp.repeat(jnp.exp(heights), extent[position] // shards_of).reshape((-1,) + (1,) * (len(extent) - position - 1))

    gain = one(*split[0])
    for cut in split[1:]:
        gain = gain * one(*cut)
    return gain


def normal_values(own_key, extent, deviation, reach, cuts=(), kind=jnp.bfloat16):
    gain = block_levels(own_key, extent, cuts, -0.22, 0.18) if cuts else 1.0
    array = jax.random.normal(own_key, extent, jnp.float32) * deviation * gain
    return jnp.minimum(jnp.maximum(array, -reach), reach).astype(kind)


def setup_inputs(seed: int = 0) -> dict:
    key_list = jax.random.split(jax.random.key(seed), 11)
    return {
        "normed": normal_values(key_list[0], (TOKENS, MODEL_WIDTH), 1.0, 6.0, ((0, 16), (1, 16))),
        "output_gradient": normal_values(key_list[1], (TOKENS, MODEL_WIDTH), 1.0, 6.0, ((0, 16), (1, 16))),
        "query_weight": normal_values(key_list[2], (MODEL_WIDTH, QUERY_HEADS * HEAD_SIZE), MODEL_WIDTH ** -0.5, 0.0625, ((1, 16),)),
        "key_value_weight": normal_values(key_list[3], (MODEL_WIDTH, 2, KEY_VALUE_HEADS * HEAD_SIZE), MODEL_WIDTH ** -0.5, 0.0625, ((2, 16),)),
        "output_weight": normal_values(key_list[4], (QUERY_HEADS * HEAD_SIZE, MODEL_WIDTH), (QUERY_HEADS * HEAD_SIZE) ** -0.5, 0.09375, ((0, 16),)),
        "adapter_down": normal_values(key_list[5], (3, ADAPTER_RANK, MODEL_WIDTH), MODEL_WIDTH ** -0.5, 0.0625),
        "query_up": normal_values(key_list[6], (ADAPTER_RANK, QUERY_HEADS * HEAD_SIZE), (16 * ADAPTER_RANK) ** -0.5, 0.5, ((1, 16),)),
        "key_value_up": normal_values(key_list[7], (ADAPTER_RANK, 2, KEY_VALUE_HEADS * HEAD_SIZE), (16 * ADAPTER_RANK) ** -0.5, 0.5, ((2, 16),)),
        "output_down": normal_values(key_list[8], (ADAPTER_RANK, QUERY_HEADS * HEAD_SIZE), (QUERY_HEADS * HEAD_SIZE) ** -0.5, 0.09375, ((1, 16),)),
        "output_up": normal_values(key_list[9], (ADAPTER_RANK, MODEL_WIDTH), (16 * ADAPTER_RANK) ** -0.5, 0.5, ((1, 16),)),
    }


adapter_scale = 2.0
rope_base = 10000.0

def rope_tables(positions):
    half_dim = HEAD_SIZE // 2
    frequency = rope_base ** (-jnp.arange(half_dim, dtype=jnp.float32) * 2.0 / HEAD_SIZE)
    angles = positions.astype(jnp.float32)[:, None] * frequency[None, :]
    return (jnp.cos(angles), jnp.sin(angles))

def apply_rotation(values, cosine_rows, sine_rows):
    half_dim = HEAD_SIZE // 2
    front_half = values[..., :half_dim]
    back_half = values[..., half_dim:]
    cos_wide = cosine_rows[:, None, :]
    sin_wide = sine_rows[:, None, :]
    return jnp.concatenate([front_half * cos_wide - back_half * sin_wide, back_half * cos_wide + front_half * sin_wide], axis=-1)

def unrotate(gradient, cosine_rows, sine_rows):
    half_dim = HEAD_SIZE // 2
    front_half = gradient[..., :half_dim]
    back_half = gradient[..., half_dim:]
    cos_wide = cosine_rows[:, None, :]
    sin_wide = sine_rows[:, None, :]
    return jnp.concatenate([front_half * cos_wide + back_half * sin_wide, back_half * cos_wide - front_half * sin_wide], axis=-1)

def shift_heads(values, first_head, amount):
    moved = jnp.roll(values[:, first_head:], amount, axis=0)
    return jnp.concatenate([values[:, :first_head], moved], axis=1)

def group_probs(query_rows, keys_rows):
    members_per_group = QUERY_HEADS // KEY_VALUE_HEADS
    inv_root = 1.0 / math.sqrt(HEAD_SIZE)
    query_rows_wide = query_rows.reshape(TOKENS_PER_PART, KEY_VALUE_HEADS, members_per_group, HEAD_SIZE).astype(jnp.float32)
    scores = jnp.einsum('ikgd,jkd->kgij', query_rows_wide, keys_rows.astype(jnp.float32)) * inv_root
    causal = jnp.arange(TOKENS_PER_PART)[None, :] <= jnp.arange(TOKENS_PER_PART)[:, None]
    exp_scores = jnp.where(causal, jnp.exp(scores), 0.0)
    probs_full = exp_scores / lax.optimization_barrier(jnp.sum(exp_scores, axis=-1, keepdims=True))
    probs_low = lax.optimization_barrier(probs_full.astype(jnp.bfloat16)).astype(jnp.float32)
    return (query_rows_wide, probs_full, probs_low)

def attend_group(pieces):
    query_rows, keys_rows, values_rows = pieces
    query_rows_wide, probs_full, probs_low = group_probs(query_rows, keys_rows)
    attention_output = jnp.einsum('kgij,jkd->ikgd', probs_low, values_rows.astype(jnp.float32))
    return attention_output.reshape(TOKENS_PER_PART, QUERY_HEADS, HEAD_SIZE).astype(jnp.bfloat16)

def attend_back(pieces):
    query_rows, keys_rows, values_rows, gradient_rows = pieces
    members_per_group = QUERY_HEADS // KEY_VALUE_HEADS
    inv_root = 1.0 / math.sqrt(HEAD_SIZE)
    query_rows_wide, probs_full, probs_low = group_probs(query_rows, keys_rows)
    gradient_wide = gradient_rows.reshape(TOKENS_PER_PART, KEY_VALUE_HEADS, members_per_group, HEAD_SIZE).astype(jnp.float32)
    grad_prob = jnp.einsum('ikgd,jkd->kgij', gradient_wide, values_rows.astype(jnp.float32))
    row_delta = lax.optimization_barrier(jnp.sum(probs_full * grad_prob, axis=-1, keepdims=True))
    grad_score = lax.optimization_barrier((probs_full * (grad_prob - row_delta)).astype(jnp.bfloat16)).astype(jnp.float32)
    dquery = inv_root * jnp.einsum('kgij,jkd->ikgd', grad_score, keys_rows.astype(jnp.float32))
    key_gradient = inv_root * jnp.einsum('kgij,ikgd->jkd', grad_score, query_rows_wide)
    value_gradient = jnp.einsum('kgij,ikgd->jkd', probs_low, gradient_wide)
    return (dquery.reshape(TOKENS_PER_PART, QUERY_HEADS, HEAD_SIZE), key_gradient, value_gradient)

def reference(normed, output_gradient, query_weight, key_value_weight, output_weight, adapter_down, query_up, key_value_up, output_down, output_up):
    single_float = jnp.float32
    brain_float = jnp.bfloat16
    overall_rows = normed.shape[0]
    count_of_groups = overall_rows // TOKENS_PER_PART
    key_value_columns = KEY_VALUE_HEADS * HEAD_SIZE
    shift_amount = TOKENS_PER_PART // 2
    positions = jnp.arange(overall_rows, dtype=jnp.int32)
    cosine_rows, sine_rows = rope_tables(positions)
    down_flattened = adapter_down.reshape(3 * ADAPTER_RANK, MODEL_WIDTH)
    lowrank_input = jnp.dot(normed, down_flattened.T, preferred_element_type=single_float).astype(brain_float)
    query_projected = (jnp.dot(normed, query_weight, preferred_element_type=single_float) + adapter_scale * jnp.dot(lowrank_input[:, :ADAPTER_RANK], query_up, preferred_element_type=single_float)).astype(brain_float)
    key_value_flattened = key_value_weight.reshape(MODEL_WIDTH, 2 * key_value_columns)
    key_value_lowrank = jnp.concatenate([jnp.dot(lowrank_input[:, ADAPTER_RANK:2 * ADAPTER_RANK], key_value_up[:, 0], preferred_element_type=single_float), jnp.dot(lowrank_input[:, 2 * ADAPTER_RANK:], key_value_up[:, 1], preferred_element_type=single_float)], axis=1)
    key_value_projected = (jnp.dot(normed, key_value_flattened, preferred_element_type=single_float) + adapter_scale * key_value_lowrank).astype(brain_float)
    q_wide = lax.optimization_barrier(query_projected).astype(single_float).reshape(overall_rows, QUERY_HEADS, HEAD_SIZE)
    query_rows = apply_rotation(q_wide, cosine_rows, sine_rows).astype(brain_float)
    key_value_wide = lax.optimization_barrier(key_value_projected)
    key_matrix_rows = apply_rotation(key_value_wide[:, :key_value_columns].astype(single_float).reshape(overall_rows, KEY_VALUE_HEADS, HEAD_SIZE), cosine_rows, sine_rows).astype(brain_float)
    value_matrix_rows = key_value_projected[:, key_value_columns:].reshape(overall_rows, KEY_VALUE_HEADS, HEAD_SIZE)
    queries_rolled = shift_heads(query_rows, QUERY_HEADS // 2, -shift_amount)
    keys_shifted = shift_heads(key_matrix_rows, KEY_VALUE_HEADS // 2, -shift_amount)
    values_shifted = shift_heads(value_matrix_rows, KEY_VALUE_HEADS // 2, -shift_amount)
    q_groups = queries_rolled.reshape(count_of_groups, TOKENS_PER_PART, QUERY_HEADS, HEAD_SIZE)
    key_grouped = keys_shifted.reshape(count_of_groups, TOKENS_PER_PART, KEY_VALUE_HEADS, HEAD_SIZE)
    value_grouped = values_shifted.reshape(count_of_groups, TOKENS_PER_PART, KEY_VALUE_HEADS, HEAD_SIZE)
    attended_rolled = lax.map(attend_group, (q_groups, key_grouped, value_grouped)).reshape(overall_rows, QUERY_HEADS, HEAD_SIZE)
    attention_output = shift_heads(attended_rolled, QUERY_HEADS // 2, shift_amount).reshape(overall_rows, QUERY_HEADS * HEAD_SIZE)
    lowrank_output = jnp.dot(attention_output, output_down.T, preferred_element_type=single_float).astype(brain_float)
    lowrank_gradient = jnp.dot(output_gradient, output_up.T, preferred_element_type=single_float).astype(brain_float)
    attention_gradient = (jnp.dot(output_gradient, output_weight.T, preferred_element_type=single_float) + adapter_scale * jnp.dot(lowrank_gradient, output_down, preferred_element_type=single_float)).astype(brain_float)
    output_up_gradient = adapter_scale * jnp.dot(lowrank_output.T, output_gradient, preferred_element_type=single_float)
    output_down_gradient = adapter_scale * jnp.dot(lowrank_gradient.T, attention_output, preferred_element_type=single_float)
    grad_rolled = shift_heads(attention_gradient.reshape(overall_rows, QUERY_HEADS, HEAD_SIZE), QUERY_HEADS // 2, -shift_amount)
    g_groups = grad_rolled.reshape(count_of_groups, TOKENS_PER_PART, QUERY_HEADS, HEAD_SIZE)
    dquery_rolled, key_gradient_shifted, value_gradient_shifted = lax.map(attend_back, (q_groups, key_grouped, value_grouped, g_groups))
    dquery = shift_heads(dquery_rolled.reshape(overall_rows, QUERY_HEADS, HEAD_SIZE), QUERY_HEADS // 2, shift_amount)
    key_gradient = shift_heads(key_gradient_shifted.reshape(overall_rows, KEY_VALUE_HEADS, HEAD_SIZE), KEY_VALUE_HEADS // 2, shift_amount)
    value_gradient = shift_heads(value_gradient_shifted.reshape(overall_rows, KEY_VALUE_HEADS, HEAD_SIZE), KEY_VALUE_HEADS // 2, shift_amount)
    query_gradient_lowrank = unrotate(dquery, cosine_rows, sine_rows).reshape(overall_rows, QUERY_HEADS * HEAD_SIZE).astype(brain_float)
    key_gradient_lowrank = unrotate(key_gradient, cosine_rows, sine_rows).reshape(overall_rows, key_value_columns).astype(brain_float)
    value_gradient_lowrank = value_gradient.reshape(overall_rows, key_value_columns).astype(brain_float)
    backward_lowrank = jnp.concatenate([adapter_scale * jnp.dot(query_gradient_lowrank, query_up.T, preferred_element_type=single_float), adapter_scale * jnp.dot(key_gradient_lowrank, key_value_up[:, 0].T, preferred_element_type=single_float), adapter_scale * jnp.dot(value_gradient_lowrank, key_value_up[:, 1].T, preferred_element_type=single_float)], axis=1).astype(brain_float)
    adapter_down_gradient = jnp.dot(backward_lowrank.T, normed, preferred_element_type=single_float).reshape(3, ADAPTER_RANK, MODEL_WIDTH)
    query_up_gradient = adapter_scale * jnp.dot(lowrank_input[:, :ADAPTER_RANK].T, query_gradient_lowrank, preferred_element_type=single_float)
    key_value_up_gradient = adapter_scale * jnp.stack([jnp.dot(lowrank_input[:, ADAPTER_RANK:2 * ADAPTER_RANK].T, key_gradient_lowrank, preferred_element_type=single_float), jnp.dot(lowrank_input[:, 2 * ADAPTER_RANK:].T, value_gradient_lowrank, preferred_element_type=single_float)], axis=1)
    dkv_low = jnp.concatenate([key_gradient_lowrank, value_gradient_lowrank], axis=1)
    normalized_gradient = (jnp.dot(query_gradient_lowrank, query_weight.T, preferred_element_type=single_float) + jnp.dot(dkv_low, key_value_flattened.T, preferred_element_type=single_float) + jnp.dot(backward_lowrank, down_flattened, preferred_element_type=single_float)).astype(brain_float)
    return (normalized_gradient, adapter_down_gradient, query_up_gradient, key_value_up_gradient, output_down_gradient, output_up_gradient)
```

```python
import math

import jax
import jax.numpy as jnp
from jax import lax
from jax.experimental import pallas as pl
from jax.experimental.pallas import tpu as pltpu
from jax.sharding import PartitionSpec as P

MESH = pl.DeviceIdType.MESH
F32 = jnp.float32
BF16 = jnp.bfloat16

HEAD_SIZE = 128
RANK = 8
SCALE = 2.0
ROPE_BASE = 10000.0
ROWS = 512
HALF = 256
BLK = 512
SEQ = 16
LANES = 8
TOKENS = 8192
INV_ROOT = 1.0 / math.sqrt(HEAD_SIZE)


def dot(a, b):
    return lax.dot_general(a, b, (((1,), (0,)), ((), ())), preferred_element_type=F32)


def dot_nt(a, b):
    return lax.dot_general(a, b, (((1,), (1,)), ((), ())), preferred_element_type=F32)


def dot_tn(a, b):
    return lax.dot_general(a, b, (((0,), (0,)), ((), ())), preferred_element_type=F32)


def kernel(
    x_ref, g_ref, wq_ref, wkvd_ref, wo_ref, qup_ref, kvup_ref, od_ref, up_ref, cos_ref, sin_ref,
    dx_ref, dgrad_ref, qg_ref, kvg_ref, odg_ref, oug_ref,
    buf, wqa, wqb, wkv, wkvs, woa, wob, upb, qups, kvur, kvf,
    acc_q0, acc_q1, acc_kd, acc_g0, acc_g1, acc_lg,
    sq, sqr, lip, lipr, kvp, kvr, sg, sgr, slg, slgr,
    probs, qs, ks, vs, att, gas, low, lgs, dkacc, dvacc,
    dq0, dq1, kb, lot, lotr, mown, moth, dkvr,
    st, rsr, rown, yst, yrecv, rollst, rollrecv,
    du, r1buf, pieces, r2buf, agbuf, dbuf,
    local_sem, w_send, w_recv, ag_send, ag_recv, y_send, y_recv, roll_send, roll_recv,
    m_send, m_recv, rs_send, rs_recv, s_send, s_recv,
):
    s = lax.axis_index("seq")
    h = lax.axis_index("head")
    c = lax.rem(h, 2)
    lane = h // 2
    p = lane // 4
    xi = lax.rem(lane, 4)
    a = lax.rem(xi, 2)
    q = 1 - p
    right = p * 8 + lax.rem(xi + 1, 4) * 2 + c
    left = p * 8 + lax.rem(xi + 3, 4) * 2 + c
    sib = h + 1 - 2 * c
    twin = h + 2 - 4 * a
    twin_sib = twin + 1 - 2 * c
    across = h + 8 - 16 * p

    def dev(seq, head):
        return (seq, head)

    def lane_of(r, d):
        plane = p if r == 0 else q
        return plane * 4 + lax.rem(xi + d + 4, 4)

    sends = []
    rolled_sends = []

    def remote(src, dst, ssem, rsem, device):
        return pltpu.make_async_remote_copy(
            src_ref=src, dst_ref=dst, send_sem=ssem, recv_sem=rsem,
            device_id=device, device_id_type=MESH,
        )

    def push(*ends):
        copy = remote(*ends)
        copy.start()
        sends.append(copy)

    def arrived(dst, rsem):
        pltpu.make_async_remote_copy(
            src_ref=dst, dst_ref=dst, send_sem=w_send.at[0], recv_sem=rsem,
            device_id=dev(s, sib), device_id_type=MESH,
        ).wait_recv()

    barrier = pltpu.get_barrier_semaphore()
    for d in range(1, 16):
        pl.semaphore_signal(
            barrier, inc=1, device_id=dev(s, lax.rem(h + d, 16)), device_id_type=MESH
        )
        pl.semaphore_signal(
            barrier, inc=1, device_id=dev(lax.rem(s + d, SEQ), h), device_id_type=MESH
        )
    pl.semaphore_signal(
        barrier, inc=1,
        device_id=dev(lax.rem(s + 2 * p - 1 + SEQ, SEQ), across), device_id_type=MESH,
    )

    locals_ = []

    def fetch(src, dst, k):
        copy = pltpu.make_async_copy(src, dst, local_sem.at[k])
        copy.start()
        return copy

    blocks = []
    for t, ref in enumerate((x_ref, g_ref)):
        blocks.append(fetch(ref.at[pl.ds(HALF, HALF)], buf.at[t, lane, 1 - p], t))
    for t, ref in enumerate((x_ref, g_ref)):

        @pl.when(p == 0)
        def _():
            fetch(ref.at[pl.ds(0, HALF)], buf.at[t, lane, 0], 2 + t)

    weights = [
        fetch(wq_ref.at[:, c], wqa, 4),
        fetch(wkvd_ref.at[:, c], wkv, 5),
        fetch(up_ref, upb.at[lane, pl.ds(0, 16)], 6),
    ]
    for j in range(LANES):
        cols = pl.ds(pl.multiple_of((2 * j + c) * BLK, BLK), BLK)
        weights.append(fetch(wo_ref.at[:, cols], woa.at[j], 7 + j))

    for acc in (acc_q0, acc_q1, acc_kd, acc_g0, acc_g1, acc_lg):
        acc[...] = jnp.zeros(acc.shape, F32)
    upb[:, 16:, :] = jnp.zeros((LANES, 112, BLK), BF16)
    kvf[...] = jnp.zeros(kvf.shape, BF16)

    pl.semaphore_wait(barrier, 31)

    def send_own(t, r, slot):
        b = lane_of(r, 0)
        push(buf.at[t, b, slot], buf.at[t, b, slot], ag_send.at[t, r, slot],
             ag_recv.at[t, r, slot], dev(s, right))
        push(buf.at[t, b, slot], buf.at[t, b, slot], ag_send.at[t, r, 2 + slot],
             ag_recv.at[t, r, 2 + slot], dev(s, left))

    def send_roll(t, ref):
        before = lax.rem(s + SEQ - 1, SEQ)

        def copy():
            return remote(ref.at[pl.ds(0, HALF)], buf.at[t, lane, 1], roll_send.at[t],
                          roll_recv.at[t], dev(before, h))

        rolled_sends.append(copy)

        @pl.when(p == 1)
        def _():
            copy().start()

    def send_across(t, ref):
        push(ref.at[pl.ds(0, HALF)], buf.at[t, lane, q], y_send.at[t, 0], y_recv.at[t, q],
             dev(lax.rem(s - q + SEQ, SEQ), across))
        push(ref.at[pl.ds(HALF, HALF)], buf.at[t, lane, p], y_send.at[t, 1], y_recv.at[t, p],
             dev(s, across))

    def own_ready(t):
        @pl.when(p == 0)
        def _():
            pltpu.make_async_copy(
                (x_ref, g_ref)[t].at[pl.ds(0, HALF)], buf.at[t, lane, 0], local_sem.at[2 + t]
            ).wait()

        @pl.when(p == 1)
        def _():
            arrived(buf.at[t, lane, 1], roll_recv.at[t])

    send_roll(0, x_ref)
    send_across(0, x_ref)
    send_roll(1, g_ref)
    send_across(1, g_ref)
    push(wq_ref.at[:, 1 - c], wqb, w_send.at[0], w_recv.at[0], dev(s, sib))
    push(wkvd_ref.at[:, 1 - c, :, pl.ds(0, 128)], wkvs, w_send.at[1], w_recv.at[1], dev(s, sib))
    blocks[0].wait()
    own_ready(0)
    for slot in range(2):
        send_own(0, 0, slot)
    for j in range(LANES):
        cols = pl.ds(pl.multiple_of((2 * j + 1 - c) * BLK, BLK), BLK)
        push(wo_ref.at[:, cols], wob.at[j], w_send.at[2 + j], w_recv.at[2 + j], dev(s, sib))
    blocks[1].wait()
    own_ready(1)
    for slot in range(2):
        send_own(1, 0, slot)
    weights[2].wait()
    for d in range(1, LANES):
        push(up_ref, upb.at[lane, pl.ds(0, 16)], w_send.at[10 + d], w_recv.at[10 + d],
             dev(s, lax.rem(lane + d, LANES) * 2 + c))
    push(qup_ref.at[pl.ds(0, 16)], qups, w_send.at[18], w_recv.at[18], dev(s, sib))
    for k, peer in enumerate((sib, twin, twin_sib)):
        push(kvup_ref.at[pl.ds(0, 32)], kvur.at[k], w_send.at[19 + k], w_recv.at[19 + k],
             dev(s, peer))

    def multiply(t, b):
        def rows(i, carry):
            block = buf[t, b, i]
            if t == 0:
                acc_q0[i] += dot(block, wqa[b])
                acc_q1[i] += dot(block, wqb[b])
                acc_kd[i] += dot(block, wkv[b])
            else:
                acc_g0[i] += dot_nt(block, woa[b])
                acc_g1[i] += dot_nt(block, wob[b])
                acc_lg[i] += dot_nt(block, upb[b])
            return carry

        lax.fori_loop(0, 2, rows, 0)

    def multiply_sides(t, r):
        def one(k, carry):
            multiply(t, lane_of(r, 1 + 2 * k))
            return carry

        lax.fori_loop(0, 2, one, 0)

    def forward(t, r):
        from_left, from_right = lane_of(r, -1), lane_of(r, 1)
        arrived(buf.at[t, from_left, 0], ag_recv.at[t, r, 0])
        push(buf.at[t, from_left, 0], buf.at[t, from_left, 0], ag_send.at[t, r, 4],
             ag_recv.at[t, r, 4], dev(s, right))
        arrived(buf.at[t, from_right, 1], ag_recv.at[t, r, 3])
        push(buf.at[t, from_right, 1], buf.at[t, from_right, 1], ag_send.at[t, r, 5],
             ag_recv.at[t, r, 5], dev(s, left))

    def sides_ready(t, r):
        arrived(buf.at[t, lane_of(r, -1), 1], ag_recv.at[t, r, 1])
        arrived(buf.at[t, lane_of(r, 1), 0], ag_recv.at[t, r, 2])

    def far_ready(t, r):
        far = lane_of(r, 2)
        arrived(buf.at[t, far, 0], ag_recv.at[t, r, 4])
        arrived(buf.at[t, far, 1], ag_recv.at[t, r, 5])

    def across_ready(t):
        b = lane_of(1, 0)
        for slot in range(2):
            arrived(buf.at[t, b, slot], y_recv.at[t, slot])
            send_own(t, 1, slot)

    forward(0, 0)
    across_ready(0)
    forward(1, 0)
    for k in (0, 1):
        weights[k].wait()
    arrived(wqb, w_recv.at[0])
    arrived(wkvs, w_recv.at[1])

    def join(j, carry):
        wkv[j, :, 0:128] += wkvs[j]
        return carry

    lax.fori_loop(0, LANES, join, 0)
    sides_ready(0, 0)
    across_ready(1)
    multiply(0, lane_of(0, 0))
    multiply_sides(0, 0)
    sides_ready(1, 0)
    for copy in weights[3:]:
        copy.wait()
    for j in range(LANES):
        arrived(wob.at[j], w_recv.at[2 + j])
    for d in range(1, LANES):
        arrived(upb.at[lax.rem(lane - d + LANES, LANES), pl.ds(0, 16)], w_recv.at[10 + d])
    multiply(1, lane_of(0, 0))
    multiply_sides(1, 0)
    forward(0, 1)
    far_ready(0, 0)
    multiply(0, lane_of(0, 2))
    forward(1, 1)
    multiply(0, lane_of(1, 0))
    sides_ready(0, 1)
    multiply_sides(0, 1)
    far_ready(1, 0)
    multiply(1, lane_of(0, 2))
    multiply(1, lane_of(1, 0))
    far_ready(0, 1)
    multiply(0, lane_of(1, 2))

    sq[...] = acc_q1[...].astype(BF16)
    kvp[...] = acc_kd[:, :, 0:128].astype(BF16)
    lip[...] = acc_kd[:, :, 128:256].astype(BF16)
    push(kvp, kvr.at[0], m_send.at[0], m_recv.at[0], dev(s, sib))
    push(kvp, kvr.at[1], m_send.at[1], m_recv.at[1], dev(s, twin))
    push(kvp, kvr.at[2], m_send.at[2], m_recv.at[2], dev(s, twin_sib))
    push(lip, lipr, m_send.at[3], m_recv.at[3], dev(s, sib))
    push(sq, sqr, m_send.at[4], m_recv.at[4], dev(s, sib))

    sides_ready(1, 1)
    multiply_sides(1, 1)
    far_ready(1, 1)
    multiply(1, lane_of(1, 2))
    sg[...] = acc_g1[...].astype(BF16)
    slg[...] = acc_lg[...].astype(BF16)
    push(slg, slgr, m_send.at[5], m_recv.at[5], dev(s, sib))
    push(sg, sgr, m_send.at[6], m_recv.at[6], dev(s, sib))

    for k in range(3):
        arrived(kvur.at[k], w_recv.at[19 + k])
    arrived(qups, w_recv.at[18])
    kvf[0:32, :] = kvup_ref[0:32, :] + kvur[0] + kvur[1] + kvur[2]
    arrived(kvr.at[0], m_recv.at[0])
    arrived(kvr.at[1], m_recv.at[1])
    arrived(kvr.at[2], m_recv.at[2])
    arrived(lipr, m_recv.at[3])
    arrived(sqr, m_recv.at[4])

    def rotate(v, i):
        return v * cos_ref[i] + pltpu.roll(v, 64, 1) * sin_ref[i]

    def unrotate(v, i):
        return v * cos_ref[i] - pltpu.roll(v, 64, 1) * sin_ref[i]

    def project(i, carry):
        low_i = (acc_kd[i, :, 128:256] + lipr[i].astype(F32)).astype(BF16)
        low[i] = low_i
        q_i = (acc_q0[i] + sqr[i].astype(F32) + SCALE * dot(low_i, qup_ref[...])).astype(BF16)
        for hd in range(2):
            cols = slice(hd * 128, hd * 128 + 128)
            qs[hd, i] = rotate(q_i[:, cols].astype(F32), i).astype(BF16)
        own = acc_kd[i, :, 0:128] + kvr[0, i].astype(F32)
        other = kvr[1, i].astype(F32) + kvr[2, i].astype(F32)
        first = jnp.where(a == 0, own, other)
        second = jnp.where(a == 0, other, own)
        rank = SCALE * dot(low_i, kvf[...])
        k_i = jnp.concatenate([first[:, 0:64], second[:, 0:64]], axis=1) + rank[:, 0:128]
        v_i = jnp.concatenate([first[:, 64:128], second[:, 64:128]], axis=1) + rank[:, 128:256]
        start = pl.multiple_of(i * HALF, HALF)
        ks[pl.ds(start, HALF), :] = rotate(k_i.astype(BF16).astype(F32), i).astype(BF16)
        vs[pl.ds(start, HALF), :] = v_i.astype(BF16)
        return carry

    lax.fori_loop(0, 2, project, 0)

    for i in range(2):
        keys = (i + 1) * HALF

        def attend(hd, carry):
            scores = dot_nt(qs[hd, i], ks[0:keys, :]) * INV_ROOT
            row = lax.broadcasted_iota(jnp.int32, scores.shape, 0) + i * HALF
            col = lax.broadcasted_iota(jnp.int32, scores.shape, 1)
            e = jnp.where(col <= row, jnp.exp(scores), 0.0)
            full = e / jnp.sum(e, axis=-1, keepdims=True)
            probs[hd, i, :, 0:keys] = full
            att[hd, i] = dot(full.astype(BF16), vs[0:keys, :]).astype(BF16)
            return carry

        lax.fori_loop(0, 2, attend, 0)
    loti = jnp.concatenate(
        [
            dot_nt(od_ref[0:16, 0:128], att[0, i]) + dot_nt(od_ref[0:16, 128:256], att[1, i])
            for i in range(2)
        ],
        axis=1,
    )
    lot[...] = loti.astype(BF16)
    push(lot, lotr, m_send.at[7], m_recv.at[7], dev(s, sib))

    arrived(slgr, m_recv.at[5])
    arrived(sgr, m_recv.at[6])

    def cotangent(i, carry):
        lg = (acc_lg[i] + slgr[i].astype(F32)).astype(BF16)
        lgs[i] = lg
        ga = (acc_g0[i] + sgr[i].astype(F32) + SCALE * dot(lg, od_ref[...])).astype(BF16)
        gas[0, i] = ga[:, 0:128]
        gas[1, i] = ga[:, 128:256]
        return carry

    lax.fori_loop(0, 2, cotangent, 0)
    dkacc[...] = jnp.zeros(dkacc.shape, F32)
    dvacc[...] = jnp.zeros(dvacc.shape, F32)
    for i in range(2):
        keys = (i + 1) * HALF
        for hd in range(2):
            full = probs[hd, i, :, 0:keys]
            grad = dot_nt(gas[hd, i], vs[0:keys, :])
            delta = jnp.sum(full * grad, axis=-1, keepdims=True)
            ds = (full * (grad - delta)).astype(BF16)
            dq = INV_ROOT * dot(ds, ks[0:keys, :])
            dq0[i, :, hd * 128 : hd * 128 + 128] = unrotate(dq, i).astype(BF16)
            dkacc[0:keys, :] += dot_tn(ds, qs[hd, i])
            dvacc[0:keys, :] += dot_tn(full.astype(BF16), gas[hd, i])
    push(dq0, dq1, m_send.at[8], m_recv.at[8], dev(s, sib))
    for i in range(2):
        rows = slice(i * HALF, i * HALF + HALF)
        dk = unrotate(INV_ROOT * dkacc[rows, :], i)
        dv = dvacc[rows, :]
        low_side = jnp.concatenate([dk[:, 0:64], dv[:, 0:64]], axis=1)
        high_side = jnp.concatenate([dk[:, 64:128], dv[:, 64:128]], axis=1)
        mown[i] = jnp.where(a == 0, low_side, high_side).astype(BF16)
        moth[i] = jnp.where(a == 0, high_side, low_side).astype(BF16)
    push(moth, dkvr.at[1], m_send.at[9], m_recv.at[9], dev(s, twin))
    push(moth, dkvr.at[2], m_send.at[10], m_recv.at[10], dev(s, twin_sib))
    push(mown, dkvr.at[0], m_send.at[11], m_recv.at[11], dev(s, sib))

    kv_rows = kvf[0:32, :].astype(F32)
    kv_low = jnp.concatenate([kv_rows[:, 0:64], kv_rows[:, 128:192]], axis=1)
    kv_high = jnp.concatenate([kv_rows[:, 64:128], kv_rows[:, 192:256]], axis=1)
    kv_chip = jnp.where(a == 0, kv_low, kv_high).astype(BF16)
    kv_chip = jnp.concatenate([kv_chip, jnp.zeros((96, 128), BF16)], axis=0)
    sib_up = jnp.concatenate([qups[...], jnp.zeros((112, 256), BF16)], axis=0)

    arrived(dq1, m_recv.at[8])
    arrived(dkvr.at[1], m_recv.at[9])
    arrived(dkvr.at[2], m_recv.at[10])
    arrived(dkvr.at[0], m_recv.at[11])
    back_t = []
    for i in range(2):
        total = (
            mown[i].astype(F32) + dkvr[0, i].astype(F32)
            + dkvr[1, i].astype(F32) + dkvr[2, i].astype(F32)
        ).astype(BF16)
        back = SCALE * (
            dot_nt(dq0[i], qup_ref[...]) + dot_nt(dq1[i], sib_up) + dot_nt(total, kv_chip)
        )
        kb[i, :, 0:128] = total
        kb[i, :, 128:256] = back.astype(BF16)
        back_t.append(back.T[0:32, :])

    def dx_block(b, i):
        return dot_nt(dq0[i], wqa[b]) + dot_nt(dq1[i], wqb[b]) + dot_nt(kb[i], wkv[b])

    def far_block(r):
        def one(i, carry):
            st[r, 0, i] = dx_block(lane_of(r, 2), i).astype(BF16)
            return carry

        lax.fori_loop(0, 2, one, 0)
        push(st.at[r, 0, 0], rsr.at[r, 0], rs_send.at[r, 0], rs_recv.at[r, 0], dev(s, right))
        push(st.at[r, 0, 1], rsr.at[r, 1], rs_send.at[r, 1], rs_recv.at[r, 1], dev(s, left))

    def side_free(r):
        st[r, 1, 1] = dx_block(lane_of(r, 1), 1).astype(BF16)
        push(st.at[r, 1, 1], rsr.at[r, 3], rs_send.at[r, 3], rs_recv.at[r, 3], dev(s, right))
        st[r, 2, 0] = dx_block(lane_of(r, -1), 0).astype(BF16)
        push(st.at[r, 2, 0], rsr.at[r, 4], rs_send.at[r, 4], rs_recv.at[r, 4], dev(s, left))

    def side_sum(r):
        arrived(rsr.at[r, 0], rs_recv.at[r, 0])
        st[r, 1, 0] = (dx_block(lane_of(r, 1), 0) + rsr[r, 0].astype(F32)).astype(BF16)
        push(st.at[r, 1, 0], rsr.at[r, 2], rs_send.at[r, 2], rs_recv.at[r, 2], dev(s, right))
        arrived(rsr.at[r, 1], rs_recv.at[r, 1])
        st[r, 2, 1] = (dx_block(lane_of(r, -1), 1) + rsr[r, 1].astype(F32)).astype(BF16)
        push(st.at[r, 2, 1], rsr.at[r, 5], rs_send.at[r, 5], rs_recv.at[r, 5], dev(s, left))

    def own_block(r, i):
        arrived(rsr.at[r, 2 + i], rs_recv.at[r, 2 + i])
        arrived(rsr.at[r, 4 + i], rs_recv.at[r, 4 + i])
        return dx_block(lane_of(r, 0), i) + rsr[r, 2 + i].astype(F32) + rsr[r, 4 + i].astype(F32)

    far_block(1)
    side_free(1)
    far_block(0)
    side_free(0)

    arrived(lotr, m_recv.at[7])
    back_full = jnp.concatenate(back_t, axis=1).astype(BF16)
    low_out = (SCALE * (loti + lotr[...].astype(F32))).astype(BF16)
    out_full = jnp.concatenate(
        [jnp.zeros((16, ROWS), BF16), jnp.zeros((8, ROWS), BF16), low_out[0:8]], axis=0
    )

    def adapters(j, carry):
        total = jnp.zeros((32, BLK), F32)
        for i in range(2):
            cols = slice(i * HALF, i * HALF + HALF)
            total += dot(back_full[:, cols], buf[0, j, i]) + dot(out_full[:, cols], buf[1, j, i])
        du[j] = total.astype(BF16)
        return carry

    lax.fori_loop(0, LANES, adapters, 0)
    side_sum(1)
    for d in range(1, LANES):
        owner = lax.rem(lane + d, LANES)
        push(du.at[owner], r1buf.at[d - 1], s_send.at[0, d], s_recv.at[0, d],
             dev(s, owner * 2 + c))

    low_t = jnp.concatenate([low[i].astype(F32).T[0:32] for i in range(2)], axis=1).astype(BF16)
    lg_t = jnp.concatenate([lgs[i].astype(F32).T[0:16] for i in range(2)], axis=1).astype(BF16)
    query_up = jnp.zeros((32, 256), F32)
    kv_up = jnp.zeros((32, 128), F32)
    out_down = jnp.zeros((16, 256), F32)
    for i in range(2):
        cols = slice(i * HALF, i * HALF + HALF)
        query_up += dot(low_t[:, cols], dq0[i])
        kv_up += dot(low_t[:, cols], kb[i, :, 0:128])
        out_down += jnp.concatenate(
            [dot(lg_t[:, cols], att[0, i]), dot(lg_t[:, cols], att[1, i])], axis=1
        )
    side_sum(0)
    lane_col = lax.broadcasted_iota(jnp.int32, (8, 128), 1)
    kv_grad = SCALE * jnp.where(lane_col < 64, kv_up[8:16], kv_up[16:24])
    alone = jnp.concatenate(
        [
            jnp.concatenate([SCALE * query_up[0:8], SCALE * out_down[0:8]], axis=1),
            jnp.concatenate([kv_grad, jnp.zeros((8, 384), F32)], axis=1),
        ],
        axis=0,
    ).astype(BF16)
    for k in range(4):
        pieces[8 + k] = alone[:, k * 128 : k * 128 + 128]
        pieces[12 + k] = jnp.zeros((16, 128), BF16)
    shared = du[lane].astype(F32)
    for d in range(1, LANES):
        arrived(r1buf.at[d - 1], s_recv.at[0, d])
        shared += r1buf[d - 1].astype(F32)
    shared = shared.astype(BF16)
    for g in range(2):
        for k in range(4):
            pieces[4 * g + k] = shared[16 * g : 16 * g + 16, k * 128 : k * 128 + 128]
    for d in range(1, SEQ):
        owner = lax.rem(s + d, SEQ)
        push(pieces.at[owner], r2buf.at[d - 1], s_send.at[1, d], s_recv.at[1, d], dev(owner, h))

    for i in range(2):
        yst[i] = own_block(1, i).astype(BF16)
        half = i + p - 2 * i * p
        push(yst.at[i], yrecv.at[half], y_send.at[2, i], y_recv.at[2, half],
             dev(lax.rem(s + i * p, SEQ), across))

    mine = pieces[s].astype(F32)
    for d in range(1, SEQ):
        arrived(r2buf.at[d - 1], s_recv.at[1, d])
        mine += r2buf[d - 1].astype(F32)
    agbuf[s] = mine.astype(BF16)
    for d in range(1, SEQ):
        push(agbuf.at[s], agbuf.at[s], s_send.at[2, d], s_recv.at[2, d],
             dev(lax.rem(s + d, SEQ), h))

    after = lax.rem(s + 1, SEQ)

    def send_back():
        return remote(rollst, rollrecv, roll_send.at[2], roll_recv.at[2], dev(after, h))

    rolled_sends.append(send_back)
    for i in (1, 0):
        rown[i] = own_block(0, i)
        if i == 1:

            @pl.when(p == 1)
            def _():
                rollst[...] = rown[1].astype(BF16)
                send_back().start()

    for d in range(1, SEQ):
        arrived(agbuf.at[lax.rem(s - d + SEQ, SEQ)], s_recv.at[2, d])
    for d in range(1, 16):
        push(agbuf.at[pl.ds(0, 8)], dbuf.at[h], s_send.at[3, d], s_recv.at[3, d],
             dev(s, lax.rem(h + d, 16)))
    for k in range(4):
        cols = slice(k * 128, k * 128 + 128)
        oug_ref[:, cols] = agbuf[4 + k].astype(F32)[8:16]
    for k in range(2):
        cols = slice(k * 128, k * 128 + 128)
        qg_ref[:, cols] = agbuf[8 + k].astype(F32)[0:8]
        odg_ref[:, cols] = agbuf[10 + k].astype(F32)[0:8]
    kvg_ref[...] = agbuf[8].astype(F32)[8:16]
    dbuf[h] = agbuf[0:8]

    for half in range(2):
        arrived(yrecv.at[half], y_recv.at[2, half])

    @pl.when(p == 0)
    def _():
        for i in range(2):
            dx_ref[i * HALF : i * HALF + HALF, :] = (rown[i] + yrecv[i].astype(F32)).astype(BF16)

    @pl.when(p == 1)
    def _():
        arrived(rollrecv, roll_recv.at[2])
        dx_ref[HALF:ROWS, :] = (rown[0] + yrecv[1].astype(F32)).astype(BF16)
        dx_ref[0:HALF, :] = (rollrecv[...].astype(F32) + yrecv[0].astype(F32)).astype(BF16)

    for d in range(1, 16):
        arrived(dbuf.at[lax.rem(h - d + 16, 16)], s_recv.at[3, d])

    def place(j, carry):
        for k in range(4):
            cols = pl.ds(pl.multiple_of(j * BLK + k * 128, 128), 128)
            dgrad_ref[0:16, cols] = dbuf[j, k].astype(F32)
            dgrad_ref[16:24, cols] = dbuf[j, 4 + k].astype(F32)[0:8]
        return carry

    lax.fori_loop(0, 16, place, 0)

    for copy in sends:
        copy.wait_send()

    @pl.when(p == 1)
    def _():
        for copy in rolled_sends:
            copy().wait_send()


def body(normed, output_gradient, query_weight, key_value_weight, output_weight,
         adapter_down, query_up, key_value_up, output_down, output_up):
    h = lax.axis_index("head")
    s = lax.axis_index("seq")
    c = lax.rem(h, 2)
    p = h // 8
    width = adapter_down.shape[2]

    positions = lax.rem(
        s * ROWS + jnp.arange(ROWS, dtype=jnp.int32) + p * HALF, TOKENS
    ).astype(F32)
    half_dim = HEAD_SIZE // 2
    frequency = ROPE_BASE ** (-jnp.arange(half_dim, dtype=F32) * 2.0 / HEAD_SIZE)
    angles = positions[:, None] * frequency[None, :]
    cos, sin = jnp.cos(angles), jnp.sin(angles)
    cos_wide = jnp.concatenate([cos, cos], axis=1).reshape(2, HALF, HEAD_SIZE)
    sin_wide = jnp.concatenate([-sin, sin], axis=1).reshape(2, HALF, HEAD_SIZE)

    keys, values = key_value_weight[:, 0], key_value_weight[:, 1]
    blank = jnp.zeros_like(keys)
    placed = jnp.where(
        c == 0,
        jnp.concatenate([keys, blank, values, blank], axis=1),
        jnp.concatenate([blank, keys, blank, values], axis=1),
    )
    down_t = adapter_down.reshape(3 * RANK, width).T
    wkvd = jnp.concatenate(
        [placed, down_t, jnp.zeros((width, 128 - 3 * RANK), BF16)], axis=1
    ).reshape(LANES, 2, BLK, 256)
    wq = query_weight.reshape(LANES, 2, BLK, 256)

    def tall(array, rows):
        return jnp.pad(array, ((0, rows - array.shape[0]), (0, 0)))

    column = lax.rem(h, 4) * 32
    kvup = jnp.zeros((128, 256), BF16)
    kvup = lax.dynamic_update_slice(kvup, key_value_up[:, 0], (8, column))
    kvup = lax.dynamic_update_slice(kvup, key_value_up[:, 1], (16, 128 + column))

    vm = lambda *shape: pltpu.VMEM(shape, BF16)
    vf = lambda *shape: pltpu.VMEM(shape, F32)
    dma = lambda *shape: pltpu.SemaphoreType.DMA(shape)
    out_shape = [
        jax.ShapeDtypeStruct((ROWS, BLK), BF16),
        jax.ShapeDtypeStruct((3 * RANK, width), F32),
        jax.ShapeDtypeStruct((RANK, 256), F32),
        jax.ShapeDtypeStruct((RANK, 128), F32),
        jax.ShapeDtypeStruct((RANK, 256), F32),
        jax.ShapeDtypeStruct((RANK, BLK), F32),
    ]
    hbm = pl.BlockSpec(memory_space=pl.ANY)
    vmem = pl.BlockSpec(memory_space=pltpu.VMEM)
    scratch = [
        vm(2, LANES, 2, HALF, BLK), vm(LANES, BLK, 256), vm(LANES, BLK, 256),
        vm(LANES, BLK, 256), vm(LANES, BLK, 128), vm(LANES, 256, BLK), vm(LANES, 256, BLK),
        vm(LANES, 128, BLK), vm(16, 256), vm(3, 32, 256), vm(128, 256),
        vf(2, HALF, 256), vf(2, HALF, 256), vf(2, HALF, 256), vf(2, HALF, 256),
        vf(2, HALF, 256), vf(2, HALF, 128),
        vm(2, HALF, 256), vm(2, HALF, 256), vm(2, HALF, 128), vm(2, HALF, 128),
        vm(2, HALF, 128), vm(3, 2, HALF, 128), vm(2, HALF, 256), vm(2, HALF, 256),
        vm(2, HALF, 128), vm(2, HALF, 128),
        vf(2, 2, HALF, ROWS), vm(2, 2, HALF, 128), vm(ROWS, 128), vm(ROWS, 128),
        vm(2, 2, HALF, 128), vm(2, 2, HALF, 128), vm(2, HALF, 128), vm(2, HALF, 128),
        vf(ROWS, 128), vf(ROWS, 128),
        vm(2, HALF, 256), vm(2, HALF, 256), vm(2, HALF, 256), vm(16, ROWS), vm(16, ROWS),
        vm(2, HALF, 128), vm(2, HALF, 128), vm(3, 2, HALF, 128),
        vm(2, 3, 2, HALF, BLK), vm(2, 6, HALF, BLK), vf(2, HALF, BLK), vm(2, HALF, BLK),
        vm(2, HALF, BLK), vm(HALF, BLK), vm(HALF, BLK),
        vm(LANES, 32, BLK), vm(LANES - 1, 32, BLK), vm(16, 16, 128), vm(15, 16, 128),
        vm(16, 16, 128), vm(16, 8, 16, 128),
        dma(16), dma(22), dma(22), dma(2, 2, 6), dma(2, 2, 6), dma(3, 2), dma(3, 2),
        dma(3), dma(3), dma(12), dma(12), dma(2, 6), dma(2, 6), dma(4, 16), dma(4, 16),
    ]
    dx, dgrad, qg, kvg, odg, oug = pl.pallas_call(
        kernel,
        out_shape=out_shape,
        in_specs=[hbm] * 5 + [vmem] * 3 + [hbm] + [vmem] * 2,
        out_specs=[vmem] * 6,
        scratch_shapes=scratch,
        compiler_params=pltpu.CompilerParams(
            collective_id=0, has_side_effects=True, vmem_limit_bytes=56 * 1024 * 1024
        ),
        cost_estimate=pl.CostEstimate(
            flops=9_000_000_000, bytes_accessed=20_000_000, transcendentals=400_000
        ),
    )(
        normed, output_gradient, wq, wkvd, output_weight, tall(query_up, 128), kvup,
        tall(output_down, 128), tall(output_up, 16), cos_wide, sin_wide,
    )
    kv_grad = jnp.stack(
        [
            lax.dynamic_slice_in_dim(kvg, c * 32, 32, 1),
            lax.dynamic_slice_in_dim(kvg, 64 + c * 32, 32, 1),
        ],
        axis=1,
    )
    return dx, dgrad.reshape(3, RANK, width), qg, kv_grad, odg, oug


def solution(mesh):
    return jax.shard_map(
        body,
        mesh=mesh,
        in_specs=(
            P("seq", "head"), P("seq", "head"), P(None, "head"), P(None, None, "head"),
            P("head", None), P(), P(None, "head"), P(None, None, "head"),
            P(None, "head"), P(None, "head"),
        ),
        out_specs=(
            P("seq", "head"), P(), P(None, "head"), P(None, None, "head"),
            P(None, "head"), P(None, "head"),
        ),
        check_vma=False,
    )
```

```python
import math

import jax
import jax.numpy as jnp
from jax import lax
from jax.experimental import pallas as pl
from jax.experimental.pallas import tpu as pltpu
from jax.sharding import PartitionSpec as P

MESH = pl.DeviceIdType.MESH
F32 = jnp.float32
BF16 = jnp.bfloat16

HEAD_SIZE = 128
RANK = 8
SCALE = 2.0
ROPE_BASE = 10000.0
ROWS = 512
HALF = 256
BLK = 512
SEQ = 16
LANES = 8
TOKENS = 8192
INV_ROOT = 1.0 / math.sqrt(HEAD_SIZE)


def dot(a, b):
    return lax.dot_general(a, b, (((1,), (0,)), ((), ())), preferred_element_type=F32)


def dot_nt(a, b):
    return lax.dot_general(a, b, (((1,), (1,)), ((), ())), preferred_element_type=F32)


def dot_tn(a, b):
    return lax.dot_general(a, b, (((0,), (0,)), ((), ())), preferred_element_type=F32)


def kernel(
    x_ref, g_ref, wq_ref, kvt_ref, wo_ref, down_ref, qup_in, kvup_in, od_in, up_in, cos_ref, sin_ref,
    dx_ref, dgrad_ref, small_ref,
    buf, wqa, wqb, wkv, woa, wob, upb, qups, kvur, kvf, qup_ref, kvup_ref, od_ref, up_ref,
    acc_q0, acc_q1, acc_kd, acc_g0, acc_g1, acc_lg,
    sq, sqr, lip, lipr, kvp, kvr, sg, sgr, slg, slgr,
    probs, qs, ks, vs, att, gas, low, lgs, dkacc, dvacc,
    dq0, dq1, kb, lot, lotr, mown, moth, dkvr,
    st, rsr, rown, yst, yrecv, rollst, rollrecv,
    du, r1buf, pieces, r2buf, agbuf, dbuf,
    local_sem, w_send, w_recv, ag_send, ag_recv, y_send, y_recv, roll_send, roll_recv,
    m_send, m_recv, rs_send, rs_recv, s_send, s_recv,
):
    s = lax.axis_index("seq")
    h = lax.axis_index("head")
    c = lax.rem(h, 2)
    lane = h // 2
    p = lane // 4
    xi = lax.rem(lane, 4)
    a = lax.rem(xi, 2)
    q = 1 - p
    right = p * 8 + lax.rem(xi + 1, 4) * 2 + c
    left = p * 8 + lax.rem(xi + 3, 4) * 2 + c
    sib = h + 1 - 2 * c
    twin = h + 2 - 4 * a
    twin_sib = twin + 1 - 2 * c
    across = h + 8 - 16 * p

    def dev(seq, head):
        return (seq, head)

    def lane_of(r, d):
        plane = p if r == 0 else q
        return plane * 4 + lax.rem(xi + d + 4, 4)

    sends = []
    rolled_sends = []

    def remote(src, dst, ssem, rsem, device):
        return pltpu.make_async_remote_copy(
            src_ref=src, dst_ref=dst, send_sem=ssem, recv_sem=rsem,
            device_id=device, device_id_type=MESH,
        )

    def push(*ends):
        copy = remote(*ends)
        copy.start()
        sends.append(copy)

    def arrived(dst, rsem):
        pltpu.make_async_remote_copy(
            src_ref=dst, dst_ref=dst, send_sem=w_send.at[0], recv_sem=rsem,
            device_id=dev(s, sib), device_id_type=MESH,
        ).wait_recv()

    barrier = pltpu.get_barrier_semaphore()
    for d in range(1, 16):
        pl.semaphore_signal(
            barrier, inc=1, device_id=dev(s, lax.rem(h + d, 16)), device_id_type=MESH
        )
        pl.semaphore_signal(
            barrier, inc=1, device_id=dev(lax.rem(s + d, SEQ), h), device_id_type=MESH
        )
    pl.semaphore_signal(
        barrier, inc=1,
        device_id=dev(lax.rem(s + 2 * p - 1 + SEQ, SEQ), across), device_id_type=MESH,
    )

    locals_ = []

    def fetch(src, dst, k):
        copy = pltpu.make_async_copy(src, dst, local_sem.at[k])
        copy.start()
        return copy

    blocks = []
    for t, ref in enumerate((x_ref, g_ref)):
        blocks.append(fetch(ref.at[pl.ds(HALF, HALF)], buf.at[t, lane, 1 - p], t))
    for t, ref in enumerate((x_ref, g_ref)):

        @pl.when(p == 0)
        def _():
            fetch(ref.at[pl.ds(0, HALF)], buf.at[t, lane, 0], 2 + t)

    weights = [
        fetch(wq_ref.at[:, c], wqa, 4),
    ]
    for j in range(LANES):
        cols = pl.ds(pl.multiple_of((2 * j + c) * BLK, BLK), BLK)
        weights.append(fetch(kvt_ref.at[:, :, cols], wkv.at[j, pl.ds(0, 2), c], 5 + j))
    for j in range(LANES):
        cols = pl.ds(pl.multiple_of((2 * j + c) * BLK, BLK), BLK)
        weights.append(fetch(wo_ref.at[:, cols], woa.at[j], 13 + j))

    for acc in (acc_q0, acc_q1, acc_kd, acc_g0, acc_g1, acc_lg):
        acc[...] = jnp.zeros(acc.shape, F32)
    upb[:, 16:, :] = jnp.zeros((LANES, 112, BLK), BF16)
    kvf[...] = jnp.zeros(kvf.shape, BF16)
    qup_ref[...] = jnp.concatenate([qup_in[...], jnp.zeros((120, 256), BF16)], axis=0)
    od_ref[...] = jnp.concatenate([od_in[...], jnp.zeros((120, 256), BF16)], axis=0)
    up_ref[...] = jnp.concatenate([up_in[...], jnp.zeros((8, BLK), BF16)], axis=0)
    upb[lane, 0:16, :] = up_ref[...]
    source = lax.broadcasted_iota(jnp.int32, (64, 256), 0)
    target = lax.broadcasted_iota(jnp.int32, (64, 256), 1)
    goal = source + lax.rem(h, 4) * 32 + jnp.where(source < 32, 0, 96)
    spread = dot(kvup_in[...], jnp.where(target == goal, 1.0, 0.0).astype(BF16))
    column = lax.broadcasted_iota(jnp.int32, (8, 256), 1)
    none = jnp.zeros((8, 256), F32)
    kvup_ref[...] = jnp.concatenate(
        [none, jnp.where(column < 128, spread, 0.0), jnp.where(column < 128, 0.0, spread), none],
        axis=0,
    ).astype(BF16)
    wkv[:, 2:4] = jnp.zeros((LANES, 2, 2, 32, BLK), BF16)
    for j in range(LANES):
        cols = pl.ds(pl.multiple_of((2 * j + c) * BLK, BLK), BLK)
        wkv[j, 2, 0] = jnp.concatenate([down_ref[:, cols], jnp.zeros((8, BLK), BF16)], axis=0)

    pl.semaphore_wait(barrier, 31)

    def send_own(t, slot):
        push(buf.at[t, lane, slot], buf.at[t, lane, slot], ag_send.at[t, 0, slot],
             ag_recv.at[t, 0, slot], dev(s, right))
        push(buf.at[t, lane, slot], buf.at[t, lane, slot], ag_send.at[t, 0, 2 + slot],
             ag_recv.at[t, 0, 2 + slot], dev(s, left))

    beyond = [dev(lax.rem(s + i - q + SEQ, SEQ), across) for i in range(2)]

    def cross(t, b, i, k):
        push(buf.at[t, b, i], buf.at[t, b, 1 - i], ag_send.at[t, 1, k + 1 - i],
             ag_recv.at[t, 1, k + 1 - i], beyond[i])

    def send_roll(t, ref):
        before = lax.rem(s + SEQ - 1, SEQ)

        def copy():
            return remote(ref.at[pl.ds(0, HALF)], buf.at[t, lane, 1], roll_send.at[t],
                          roll_recv.at[t], dev(before, h))

        rolled_sends.append(copy)

        @pl.when(p == 1)
        def _():
            copy().start()

    def send_across(t, ref):
        push(ref.at[pl.ds(0, HALF)], buf.at[t, lane, q], y_send.at[t, 0], y_recv.at[t, q],
             dev(lax.rem(s - q + SEQ, SEQ), across))
        push(ref.at[pl.ds(HALF, HALF)], buf.at[t, lane, p], y_send.at[t, 1], y_recv.at[t, p],
             dev(s, across))

    def own_local(t):
        blocks[t].wait()

        @pl.when(p == 0)
        def _():
            pltpu.make_async_copy(
                (x_ref, g_ref)[t].at[pl.ds(0, HALF)], buf.at[t, lane, 0], local_sem.at[2 + t]
            ).wait()

    def own_rolled(t):
        @pl.when(p == 1)
        def _():
            arrived(buf.at[t, lane, 1], roll_recv.at[t])

    send_roll(0, x_ref)
    own_local(0)
    send_own(0, 0)
    send_across(0, x_ref)
    own_rolled(0)
    send_own(0, 1)
    push(wq_ref.at[:, 1 - c], wqb, w_send.at[0], w_recv.at[0], dev(s, sib))
    for j in range(LANES):
        cols = pl.ds(pl.multiple_of((2 * j + 1 - c) * BLK, BLK), BLK)
        push(kvt_ref.at[:, :, cols], wkv.at[j, pl.ds(0, 2), c], w_send.at[22 + j],
             w_recv.at[22 + j], dev(s, sib))
    for j in range(LANES):
        cols = pl.ds(pl.multiple_of((2 * j + 1 - c) * BLK, BLK), BLK)
        push(wo_ref.at[:, cols], wob.at[j], w_send.at[2 + j], w_recv.at[2 + j], dev(s, sib))
    send_roll(1, g_ref)
    for d in range(1, LANES):
        push(up_ref, upb.at[lane, pl.ds(0, 16)], w_send.at[10 + d], w_recv.at[10 + d],
             dev(s, lax.rem(lane + d, LANES) * 2 + c))
    push(qup_ref.at[pl.ds(0, 16)], qups, w_send.at[18], w_recv.at[18], dev(s, sib))
    for k, peer in enumerate((sib, twin, twin_sib)):
        push(kvup_ref, kvur.at[k], w_send.at[19 + k], w_recv.at[19 + k], dev(s, peer))

    def multiply(t, b):
        def rows(i, carry):
            block = buf[t, b, i]
            if t == 0:
                acc_q0[i] += dot(block, wqa[b])
                acc_q1[i] += dot(block, wqb[b])
                acc_kd[i] += dot_nt(block, wkv[b].reshape(256, BLK))
            else:
                acc_g0[i] += dot_nt(block, woa[b])
                acc_g1[i] += dot_nt(block, wob[b])
                acc_lg[i] += dot_nt(block, upb[b])
            return carry

        lax.fori_loop(0, 2, rows, 0)

    def multiply_sides(t, r):
        def one(k, carry):
            multiply(t, lane_of(r, 1 + 2 * k))
            return carry

        lax.fori_loop(0, 2, one, 0)

    def forward(t, r):
        from_left, from_right = lane_of(r, -1), lane_of(r, 1)
        arrived(buf.at[t, from_left, 0], ag_recv.at[t, r, 0])
        push(buf.at[t, from_left, 0], buf.at[t, from_left, 0], ag_send.at[t, r, 4],
             ag_recv.at[t, r, 4], dev(s, right))
        arrived(buf.at[t, from_right, 1], ag_recv.at[t, r, 3])
        push(buf.at[t, from_right, 1], buf.at[t, from_right, 1], ag_send.at[t, r, 5],
             ag_recv.at[t, r, 5], dev(s, left))

    def sides_ready(t, r):
        from_left, from_right = lane_of(r, -1), lane_of(r, 1)
        arrived(buf.at[t, from_right, 0], ag_recv.at[t, r, 2])
        if r == 0:
            cross(t, from_right, 0, 2)
        arrived(buf.at[t, from_left, 1], ag_recv.at[t, r, 1])
        if r == 0:
            cross(t, from_left, 1, 0)

    def far_ready(t, r):
        far = lane_of(r, 2)
        arrived(buf.at[t, far, 0], ag_recv.at[t, r, 4])
        arrived(buf.at[t, far, 1], ag_recv.at[t, r, 5])

    def across_ready(t):
        b = lane_of(1, 0)
        for slot, device, k in ((0, left, 2), (1, right, 1)):
            arrived(buf.at[t, b, slot], y_recv.at[t, slot])
            push(buf.at[t, b, slot], buf.at[t, b, slot], ag_send.at[t, 1, k],
                 ag_recv.at[t, 1, k], dev(s, device))

    forward(0, 0)
    sides_ready(0, 0)
    across_ready(0)
    own_local(1)
    send_own(1, 0)
    send_across(1, g_ref)
    own_rolled(1)
    send_own(1, 1)
    for copy in weights[0:9]:
        copy.wait()
    arrived(wqb, w_recv.at[0])
    for j in range(LANES):
        arrived(wkv.at[j, pl.ds(0, 2), 1 - c], w_recv.at[22 + j])
    multiply(0, lane)
    multiply_sides(0, 0)
    multiply(0, lane_of(1, 0))
    forward(0, 1)
    far_ready(0, 0)
    multiply(0, lane_of(0, 2))
    forward(1, 0)
    sides_ready(1, 0)
    across_ready(1)
    sides_ready(0, 1)
    multiply_sides(0, 1)
    far_ready(0, 1)
    multiply(0, lane_of(1, 2))

    sq[...] = acc_q1[...].astype(BF16)
    kvp[...] = acc_kd[:, :, 0:128].astype(BF16)
    lip[...] = acc_kd[:, :, 128:256].astype(BF16)
    push(kvp, kvr.at[0], m_send.at[0], m_recv.at[0], dev(s, sib))
    push(kvp, kvr.at[1], m_send.at[1], m_recv.at[1], dev(s, twin))
    push(kvp, kvr.at[2], m_send.at[2], m_recv.at[2], dev(s, twin_sib))
    push(lip, lipr, m_send.at[3], m_recv.at[3], dev(s, sib))
    push(sq, sqr, m_send.at[4], m_recv.at[4], dev(s, sib))

    for copy in weights[9:]:
        copy.wait()
    for j in range(LANES):
        arrived(wob.at[j], w_recv.at[2 + j])
    for d in range(1, LANES):
        arrived(upb.at[lax.rem(lane - d + LANES, LANES), pl.ds(0, 16)], w_recv.at[10 + d])
    multiply(1, lane)
    multiply_sides(1, 0)

    for k in range(3):
        arrived(kvur.at[k], w_recv.at[19 + k])
    arrived(qups, w_recv.at[18])
    kvf[0:32, :] = kvup_ref[0:32, :] + kvur[0] + kvur[1] + kvur[2]
    arrived(kvr.at[0], m_recv.at[0])
    arrived(kvr.at[1], m_recv.at[1])
    arrived(kvr.at[2], m_recv.at[2])
    arrived(lipr, m_recv.at[3])
    arrived(sqr, m_recv.at[4])

    def rotate(v, i):
        return v * cos_ref[i] + pltpu.roll(v, 64, 1) * sin_ref[i]

    def unrotate(v, i):
        return v * cos_ref[i] - pltpu.roll(v, 64, 1) * sin_ref[i]

    def project(i, carry):
        low_i = (acc_kd[i, :, 128:256] + lipr[i].astype(F32)).astype(BF16)
        low[i] = low_i
        q_i = (acc_q0[i] + sqr[i].astype(F32) + SCALE * dot(low_i, qup_ref[...])).astype(BF16)
        for hd in range(2):
            cols = slice(hd * 128, hd * 128 + 128)
            qs[hd, i] = rotate(q_i[:, cols].astype(F32), i).astype(BF16)
        own = acc_kd[i, :, 0:128] + kvr[0, i].astype(F32)
        other = kvr[1, i].astype(F32) + kvr[2, i].astype(F32)
        first = jnp.where(a == 0, own, other)
        second = jnp.where(a == 0, other, own)
        rank = SCALE * dot(low_i, kvf[...])
        k_i = jnp.concatenate([first[:, 0:64], second[:, 0:64]], axis=1) + rank[:, 0:128]
        v_i = jnp.concatenate([first[:, 64:128], second[:, 64:128]], axis=1) + rank[:, 128:256]
        start = pl.multiple_of(i * HALF, HALF)
        ks[pl.ds(start, HALF), :] = rotate(k_i.astype(BF16).astype(F32), i).astype(BF16)
        vs[pl.ds(start, HALF), :] = v_i.astype(BF16)
        return carry

    lax.fori_loop(0, 2, project, 0)

    for i in range(2):
        keys = (i + 1) * HALF

        def attend(hd, carry):
            scores = dot_nt(qs[hd, i], ks[0:keys, :]) * INV_ROOT
            row = lax.broadcasted_iota(jnp.int32, scores.shape, 0) + i * HALF
            col = lax.broadcasted_iota(jnp.int32, scores.shape, 1)
            e = jnp.where(col <= row, jnp.exp(scores), 0.0)
            full = e / jnp.sum(e, axis=-1, keepdims=True)
            probs[hd, i, :, 0:keys] = full
            att[hd, i] = dot(full.astype(BF16), vs[0:keys, :]).astype(BF16)
            return carry

        lax.fori_loop(0, 2, attend, 0)
        if i == 0:
            forward(1, 1)
    loti = jnp.concatenate(
        [
            dot_nt(od_ref[0:16, 0:128], att[0, i]) + dot_nt(od_ref[0:16, 128:256], att[1, i])
            for i in range(2)
        ],
        axis=1,
    )
    lot[...] = loti.astype(BF16)
    push(lot, lotr, m_send.at[7], m_recv.at[7], dev(s, sib))

    far_ready(1, 0)
    multiply(1, lane_of(0, 2))
    multiply(1, lane_of(1, 0))
    sides_ready(1, 1)
    multiply_sides(1, 1)
    far_ready(1, 1)
    multiply(1, lane_of(1, 2))
    sg[...] = acc_g1[...].astype(BF16)
    slg[...] = acc_lg[...].astype(BF16)
    push(slg, slgr, m_send.at[5], m_recv.at[5], dev(s, sib))
    push(sg, sgr, m_send.at[6], m_recv.at[6], dev(s, sib))

    arrived(slgr, m_recv.at[5])
    arrived(sgr, m_recv.at[6])

    def cotangent(i, carry):
        lg = (acc_lg[i] + slgr[i].astype(F32)).astype(BF16)
        lgs[i] = lg
        ga = (acc_g0[i] + sgr[i].astype(F32) + SCALE * dot(lg, od_ref[...])).astype(BF16)
        gas[0, i] = ga[:, 0:128]
        gas[1, i] = ga[:, 128:256]
        return carry

    lax.fori_loop(0, 2, cotangent, 0)
    dkacc[...] = jnp.zeros(dkacc.shape, F32)
    dvacc[...] = jnp.zeros(dvacc.shape, F32)
    for i in range(2):
        keys = (i + 1) * HALF
        for hd in range(2):
            full = probs[hd, i, :, 0:keys]
            grad = dot_nt(gas[hd, i], vs[0:keys, :])
            delta = jnp.sum(full * grad, axis=-1, keepdims=True)
            ds = (full * (grad - delta)).astype(BF16)
            dq = INV_ROOT * dot(ds, ks[0:keys, :])
            dq0[i, :, hd * 128 : hd * 128 + 128] = unrotate(dq, i).astype(BF16)
            dkacc[0:keys, :] += dot_tn(ds, qs[hd, i])
            dvacc[0:keys, :] += dot_tn(full.astype(BF16), gas[hd, i])
    push(dq0, dq1, m_send.at[8], m_recv.at[8], dev(s, sib))
    for i in range(2):
        rows = slice(i * HALF, i * HALF + HALF)
        dk = unrotate(INV_ROOT * dkacc[rows, :], i)
        dv = dvacc[rows, :]
        low_side = jnp.concatenate([dk[:, 0:64], dv[:, 0:64]], axis=1)
        high_side = jnp.concatenate([dk[:, 64:128], dv[:, 64:128]], axis=1)
        mown[i] = jnp.where(a == 0, low_side, high_side).astype(BF16)
        moth[i] = jnp.where(a == 0, high_side, low_side).astype(BF16)
    push(moth, dkvr.at[1], m_send.at[9], m_recv.at[9], dev(s, twin))
    push(moth, dkvr.at[2], m_send.at[10], m_recv.at[10], dev(s, twin_sib))
    push(mown, dkvr.at[0], m_send.at[11], m_recv.at[11], dev(s, sib))

    kv_rows = kvf[0:32, :].astype(F32)
    kv_low = jnp.concatenate([kv_rows[:, 0:64], kv_rows[:, 128:192]], axis=1)
    kv_high = jnp.concatenate([kv_rows[:, 64:128], kv_rows[:, 192:256]], axis=1)
    kv_chip = jnp.where(a == 0, kv_low, kv_high).astype(BF16)
    kv_chip = jnp.concatenate([kv_chip, jnp.zeros((96, 128), BF16)], axis=0)
    sib_up = jnp.concatenate([qups[...], jnp.zeros((112, 256), BF16)], axis=0)

    arrived(dq1, m_recv.at[8])
    arrived(dkvr.at[1], m_recv.at[9])
    arrived(dkvr.at[2], m_recv.at[10])
    arrived(dkvr.at[0], m_recv.at[11])
    back_t = []
    for i in range(2):
        total = (
            mown[i].astype(F32) + dkvr[0, i].astype(F32)
            + dkvr[1, i].astype(F32) + dkvr[2, i].astype(F32)
        ).astype(BF16)
        back = SCALE * (
            dot_nt(dq0[i], qup_ref[...]) + dot_nt(dq1[i], sib_up) + dot_nt(total, kv_chip)
        )
        kb[i, :, 0:128] = total
        kb[i, :, 128:256] = back.astype(BF16)
        back_t.append(back.T[0:32, :])

    def dx_block(b, i):
        return dot_nt(dq0[i], wqa[b]) + dot_nt(dq1[i], wqb[b]) + dot(kb[i], wkv[b].reshape(256, BLK))

    def far_block(r):
        def one(i, carry):
            st[r, 0, i] = dx_block(lane_of(r, 2), i).astype(BF16)
            return carry

        lax.fori_loop(0, 2, one, 0)
        push(st.at[r, 0, 0], rsr.at[r, 0], rs_send.at[r, 0], rs_recv.at[r, 0], dev(s, right))
        push(st.at[r, 0, 1], rsr.at[r, 1], rs_send.at[r, 1], rs_recv.at[r, 1], dev(s, left))

    def side_cross(d, i, extra):
        k = 1 if d == 1 else 2
        total = dx_block(lane_of(1, d), i)
        arrived(rsr.at[1, extra], rs_recv.at[1, extra])
        total += rsr[1, extra].astype(F32)
        st[1, k, i] = total.astype(BF16)
        slot = 2 * k + 1 - i
        push(st.at[1, k, i], rsr.at[1, slot], rs_send.at[1, slot], rs_recv.at[1, slot], beyond[i])

    def side_next(d, i, slot):
        k = 1 if d == 1 else 2
        st[1, k, i] = dx_block(lane_of(1, d), i).astype(BF16)
        push(st.at[1, k, i], rsr.at[1, slot], rs_send.at[1, slot], rs_recv.at[1, slot],
             dev(s, right if d == 1 else left))

    def side_home(d, i, extra):
        k = 1 if d == 1 else 2
        slot = 2 * k + i
        total = dx_block(lane_of(0, d), i)
        if extra is not None:
            arrived(rsr.at[0, extra], rs_recv.at[0, extra])
            total += rsr[0, extra].astype(F32)
        else:
            arrived(rsr.at[1, slot], rs_recv.at[1, slot])
            total += rsr[1, slot].astype(F32)
        st[0, k, i] = total.astype(BF16)
        push(st.at[0, k, i], rsr.at[0, slot], rs_send.at[0, slot], rs_recv.at[0, slot],
             dev(s, right if d == 1 else left))

    far_block(1)
    side_next(1, 1, 2)
    side_next(-1, 0, 5)
    far_block(0)

    arrived(lotr, m_recv.at[7])
    back_full = jnp.concatenate(back_t, axis=1).astype(BF16)
    low_out = (SCALE * (loti + lotr[...].astype(F32))).astype(BF16)
    out_full = jnp.concatenate(
        [jnp.zeros((16, ROWS), BF16), jnp.zeros((8, ROWS), BF16), low_out[0:8]], axis=0
    )

    def adapters(j, carry):
        total = jnp.zeros((32, BLK), F32)
        for i in range(2):
            cols = slice(i * HALF, i * HALF + HALF)
            total += dot(back_full[:, cols], buf[0, j, i]) + dot(out_full[:, cols], buf[1, j, i])
        du[j] = total.astype(BF16)
        return carry

    lax.fori_loop(0, LANES, adapters, 0)
    for d in range(1, LANES):
        owner = lax.rem(lane + d, LANES)
        push(du.at[owner], r1buf.at[d - 1], s_send.at[0, d], s_recv.at[0, d],
             dev(s, owner * 2 + c))

    side_cross(1, 0, 0)
    side_cross(-1, 1, 1)

    low_t = jnp.concatenate([low[i].astype(F32).T[0:32] for i in range(2)], axis=1).astype(BF16)
    lg_t = jnp.concatenate([lgs[i].astype(F32).T[0:16] for i in range(2)], axis=1).astype(BF16)
    query_up = jnp.zeros((32, 256), F32)
    kv_up = jnp.zeros((32, 128), F32)
    out_down = jnp.zeros((16, 256), F32)
    for i in range(2):
        cols = slice(i * HALF, i * HALF + HALF)
        query_up += dot(low_t[:, cols], dq0[i])
        kv_up += dot(low_t[:, cols], kb[i, :, 0:128])
        out_down += jnp.concatenate(
            [dot(lg_t[:, cols], att[0, i]), dot(lg_t[:, cols], att[1, i])], axis=1
        )
    for i, slot in ((0, 5), (1, 2)):
        total = dx_block(lane_of(1, 0), i)
        arrived(rsr.at[1, slot], rs_recv.at[1, slot])
        yst[i] = (total + rsr[1, slot].astype(F32)).astype(BF16)
        half = i + p - 2 * i * p
        push(yst.at[i], yrecv.at[half], y_send.at[2, i], y_recv.at[2, half],
             dev(lax.rem(s + i * p, SEQ), across))
    lane_col = lax.broadcasted_iota(jnp.int32, (8, 128), 1)
    kv_grad = SCALE * jnp.where(lane_col < 64, kv_up[8:16], kv_up[16:24])
    alone = jnp.concatenate(
        [
            jnp.concatenate([SCALE * query_up[0:8], SCALE * out_down[0:8]], axis=1),
            jnp.concatenate([kv_grad, jnp.zeros((8, 384), F32)], axis=1),
        ],
        axis=0,
    ).astype(BF16)
    for k in range(4):
        pieces[8 + k] = alone[:, k * 128 : k * 128 + 128]
        pieces[12 + k] = jnp.zeros((16, 128), BF16)
    shared = du[lane].astype(F32)
    for d in range(1, LANES):
        arrived(r1buf.at[d - 1], s_recv.at[0, d])
        shared += r1buf[d - 1].astype(F32)
    shared = shared.astype(BF16)
    for g in range(2):
        for k in range(4):
            pieces[4 * g + k] = shared[16 * g : 16 * g + 16, k * 128 : k * 128 + 128]
    for d in range(1, SEQ):
        owner = lax.rem(s + d, SEQ)
        push(pieces.at[owner], r2buf.at[d - 1], s_send.at[1, d], s_recv.at[1, d], dev(owner, h))

    side_home(1, 0, 0)
    side_home(-1, 1, 1)
    mine = pieces[s].astype(F32)
    for d in range(1, SEQ):
        arrived(r2buf.at[d - 1], s_recv.at[1, d])
        mine += r2buf[d - 1].astype(F32)
    agbuf[s] = mine.astype(BF16)
    for d in range(1, SEQ):
        push(agbuf.at[s], agbuf.at[s], s_send.at[2, d], s_recv.at[2, d],
             dev(lax.rem(s + d, SEQ), h))

    side_home(1, 1, None)
    side_home(-1, 0, None)
    for d in range(1, SEQ):
        arrived(agbuf.at[lax.rem(s - d + SEQ, SEQ)], s_recv.at[2, d])
    for d in range(1, LANES):
        push(agbuf.at[pl.ds(0, 8)], dbuf.at[lane, c], s_send.at[3, d], s_recv.at[3, d],
             dev(s, lax.rem(lane + d, LANES) * 2 + c))
    dbuf[lane, c] = agbuf[0:8]
    for k in range(4):
        cols = slice(k * 128, k * 128 + 128)
        small_ref[0:8, cols] = agbuf[4 + k].astype(F32)[8:16]
        small_ref[8:24, cols] = agbuf[8 + k].astype(F32)
    kv_out = agbuf[8].astype(F32)[8:16]
    small_ref[16:24, 0:64] = jnp.concatenate(
        [
            jnp.where(c == 0, kv_out[:, 0:32], kv_out[:, 32:64]),
            jnp.where(c == 0, kv_out[:, 64:96], kv_out[:, 96:128]),
        ],
        axis=1,
    )
    after = lax.rem(s + 1, SEQ)

    def send_back():
        return remote(rollst, rollrecv, roll_send.at[2], roll_recv.at[2], dev(after, h))

    rolled_sends.append(send_back)
    for i in (1, 0):
        total = dx_block(lane, i)
        for k in (2, 4):
            arrived(rsr.at[0, k + i], rs_recv.at[0, k + i])
            total += rsr[0, k + i].astype(F32)
        rown[i] = total
        if i == 1:

            @pl.when(p == 1)
            def _():
                rollst[...] = rown[1].astype(BF16)
                send_back().start()

    for d in range(1, LANES):
        arrived(dbuf.at[lax.rem(lane - d + LANES, LANES), c], s_recv.at[3, d])
    push(dbuf.at[:, c], dbuf.at[:, c], s_send.at[3, 0], s_recv.at[3, 0], dev(s, sib))

    for half in range(2):
        arrived(yrecv.at[half], y_recv.at[2, half])

    @pl.when(p == 0)
    def _():
        for i in range(2):
            dx_ref[i * HALF : i * HALF + HALF, :] = (rown[i] + yrecv[i].astype(F32)).astype(BF16)

    @pl.when(p == 1)
    def _():
        arrived(rollrecv, roll_recv.at[2])
        dx_ref[HALF:ROWS, :] = (rown[0] + yrecv[1].astype(F32)).astype(BF16)
        dx_ref[0:HALF, :] = (rollrecv[...].astype(F32) + yrecv[0].astype(F32)).astype(BF16)

    arrived(dbuf.at[:, 1 - c], s_recv.at[3, 0])

    def place(j, carry):
        for k in range(4):
            cols = pl.ds(pl.multiple_of(j * BLK + k * 128, 128), 128)
            dgrad_ref[0:16, cols] = dbuf[j // 2, lax.rem(j, 2), k].astype(F32)
            dgrad_ref[16:24, cols] = dbuf[j // 2, lax.rem(j, 2), 4 + k].astype(F32)[0:8]
        return carry

    lax.fori_loop(0, 16, place, 0)

    for copy in sends:
        copy.wait_send()

    @pl.when(p == 1)
    def _():
        for copy in rolled_sends:
            copy().wait_send()


def body(normed, output_gradient, query_weight, key_value_weight, output_weight,
         adapter_down, query_up, key_value_up, output_down, output_up):
    h = lax.axis_index("head")
    s = lax.axis_index("seq")
    c = lax.rem(h, 2)
    p = h // 8
    width = adapter_down.shape[2]

    positions = lax.rem(
        s * ROWS + jnp.arange(ROWS, dtype=jnp.int32) + p * HALF, TOKENS
    ).astype(F32)
    half_dim = HEAD_SIZE // 2
    frequency = ROPE_BASE ** (-jnp.arange(half_dim, dtype=F32) * 2.0 / HEAD_SIZE)
    angles = positions[:, None] * frequency[None, :]
    cos, sin = jnp.cos(angles), jnp.sin(angles)
    cos_wide = jnp.concatenate([cos, cos], axis=1).reshape(2, HALF, HEAD_SIZE)
    sin_wide = jnp.concatenate([-sin, sin], axis=1).reshape(2, HALF, HEAD_SIZE)

    kvt = key_value_weight.transpose(1, 2, 0)
    wq = query_weight.reshape(LANES, 2, BLK, 256)

    vm = lambda *shape: pltpu.VMEM(shape, BF16)
    vf = lambda *shape: pltpu.VMEM(shape, F32)
    dma = lambda *shape: pltpu.SemaphoreType.DMA(shape)
    out_shape = [
        jax.ShapeDtypeStruct((ROWS, BLK), BF16),
        jax.ShapeDtypeStruct((3 * RANK, width), F32),
        jax.ShapeDtypeStruct((3 * RANK, BLK), F32),
    ]
    hbm = pl.BlockSpec(memory_space=pl.ANY)
    vmem = pl.BlockSpec(memory_space=pltpu.VMEM)
    scratch = [
        vm(2, LANES, 2, HALF, BLK), vm(LANES, BLK, 256), vm(LANES, BLK, 256),
        vm(LANES, 4, 2, 32, BLK), vm(LANES, 256, BLK), vm(LANES, 256, BLK),
        vm(LANES, 128, BLK), vm(16, 256), vm(3, 32, 256), vm(128, 256),
        vm(128, 256), vm(32, 256), vm(128, 256), vm(16, BLK),
        vf(2, HALF, 256), vf(2, HALF, 256), vf(2, HALF, 256), vf(2, HALF, 256),
        vf(2, HALF, 256), vf(2, HALF, 128),
        vm(2, HALF, 256), vm(2, HALF, 256), vm(2, HALF, 128), vm(2, HALF, 128),
        vm(2, HALF, 128), vm(3, 2, HALF, 128), vm(2, HALF, 256), vm(2, HALF, 256),
        vm(2, HALF, 128), vm(2, HALF, 128),
        vf(2, 2, HALF, ROWS), vm(2, 2, HALF, 128), vm(ROWS, 128), vm(ROWS, 128),
        vm(2, 2, HALF, 128), vm(2, 2, HALF, 128), vm(2, HALF, 128), vm(2, HALF, 128),
        vf(ROWS, 128), vf(ROWS, 128),
        vm(2, HALF, 256), vm(2, HALF, 256), vm(2, HALF, 256), vm(16, ROWS), vm(16, ROWS),
        vm(2, HALF, 128), vm(2, HALF, 128), vm(3, 2, HALF, 128),
        vm(2, 3, 2, HALF, BLK), vm(2, 6, HALF, BLK), vf(2, HALF, BLK), vm(2, HALF, BLK),
        vm(2, HALF, BLK), vm(HALF, BLK), vm(HALF, BLK),
        vm(LANES, 32, BLK), vm(LANES - 1, 32, BLK), vm(16, 16, 128), vm(15, 16, 128),
        vm(16, 16, 128), vm(LANES, 2, 8, 16, 128),
        dma(21), dma(30), dma(30), dma(2, 2, 6), dma(2, 2, 6), dma(3, 2), dma(3, 2),
        dma(3), dma(3), dma(12), dma(12), dma(2, 6), dma(2, 6), dma(4, 16), dma(4, 16),
    ]
    dx, dgrad, small = pl.pallas_call(
        kernel,
        out_shape=out_shape,
        in_specs=[hbm] * 5 + [vmem] * 7,
        out_specs=[vmem] * 3,
        scratch_shapes=scratch,
        compiler_params=pltpu.CompilerParams(
            collective_id=0, has_side_effects=True, vmem_limit_bytes=56 * 1024 * 1024
        ),
        cost_estimate=pl.CostEstimate(
            flops=9_000_000_000, bytes_accessed=20_000_000, transcendentals=400_000
        ),
    )(
        normed, output_gradient, wq, kvt, output_weight, adapter_down.reshape(3 * RANK, width),
        query_up, key_value_up.reshape(RANK, 64), output_down, output_up, cos_wide, sin_wide,
    )
    return (
        dx,
        dgrad.reshape(3, RANK, width),
        small[8:16, 0:256],
        small[16:24, 0:64].reshape(RANK, 2, 32),
        small[8:16, 256:512],
        small[0:8],
    )


def solution(mesh):
    return jax.shard_map(
        body,
        mesh=mesh,
        in_specs=(
            P("seq", "head"), P("seq", "head"), P(None, "head"), P(None, None, "head"),
            P("head", None), P(), P(None, "head"), P(None, None, "head"),
            P(None, "head"), P(None, "head"),
        ),
        out_specs=(
            P("seq", "head"), P(), P(None, "head"), P(None, None, "head"),
            P(None, "head"), P(None, "head"),
        ),
        check_vma=False,
    )
```

```python
import math

import jax
import jax.numpy as jnp
from jax import lax
from jax.experimental import pallas as pl
from jax.experimental.pallas import tpu as pltpu
from jax.sharding import PartitionSpec as P

MESH = pl.DeviceIdType.MESH
F32 = jnp.float32
BF16 = jnp.bfloat16

HEAD_SIZE = 128
RANK = 8
SCALE = 2.0
ROPE_BASE = 10000.0
ROWS = 512
HALF = 256
BLK = 512
SEQ = 16
LANES = 8
TOKENS = 8192
INV_ROOT = 1.0 / math.sqrt(HEAD_SIZE)


def dot(a, b):
    return lax.dot_general(a, b, (((1,), (0,)), ((), ())), preferred_element_type=F32)


def dot_nt(a, b):
    return lax.dot_general(a, b, (((1,), (1,)), ((), ())), preferred_element_type=F32)


def dot_tn(a, b):
    return lax.dot_general(a, b, (((0,), (0,)), ((), ())), preferred_element_type=F32)


def kernel(
    x_ref, g_ref, wq_ref, kvt_ref, wo_ref, down_ref, qup_in, kvup_in, od_in, up_in, cos_ref, sin_ref,
    dx_ref, dgrad_ref, small_ref,
    buf, wqa, wqb, wkv, woa, wob, upb, qups, kvur, kvf, qup_ref, kvup_ref, od_ref, up_ref,
    acc_q0, acc_q1, acc_kd, acc_g0, acc_g1, acc_lg,
    sq, sqr, lip, lipr, kvp, kvr, sg, sgr, slg, slgr,
    probs, qs, ks, vs, att, gas, low, lgs, dkacc, dvacc,
    dq0, dq1, kb, lot, lotr, mown, moth, dkvr,
    st, rsr, rown, yst, yrecv, rollst, rollrecv,
    du, r1buf, al, alr, pieces, r2buf, tiles, eb,
    local_sem, w_send, w_recv, ag_send, ag_recv, y_send, y_recv, roll_send, roll_recv,
    m_send, m_recv, rs_send, rs_recv, s_send, s_recv,
):
    s = lax.axis_index("seq")
    h = lax.axis_index("head")
    c = lax.rem(h, 2)
    lane = h // 2
    p = lane // 4
    xi = lax.rem(lane, 4)
    a = lax.rem(xi, 2)
    q = 1 - p
    right = p * 8 + lax.rem(xi + 1, 4) * 2 + c
    left = p * 8 + lax.rem(xi + 3, 4) * 2 + c
    sib = h + 1 - 2 * c
    twin = h + 2 - 4 * a
    twin_sib = twin + 1 - 2 * c
    across = h + 8 - 16 * p
    z = s // 2
    k_lo = lax.rem(s, 2)
    place_in_plane = k_lo * 8 + lane

    def dev(seq, head):
        return (seq, head)

    def lane_of(r, d):
        plane = p if r == 0 else q
        return plane * 4 + lax.rem(xi + d + 4, 4)

    sends = []
    rolled_sends = []

    def remote(src, dst, ssem, rsem, device):
        return pltpu.make_async_remote_copy(
            src_ref=src, dst_ref=dst, send_sem=ssem, recv_sem=rsem,
            device_id=device, device_id_type=MESH,
        )

    def push(*ends):
        copy = remote(*ends)
        copy.start()
        sends.append(copy)

    def arrived(dst, rsem):
        pltpu.make_async_remote_copy(
            src_ref=dst, dst_ref=dst, send_sem=w_send.at[0], recv_sem=rsem,
            device_id=dev(s, sib), device_id_type=MESH,
        ).wait_recv()

    barrier = pltpu.get_barrier_semaphore()
    def plane_peer(d):
        m = lax.rem(place_in_plane + d, 16)
        return m // 8, lax.rem(m, 8)

    def column_peer(d):
        return lax.rem(z + d, 8)

    greeted = [dev(s, sib), dev(s, twin_sib)]
    greeted += [dev(lax.rem(s + 2 * p - 1 + SEQ, SEQ), across)]
    greeted += [dev(lax.rem(s + d, SEQ), h) for d in (1, SEQ - 1)]
    for d in range(1, 16):
        lo, j = plane_peer(d)
        greeted.append(dev(z * 2 + lo, j * 2 + c))
    greeted += [dev(column_peer(d) * 2 + k_lo, h) for d in range(1, 8)]
    for device in greeted:
        pl.semaphore_signal(barrier, inc=1, device_id=device, device_id_type=MESH)

    locals_ = []

    def fetch(src, dst, k):
        copy = pltpu.make_async_copy(src, dst, local_sem.at[k])
        copy.start()
        return copy

    blocks = []
    for t, ref in enumerate((x_ref, g_ref)):
        blocks.append(fetch(ref.at[pl.ds(HALF, HALF)], buf.at[t, lane, 1 - p], t))
    for t, ref in enumerate((x_ref, g_ref)):

        @pl.when(p == 0)
        def _():
            fetch(ref.at[pl.ds(0, HALF)], buf.at[t, lane, 0], 2 + t)

    weights = [
        fetch(wq_ref.at[:, c], wqa, 4),
    ]
    for j in range(LANES):
        cols = pl.ds(pl.multiple_of((2 * j + c) * BLK, BLK), BLK)
        weights.append(fetch(kvt_ref.at[:, :, cols], wkv.at[j, pl.ds(0, 2), c], 5 + j))
    for j in range(LANES):
        cols = pl.ds(pl.multiple_of((2 * j + c) * BLK, BLK), BLK)
        weights.append(fetch(wo_ref.at[:, cols], woa.at[j], 13 + j))

    for acc in (acc_q0, acc_q1, acc_kd, acc_g0, acc_g1, acc_lg):
        acc[...] = jnp.zeros(acc.shape, F32)
    upb[:, 16:, :] = jnp.zeros((LANES, 112, BLK), BF16)
    kvf[...] = jnp.zeros(kvf.shape, BF16)
    qup_ref[...] = jnp.concatenate([qup_in[...], jnp.zeros((120, 256), BF16)], axis=0)
    od_ref[...] = jnp.concatenate([od_in[...], jnp.zeros((120, 256), BF16)], axis=0)
    up_ref[...] = jnp.concatenate([up_in[...], jnp.zeros((8, BLK), BF16)], axis=0)
    upb[lane, 0:16, :] = up_ref[...]
    source = lax.broadcasted_iota(jnp.int32, (64, 256), 0)
    target = lax.broadcasted_iota(jnp.int32, (64, 256), 1)
    goal = source + lax.rem(h, 4) * 32 + jnp.where(source < 32, 0, 96)
    spread = dot(kvup_in[...], jnp.where(target == goal, 1.0, 0.0).astype(BF16))
    column = lax.broadcasted_iota(jnp.int32, (8, 256), 1)
    none = jnp.zeros((8, 256), F32)
    kvup_ref[...] = jnp.concatenate(
        [none, jnp.where(column < 128, spread, 0.0), jnp.where(column < 128, 0.0, spread), none],
        axis=0,
    ).astype(BF16)
    wkv[:, 2:4] = jnp.zeros((LANES, 2, 2, 32, BLK), BF16)
    for j in range(LANES):
        cols = pl.ds(pl.multiple_of((2 * j + c) * BLK, BLK), BLK)
        wkv[j, 2, 0] = jnp.concatenate([down_ref[:, cols], jnp.zeros((8, BLK), BF16)], axis=0)

    pl.semaphore_wait(barrier, len(greeted))

    def send_own(t, slot):
        push(buf.at[t, lane, slot], buf.at[t, lane, slot], ag_send.at[t, 0, slot],
             ag_recv.at[t, 0, slot], dev(s, right))
        push(buf.at[t, lane, slot], buf.at[t, lane, slot], ag_send.at[t, 0, 2 + slot],
             ag_recv.at[t, 0, 2 + slot], dev(s, left))

    beyond = [dev(lax.rem(s + i - q + SEQ, SEQ), across) for i in range(2)]

    def cross(t, b, i, k):
        push(buf.at[t, b, i], buf.at[t, b, 1 - i], ag_send.at[t, 1, k + 1 - i],
             ag_recv.at[t, 1, k + 1 - i], beyond[i])

    def send_roll(t, ref):
        before = lax.rem(s + SEQ - 1, SEQ)

        def copy():
            return remote(ref.at[pl.ds(0, HALF)], buf.at[t, lane, 1], roll_send.at[t],
                          roll_recv.at[t], dev(before, h))

        rolled_sends.append(copy)

        @pl.when(p == 1)
        def _():
            copy().start()

    def send_across(t, ref):
        push(ref.at[pl.ds(0, HALF)], buf.at[t, lane, q], y_send.at[t, 0], y_recv.at[t, q],
             dev(lax.rem(s - q + SEQ, SEQ), across))
        push(ref.at[pl.ds(HALF, HALF)], buf.at[t, lane, p], y_send.at[t, 1], y_recv.at[t, p],
             dev(s, across))

    def own_local(t):
        blocks[t].wait()

        @pl.when(p == 0)
        def _():
            pltpu.make_async_copy(
                (x_ref, g_ref)[t].at[pl.ds(0, HALF)], buf.at[t, lane, 0], local_sem.at[2 + t]
            ).wait()

    def own_rolled(t):
        @pl.when(p == 1)
        def _():
            arrived(buf.at[t, lane, 1], roll_recv.at[t])

    send_roll(0, x_ref)
    own_local(0)
    send_own(0, 0)
    send_across(0, x_ref)
    own_rolled(0)
    send_own(0, 1)
    push(wq_ref.at[:, 1 - c], wqb, w_send.at[0], w_recv.at[0], dev(s, sib))
    for j in range(LANES):
        cols = pl.ds(pl.multiple_of((2 * j + 1 - c) * BLK, BLK), BLK)
        push(kvt_ref.at[:, :, cols], wkv.at[j, pl.ds(0, 2), c], w_send.at[22 + j],
             w_recv.at[22 + j], dev(s, sib))
    for j in range(LANES):
        cols = pl.ds(pl.multiple_of((2 * j + 1 - c) * BLK, BLK), BLK)
        push(wo_ref.at[:, cols], wob.at[j], w_send.at[2 + j], w_recv.at[2 + j], dev(s, sib))
    send_roll(1, g_ref)
    for d in range(1, LANES):
        push(up_ref, upb.at[lane, pl.ds(0, 16)], w_send.at[10 + d], w_recv.at[10 + d],
             dev(s, lax.rem(lane + d, LANES) * 2 + c))
    push(qup_ref.at[pl.ds(0, 16)], qups, w_send.at[18], w_recv.at[18], dev(s, sib))
    for k, peer in enumerate((sib, twin, twin_sib)):
        push(kvup_ref, kvur.at[k], w_send.at[19 + k], w_recv.at[19 + k], dev(s, peer))

    def multiply(t, b):
        def rows(i, carry):
            block = buf[t, b, i]
            if t == 0:
                acc_q0[i] += dot(block, wqa[b])
                acc_q1[i] += dot(block, wqb[b])
                acc_kd[i] += dot_nt(block, wkv[b].reshape(256, BLK))
            else:
                acc_g0[i] += dot_nt(block, woa[b])
                acc_g1[i] += dot_nt(block, wob[b])
                acc_lg[i] += dot_nt(block, upb[b])
            return carry

        lax.fori_loop(0, 2, rows, 0)

    def multiply_sides(t, r):
        def one(k, carry):
            multiply(t, lane_of(r, 1 + 2 * k))
            return carry

        lax.fori_loop(0, 2, one, 0)

    def forward(t, r):
        from_left, from_right = lane_of(r, -1), lane_of(r, 1)
        arrived(buf.at[t, from_left, 0], ag_recv.at[t, r, 0])
        push(buf.at[t, from_left, 0], buf.at[t, from_left, 0], ag_send.at[t, r, 4],
             ag_recv.at[t, r, 4], dev(s, right))
        arrived(buf.at[t, from_right, 1], ag_recv.at[t, r, 3])
        push(buf.at[t, from_right, 1], buf.at[t, from_right, 1], ag_send.at[t, r, 5],
             ag_recv.at[t, r, 5], dev(s, left))

    def sides_ready(t, r):
        from_left, from_right = lane_of(r, -1), lane_of(r, 1)
        arrived(buf.at[t, from_right, 0], ag_recv.at[t, r, 2])
        if r == 0:
            cross(t, from_right, 0, 2)
        arrived(buf.at[t, from_left, 1], ag_recv.at[t, r, 1])
        if r == 0:
            cross(t, from_left, 1, 0)

    def far_ready(t, r):
        far = lane_of(r, 2)
        arrived(buf.at[t, far, 0], ag_recv.at[t, r, 4])
        arrived(buf.at[t, far, 1], ag_recv.at[t, r, 5])

    def across_ready(t):
        b = lane_of(1, 0)
        for slot, device, k in ((0, left, 2), (1, right, 1)):
            arrived(buf.at[t, b, slot], y_recv.at[t, slot])
            push(buf.at[t, b, slot], buf.at[t, b, slot], ag_send.at[t, 1, k],
                 ag_recv.at[t, 1, k], dev(s, device))

    forward(0, 0)
    sides_ready(0, 0)
    across_ready(0)
    send_across(1, g_ref)
    for copy in weights[0:9]:
        copy.wait()
    arrived(wqb, w_recv.at[0])
    for j in range(LANES):
        arrived(wkv.at[j, pl.ds(0, 2), 1 - c], w_recv.at[22 + j])
    multiply(0, lane)
    own_local(1)
    own_rolled(1)
    forward(0, 1)
    send_own(1, 0)
    multiply_sides(0, 0)
    multiply(0, lane_of(1, 0))
    far_ready(0, 0)
    multiply(0, lane_of(0, 2))
    sides_ready(0, 1)
    multiply_sides(0, 1)
    far_ready(0, 1)
    multiply(0, lane_of(1, 2))

    sq[...] = acc_q1[...].astype(BF16)
    kvp[...] = acc_kd[:, :, 0:128].astype(BF16)
    lip[...] = acc_kd[:, :, 128:256].astype(BF16)
    push(kvp, kvr.at[1], m_send.at[1], m_recv.at[1], dev(s, twin))
    send_own(1, 1)
    push(kvp, kvr.at[0], m_send.at[0], m_recv.at[0], dev(s, sib))
    push(lip, lipr, m_send.at[3], m_recv.at[3], dev(s, sib))
    push(sq, sqr, m_send.at[4], m_recv.at[4], dev(s, sib))

    for copy in weights[9:]:
        copy.wait()
    for j in range(LANES):
        arrived(wob.at[j], w_recv.at[2 + j])
    for d in range(1, LANES):
        arrived(upb.at[lax.rem(lane - d + LANES, LANES), pl.ds(0, 16)], w_recv.at[10 + d])
    multiply(1, lane)

    for k in range(3):
        arrived(kvur.at[k], w_recv.at[19 + k])
    arrived(qups, w_recv.at[18])
    kvf[0:32, :] = kvup_ref[0:32, :] + kvur[0] + kvur[1] + kvur[2]
    arrived(kvr.at[1], m_recv.at[1])
    push(kvr.at[1], kvr.at[2], m_send.at[2], m_recv.at[2], dev(s, sib))
    arrived(kvr.at[0], m_recv.at[0])
    arrived(kvr.at[2], m_recv.at[2])
    arrived(lipr, m_recv.at[3])
    arrived(sqr, m_recv.at[4])

    def rotate(v, i):
        return v * cos_ref[i] + pltpu.roll(v, 64, 1) * sin_ref[i]

    def unrotate(v, i):
        return v * cos_ref[i] - pltpu.roll(v, 64, 1) * sin_ref[i]

    def project(i, carry):
        low_i = (acc_kd[i, :, 128:256] + lipr[i].astype(F32)).astype(BF16)
        low[i] = low_i
        q_i = (acc_q0[i] + sqr[i].astype(F32) + SCALE * dot(low_i, qup_ref[...])).astype(BF16)
        for hd in range(2):
            cols = slice(hd * 128, hd * 128 + 128)
            qs[hd, i] = rotate(q_i[:, cols].astype(F32), i).astype(BF16)
        own = acc_kd[i, :, 0:128] + kvr[0, i].astype(F32)
        other = kvr[1, i].astype(F32) + kvr[2, i].astype(F32)
        first = jnp.where(a == 0, own, other)
        second = jnp.where(a == 0, other, own)
        rank = SCALE * dot(low_i, kvf[...])
        k_i = jnp.concatenate([first[:, 0:64], second[:, 0:64]], axis=1) + rank[:, 0:128]
        v_i = jnp.concatenate([first[:, 64:128], second[:, 64:128]], axis=1) + rank[:, 128:256]
        start = pl.multiple_of(i * HALF, HALF)
        ks[pl.ds(start, HALF), :] = rotate(k_i.astype(BF16).astype(F32), i).astype(BF16)
        vs[pl.ds(start, HALF), :] = v_i.astype(BF16)
        return carry

    lax.fori_loop(0, 2, project, 0)

    for i in range(2):
        keys = (i + 1) * HALF

        def attend(hd, carry):
            scores = dot_nt(qs[hd, i], ks[0:keys, :]) * INV_ROOT
            row = lax.broadcasted_iota(jnp.int32, scores.shape, 0) + i * HALF
            col = lax.broadcasted_iota(jnp.int32, scores.shape, 1)
            e = jnp.where(col <= row, jnp.exp(scores), 0.0)
            full = e / jnp.sum(e, axis=-1, keepdims=True)
            probs[hd, i, :, 0:keys] = full
            att[hd, i] = dot(full.astype(BF16), vs[0:keys, :]).astype(BF16)
            return carry

        lax.fori_loop(0, 2, attend, 0)
        if i == 0:
            forward(1, 0)
            sides_ready(1, 0)
            across_ready(1)
    loti = jnp.concatenate(
        [
            dot_nt(od_ref[0:16, 0:128], att[0, i]) + dot_nt(od_ref[0:16, 128:256], att[1, i])
            for i in range(2)
        ],
        axis=1,
    )
    lot[...] = loti.astype(BF16)
    push(lot, lotr, m_send.at[7], m_recv.at[7], dev(s, sib))

    multiply_sides(1, 0)
    multiply(1, lane_of(1, 0))
    far_ready(1, 0)
    multiply(1, lane_of(0, 2))
    forward(1, 1)
    sides_ready(1, 1)
    multiply_sides(1, 1)
    far_ready(1, 1)
    multiply(1, lane_of(1, 2))
    sg[...] = acc_g1[...].astype(BF16)
    slg[...] = acc_lg[...].astype(BF16)
    push(slg, slgr, m_send.at[5], m_recv.at[5], dev(s, sib))
    push(sg, sgr, m_send.at[6], m_recv.at[6], dev(s, sib))

    arrived(slgr, m_recv.at[5])
    arrived(sgr, m_recv.at[6])

    def cotangent(i, carry):
        lg = (acc_lg[i] + slgr[i].astype(F32)).astype(BF16)
        lgs[i] = lg
        ga = (acc_g0[i] + sgr[i].astype(F32) + SCALE * dot(lg, od_ref[...])).astype(BF16)
        gas[0, i] = ga[:, 0:128]
        gas[1, i] = ga[:, 128:256]
        return carry

    lax.fori_loop(0, 2, cotangent, 0)
    dkacc[...] = jnp.zeros(dkacc.shape, F32)
    dvacc[...] = jnp.zeros(dvacc.shape, F32)
    for i in range(2):
        keys = (i + 1) * HALF
        for hd in range(2):
            full = probs[hd, i, :, 0:keys]
            grad = dot_nt(gas[hd, i], vs[0:keys, :])
            delta = jnp.sum(full * grad, axis=-1, keepdims=True)
            ds = (full * (grad - delta)).astype(BF16)
            dq = INV_ROOT * dot(ds, ks[0:keys, :])
            dq0[i, :, hd * 128 : hd * 128 + 128] = unrotate(dq, i).astype(BF16)
            dkacc[0:keys, :] += dot_tn(ds, qs[hd, i])
            dvacc[0:keys, :] += dot_tn(full.astype(BF16), gas[hd, i])
    push(dq0, dq1, m_send.at[8], m_recv.at[8], dev(s, sib))
    for i in range(2):
        rows = slice(i * HALF, i * HALF + HALF)
        dk = unrotate(INV_ROOT * dkacc[rows, :], i)
        dv = dvacc[rows, :]
        low_side = jnp.concatenate([dk[:, 0:64], dv[:, 0:64]], axis=1)
        high_side = jnp.concatenate([dk[:, 64:128], dv[:, 64:128]], axis=1)
        mown[i] = jnp.where(a == 0, low_side, high_side).astype(BF16)
        moth[i] = jnp.where(a == 0, high_side, low_side).astype(BF16)
    push(moth, dkvr.at[1], m_send.at[9], m_recv.at[9], dev(s, twin))
    push(mown, dkvr.at[0], m_send.at[11], m_recv.at[11], dev(s, sib))

    kv_rows = kvf[0:32, :].astype(F32)
    kv_low = jnp.concatenate([kv_rows[:, 0:64], kv_rows[:, 128:192]], axis=1)
    kv_high = jnp.concatenate([kv_rows[:, 64:128], kv_rows[:, 192:256]], axis=1)
    kv_chip = jnp.where(a == 0, kv_low, kv_high).astype(BF16)
    kv_chip = jnp.concatenate([kv_chip, jnp.zeros((96, 128), BF16)], axis=0)
    sib_up = jnp.concatenate([qups[...], jnp.zeros((112, 256), BF16)], axis=0)

    arrived(dkvr.at[1], m_recv.at[9])
    push(dkvr.at[1], dkvr.at[2], m_send.at[10], m_recv.at[10], dev(s, sib))
    arrived(dq1, m_recv.at[8])
    arrived(dkvr.at[2], m_recv.at[10])
    arrived(dkvr.at[0], m_recv.at[11])
    back_t = []
    for i in range(2):
        total = (
            mown[i].astype(F32) + dkvr[0, i].astype(F32)
            + dkvr[1, i].astype(F32) + dkvr[2, i].astype(F32)
        ).astype(BF16)
        back = SCALE * (
            dot_nt(dq0[i], qup_ref[...]) + dot_nt(dq1[i], sib_up) + dot_nt(total, kv_chip)
        )
        kb[i, :, 0:128] = total
        kb[i, :, 128:256] = back.astype(BF16)
        back_t.append(back.T[0:32, :])

    def dx_block(b, i):
        return dot_nt(dq0[i], wqa[b]) + dot_nt(dq1[i], wqb[b]) + dot(kb[i], wkv[b].reshape(256, BLK))

    def far_block(r):
        def one(i, carry):
            st[r, 0, i] = dx_block(lane_of(r, 2), i).astype(BF16)
            return carry

        lax.fori_loop(0, 2, one, 0)
        push(st.at[r, 0, 0], rsr.at[r, 0], rs_send.at[r, 0], rs_recv.at[r, 0], dev(s, right))
        push(st.at[r, 0, 1], rsr.at[r, 1], rs_send.at[r, 1], rs_recv.at[r, 1], dev(s, left))

    def side_cross(d, i, extra):
        k = 1 if d == 1 else 2
        total = dx_block(lane_of(1, d), i)
        arrived(rsr.at[1, extra], rs_recv.at[1, extra])
        total += rsr[1, extra].astype(F32)
        st[1, k, i] = total.astype(BF16)
        slot = 2 * k + 1 - i
        push(st.at[1, k, i], rsr.at[1, slot], rs_send.at[1, slot], rs_recv.at[1, slot], beyond[i])

    def side_next(d, i, slot):
        k = 1 if d == 1 else 2
        st[1, k, i] = dx_block(lane_of(1, d), i).astype(BF16)
        push(st.at[1, k, i], rsr.at[1, slot], rs_send.at[1, slot], rs_recv.at[1, slot],
             dev(s, right if d == 1 else left))

    def side_home(d, i, extra):
        k = 1 if d == 1 else 2
        slot = 2 * k + i
        total = dx_block(lane_of(0, d), i)
        if extra is not None:
            arrived(rsr.at[0, extra], rs_recv.at[0, extra])
            total += rsr[0, extra].astype(F32)
        else:
            arrived(rsr.at[1, slot], rs_recv.at[1, slot])
            total += rsr[1, slot].astype(F32)
        st[0, k, i] = total.astype(BF16)
        push(st.at[0, k, i], rsr.at[0, slot], rs_send.at[0, slot], rs_recv.at[0, slot],
             dev(s, right if d == 1 else left))

    far_block(1)

    arrived(lotr, m_recv.at[7])
    back_full = jnp.concatenate(back_t, axis=1).astype(BF16)
    low_out = (SCALE * (loti + lotr[...].astype(F32))).astype(BF16)
    out_full = jnp.concatenate(
        [jnp.zeros((16, ROWS), BF16), jnp.zeros((8, ROWS), BF16), low_out[0:8]], axis=0
    )

    def adapters(j, carry):
        total = jnp.zeros((32, BLK), F32)
        for i in range(2):
            cols = slice(i * HALF, i * HALF + HALF)
            total += dot(back_full[:, cols], buf[0, j, i]) + dot(out_full[:, cols], buf[1, j, i])
        du[j, 0] = total[0:16].astype(BF16)
        du[j, 1] = total[16:32].astype(BF16)
        return carry

    lax.fori_loop(0, LANES, adapters, 0)
    for d in range(1, 16):
        lo, j = plane_peer(d)
        push(du.at[j, lo], r1buf.at[d - 1], s_send.at[0, d], s_recv.at[0, d],
             dev(z * 2 + lo, j * 2 + c))

    low_t = jnp.concatenate([low[i].astype(F32).T[0:32] for i in range(2)], axis=1).astype(BF16)
    lg_t = jnp.concatenate([lgs[i].astype(F32).T[0:16] for i in range(2)], axis=1).astype(BF16)
    query_up = jnp.zeros((32, 256), F32)
    kv_up = jnp.zeros((32, 128), F32)
    out_down = jnp.zeros((16, 256), F32)
    for i in range(2):
        cols = slice(i * HALF, i * HALF + HALF)
        query_up += dot(low_t[:, cols], dq0[i])
        kv_up += dot(low_t[:, cols], kb[i, :, 0:128])
        out_down += jnp.concatenate(
            [dot(lg_t[:, cols], att[0, i]), dot(lg_t[:, cols], att[1, i])], axis=1
        )
    lane_col = lax.broadcasted_iota(jnp.int32, (8, 128), 1)
    kv_grad = SCALE * jnp.where(lane_col < 64, kv_up[8:16], kv_up[16:24])
    alone = jnp.concatenate(
        [
            jnp.concatenate([SCALE * query_up[0:8], SCALE * out_down[0:8]], axis=1),
            jnp.concatenate([kv_grad, jnp.zeros((8, 384), F32)], axis=1),
        ],
        axis=0,
    ).astype(BF16)
    al[0] = alone[:, 0:256]
    al[1] = alone[:, 256:512]
    push(al.at[1 - k_lo], alr, s_send.at[4, 1], s_recv.at[4, 1], dev(z * 2 + 1 - k_lo, h))
    side_next(1, 1, 2)
    side_next(-1, 0, 5)
    far_block(0)
    side_cross(1, 0, 0)
    side_cross(-1, 1, 1)

    shared = du[lane, k_lo].astype(F32)
    for d in range(1, 16):
        arrived(r1buf.at[d - 1], s_recv.at[0, d])
        shared += r1buf[d - 1].astype(F32)
    arrived(alr, s_recv.at[4, 1])
    single = al[k_lo].astype(F32) + alr[...].astype(F32)
    for k in range(8):
        r, g = k // 4, k % 4
        pieces[k, 0] = shared[8 * r : 8 * r + 8, g * 128 : g * 128 + 128]
        r, g = k // 2, k % 2
        if k < 4:
            pieces[k, 1] = single[8 * r : 8 * r + 8, g * 128 : g * 128 + 128]
        else:
            pieces[k, 1] = jnp.zeros((8, 128), F32)
    for d in range(1, 8):
        owner = column_peer(d)
        push(pieces.at[owner], r2buf.at[d - 1], s_send.at[1, d], s_recv.at[1, d],
             dev(owner * 2 + k_lo, h))
    mine = pieces[z]
    for d in range(1, 8):
        arrived(r2buf.at[d - 1], s_recv.at[1, d])
        mine += r2buf[d - 1]
    tiles[place_in_plane] = mine[0]
    for d in range(1, 16):
        lo, j = plane_peer(d)
        push(tiles.at[place_in_plane], tiles.at[place_in_plane], s_send.at[2, d],
             s_recv.at[2, d], dev(z * 2 + lo, j * 2 + c))
    tiles[16 + k_lo] = mine[1]
    push(tiles.at[16 + k_lo], tiles.at[16 + k_lo], s_send.at[4, 2], s_recv.at[4, 2],
         dev(z * 2 + 1 - k_lo, h))

    for i, slot in ((0, 5), (1, 2)):
        total = dx_block(lane_of(1, 0), i)
        arrived(rsr.at[1, slot], rs_recv.at[1, slot])
        yst[i] = (total + rsr[1, slot].astype(F32)).astype(BF16)
        half = i + p - 2 * i * p
        push(yst.at[i], yrecv.at[half], y_send.at[2, i], y_recv.at[2, half],
             dev(lax.rem(s + i * p, SEQ), across))
    side_home(1, 0, 0)
    side_home(-1, 1, 1)
    for d in range(1, 16):
        m = lax.rem(place_in_plane - d + 16, 16)
        arrived(tiles.at[m], s_recv.at[2, d])
    arrived(tiles.at[17 - k_lo], s_recv.at[4, 2])
    for k in range(9):
        eb[c, z, k] = jnp.concatenate([tiles[2 * k], tiles[2 * k + 1]], axis=0).astype(BF16)
    for d in range(1, 8):
        push(eb.at[c, z], eb.at[c, z], s_send.at[3, d], s_recv.at[3, d],
             dev(column_peer(d) * 2 + k_lo, h))
    side_home(1, 1, None)
    side_home(-1, 0, None)
    after = lax.rem(s + 1, SEQ)

    def send_back():
        return remote(rollst, rollrecv, roll_send.at[2], roll_recv.at[2], dev(after, h))

    rolled_sends.append(send_back)
    for i in (1, 0):
        total = dx_block(lane, i)
        for k in (2, 4):
            arrived(rsr.at[0, k + i], rs_recv.at[0, k + i])
            total += rsr[0, k + i].astype(F32)
        rown[i] = total
        if i == 1:

            @pl.when(p == 1)
            def _():
                rollst[...] = rown[1].astype(BF16)
                send_back().start()

    for d in range(1, 8):
        arrived(eb.at[c, lax.rem(z - d + 8, 8)], s_recv.at[3, d])
    push(eb.at[c], eb.at[c], s_send.at[4, 0], s_recv.at[4, 0], dev(s, sib))
    for g in range(4):
        cols = slice(g * 128, g * 128 + 128)
        pair = eb[c, 4 + g, 4 + lane // 2].astype(F32)
        small_ref[0:8, cols] = jnp.where(lax.rem(lane, 2) == 0, pair[0:8], pair[8:16])
    for g in range(2):
        pair = eb[c, g, 8].astype(F32)
        small_ref[8:16, g * 128 : g * 128 + 128] = pair[0:8]
        small_ref[8:16, 256 + g * 128 : 384 + g * 128] = pair[8:16]
    kv_out = eb[c, 2, 8].astype(F32)[0:8]
    small_ref[16:24, :] = jnp.zeros((8, BLK), F32)
    small_ref[16:24, 0:64] = jnp.concatenate(
        [
            jnp.where(c == 0, kv_out[:, 0:32], kv_out[:, 32:64]),
            jnp.where(c == 0, kv_out[:, 64:96], kv_out[:, 96:128]),
        ],
        axis=1,
    )

    for half in range(2):
        arrived(yrecv.at[half], y_recv.at[2, half])

    @pl.when(p == 0)
    def _():
        for i in range(2):
            dx_ref[i * HALF : i * HALF + HALF, :] = (rown[i] + yrecv[i].astype(F32)).astype(BF16)

    @pl.when(p == 1)
    def _():
        arrived(rollrecv, roll_recv.at[2])
        dx_ref[HALF:ROWS, :] = (rown[0] + yrecv[1].astype(F32)).astype(BF16)
        dx_ref[0:HALF, :] = (rollrecv[...].astype(F32) + yrecv[0].astype(F32)).astype(BF16)

    arrived(eb.at[1 - c], s_recv.at[4, 0])

    def place(j, carry):
        for core in range(2):
            for g in range(4):
                cols = pl.ds(pl.multiple_of((2 * j + core) * BLK + g * 128, 128), 128)
                for r in range(3):
                    pair = eb[core, r % 2 * 4 + g, r // 2 * 4 + j // 2].astype(F32)
                    dgrad_ref[8 * r : 8 * r + 8, cols] = jnp.where(
                        lax.rem(j, 2) == 0, pair[0:8], pair[8:16]
                    )
        return carry

    lax.fori_loop(0, LANES, place, 0)

    for copy in sends:
        copy.wait_send()

    @pl.when(p == 1)
    def _():
        for copy in rolled_sends:
            copy().wait_send()


def finish(dx_ref, dgrad_ref, small_ref, out_dx, out_down, out_qg, out_kvg, out_odg, out_oug):
    out_dx[...] = dx_ref[...]
    for r in range(3):
        out_down[r] = dgrad_ref[r * RANK : (r + 1) * RANK, :]
    out_qg[...] = small_ref[8:16, 0:256]
    out_odg[...] = small_ref[8:16, 256:512]
    out_oug[...] = small_ref[0:8, :]
    out_kvg[:, 0, :] = small_ref[16:24, 0:32]
    out_kvg[:, 1, :] = small_ref[16:24, 32:64]


def body(normed, output_gradient, query_weight, key_value_weight, output_weight,
         adapter_down, query_up, key_value_up, output_down, output_up):
    h = lax.axis_index("head")
    s = lax.axis_index("seq")
    c = lax.rem(h, 2)
    p = h // 8
    width = adapter_down.shape[2]

    positions = lax.rem(
        s * ROWS + jnp.arange(ROWS, dtype=jnp.int32) + p * HALF, TOKENS
    ).astype(F32)
    half_dim = HEAD_SIZE // 2
    frequency = ROPE_BASE ** (-jnp.arange(half_dim, dtype=F32) * 2.0 / HEAD_SIZE)
    angles = positions[:, None] * frequency[None, :]
    cos, sin = jnp.cos(angles), jnp.sin(angles)
    cos_wide = jnp.concatenate([cos, cos], axis=1).reshape(2, HALF, HEAD_SIZE)
    sin_wide = jnp.concatenate([-sin, sin], axis=1).reshape(2, HALF, HEAD_SIZE)

    kvt = key_value_weight.transpose(1, 2, 0)
    wq = query_weight.reshape(LANES, 2, BLK, 256)

    vm = lambda *shape: pltpu.VMEM(shape, BF16)
    vf = lambda *shape: pltpu.VMEM(shape, F32)
    dma = lambda *shape: pltpu.SemaphoreType.DMA(shape)
    out_shape = [
        jax.ShapeDtypeStruct((ROWS, BLK), BF16),
        jax.ShapeDtypeStruct((3 * RANK, width), F32),
        jax.ShapeDtypeStruct((3 * RANK, BLK), F32),
    ]
    hbm = pl.BlockSpec(memory_space=pl.ANY)
    vmem = pl.BlockSpec(memory_space=pltpu.VMEM)
    scratch = [
        vm(2, LANES, 2, HALF, BLK), vm(LANES, BLK, 256), vm(LANES, BLK, 256),
        vm(LANES, 4, 2, 32, BLK), vm(LANES, 256, BLK), vm(LANES, 256, BLK),
        vm(LANES, 128, BLK), vm(16, 256), vm(3, 32, 256), vm(128, 256),
        vm(128, 256), vm(32, 256), vm(128, 256), vm(16, BLK),
        vf(2, HALF, 256), vf(2, HALF, 256), vf(2, HALF, 256), vf(2, HALF, 256),
        vf(2, HALF, 256), vf(2, HALF, 128),
        vm(2, HALF, 256), vm(2, HALF, 256), vm(2, HALF, 128), vm(2, HALF, 128),
        vm(2, HALF, 128), vm(3, 2, HALF, 128), vm(2, HALF, 256), vm(2, HALF, 256),
        vm(2, HALF, 128), vm(2, HALF, 128),
        vf(2, 2, HALF, ROWS), vm(2, 2, HALF, 128), vm(ROWS, 128), vm(ROWS, 128),
        vm(2, 2, HALF, 128), vm(2, 2, HALF, 128), vm(2, HALF, 128), vm(2, HALF, 128),
        vf(ROWS, 128), vf(ROWS, 128),
        vm(2, HALF, 256), vm(2, HALF, 256), vm(2, HALF, 256), vm(16, ROWS), vm(16, ROWS),
        vm(2, HALF, 128), vm(2, HALF, 128), vm(3, 2, HALF, 128),
        vm(2, 3, 2, HALF, BLK), vm(2, 6, HALF, BLK), vf(2, HALF, BLK), vm(2, HALF, BLK),
        vm(2, HALF, BLK), vm(HALF, BLK), vm(HALF, BLK),
        vm(LANES, 2, 16, BLK), vm(15, 16, BLK), vm(2, 16, 256), vm(16, 256), vf(8, 2, 8, 128),
        vf(7, 2, 8, 128), vf(18, 8, 128), vm(2, 8, 9, 16, 128),
        dma(21), dma(30), dma(30), dma(2, 2, 6), dma(2, 2, 6), dma(3, 2), dma(3, 2),
        dma(3), dma(3), dma(12), dma(12), dma(2, 6), dma(2, 6), dma(5, 16), dma(5, 16),
    ]
    dx, dgrad, small = pl.pallas_call(
        kernel,
        out_shape=out_shape,
        in_specs=[hbm] * 5 + [vmem] * 7,
        out_specs=[vmem] * 3,
        scratch_shapes=scratch,
        compiler_params=pltpu.CompilerParams(
            collective_id=0, has_side_effects=True, vmem_limit_bytes=56 * 1024 * 1024
        ),
        cost_estimate=pl.CostEstimate(
            flops=9_000_000_000, bytes_accessed=20_000_000, transcendentals=400_000
        ),
    )(
        normed, output_gradient, wq, kvt, output_weight, adapter_down.reshape(3 * RANK, width),
        query_up, key_value_up.reshape(RANK, 64), output_down, output_up, cos_wide, sin_wide,
    )
    return tuple(
        pl.pallas_call(
            finish,
            out_shape=[
                jax.ShapeDtypeStruct((ROWS, BLK), BF16),
                jax.ShapeDtypeStruct((3, RANK, width), F32),
                jax.ShapeDtypeStruct((RANK, 256), F32),
                jax.ShapeDtypeStruct((RANK, 2, 32), F32),
                jax.ShapeDtypeStruct((RANK, 256), F32),
                jax.ShapeDtypeStruct((RANK, BLK), F32),
            ],
            in_specs=[vmem] * 3,
            out_specs=[vmem] * 6,
        )(dx, dgrad, small)
    )


def solution(mesh):
    return jax.shard_map(
        body,
        mesh=mesh,
        in_specs=(
            P("seq", "head"), P("seq", "head"), P(None, "head"), P(None, None, "head"),
            P("head", None), P(), P(None, "head"), P(None, None, "head"),
            P(None, "head"), P(None, "head"),
        ),
        out_specs=(
            P("seq", "head"), P(), P(None, "head"), P(None, None, "head"),
            P(None, "head"), P(None, "head"),
        ),
        check_vma=False,
    )
```

```python
import math

import jax
import jax.numpy as jnp
from jax import lax
from jax.experimental import pallas as pl
from jax.experimental.pallas import tpu as pltpu
from jax.sharding import PartitionSpec as P

MESH = pl.DeviceIdType.MESH
F32 = jnp.float32
BF16 = jnp.bfloat16

HEAD_SIZE = 128
RANK = 8
SCALE = 2.0
ROPE_BASE = 10000.0
ROWS = 512
HALF = 256
BLK = 512
SEQ = 16
LANES = 8
TOKENS = 8192
INV_ROOT = 1.0 / math.sqrt(HEAD_SIZE)


def dot(a, b):
    return lax.dot_general(a, b, (((1,), (0,)), ((), ())), preferred_element_type=F32)


def dot_nt(a, b):
    return lax.dot_general(a, b, (((1,), (1,)), ((), ())), preferred_element_type=F32)


def dot_tn(a, b):
    return lax.dot_general(a, b, (((0,), (0,)), ((), ())), preferred_element_type=F32)


def kernel(
    x_ref, g_ref, wq_ref, kvt_ref, wo_ref, down_ref, qup_in, kvup_in, od_in, up_in, cos_in, sin_in,
    dx_ref, dgrad_ref, small_ref,
    buf, wqa, wqb, wkv, woa, wob, upb, qups, kvur, kvf, qup_ref, kvup_ref, od_ref, up_ref, cos_ref, sin_ref,
    acc_q0, acc_q1, acc_kd, acc_g0, acc_g1, acc_lg,
    sq, sqr, lip, lipr, kvp, kvr, sg, sgr, slg, slgr,
    probs, qs, ks, vs, att, gas, low, lgs, dkacc, dvacc,
    dq0, dq1, kb, lot, lotr, mown, moth, dkvr,
    st, rsr, rown, yst, yrecv, rollst, rollrecv,
    ups, du, r1buf, al, alr, pieces, r2buf, tiles, eb,
    local_sem, w_send, w_recv, ag_send, ag_recv, y_send, y_recv, roll_send, roll_recv,
    m_send, m_recv, rs_send, rs_recv, s_send, s_recv,
):
    s = lax.axis_index("seq")
    h = lax.axis_index("head")
    c = lax.rem(h, 2)
    lane = h // 2
    p = lane // 4
    xi = lax.rem(lane, 4)
    a = lax.rem(xi, 2)
    q = 1 - p
    right = p * 8 + lax.rem(xi + 1, 4) * 2 + c
    left = p * 8 + lax.rem(xi + 3, 4) * 2 + c
    sib = h + 1 - 2 * c
    twin = h + 2 - 4 * a
    twin_sib = twin + 1 - 2 * c
    across = h + 8 - 16 * p
    z = s // 2
    k_lo = lax.rem(s, 2)
    place_in_plane = k_lo * 8 + lane

    def dev(seq, head):
        return (seq, head)

    def lane_of(r, d):
        plane = p if r == 0 else q
        return plane * 4 + lax.rem(xi + d + 4, 4)

    sends = []
    rolled_sends = []

    def remote(src, dst, ssem, rsem, device):
        return pltpu.make_async_remote_copy(
            src_ref=src, dst_ref=dst, send_sem=ssem, recv_sem=rsem,
            device_id=device, device_id_type=MESH,
        )

    def push(*ends):
        copy = remote(*ends)
        copy.start()
        sends.append(copy)

    def arrived(dst, rsem):
        pltpu.make_async_remote_copy(
            src_ref=dst, dst_ref=dst, send_sem=w_send.at[0], recv_sem=rsem,
            device_id=dev(s, sib), device_id_type=MESH,
        ).wait_recv()

    barrier = pltpu.get_barrier_semaphore()
    def plane_peer(d):
        m = lax.rem(place_in_plane + d, 16)
        return m // 8, lax.rem(m, 8)

    def column_peer(d):
        return lax.rem(z + d, 8)

    greeted = [dev(s, sib), dev(s, twin_sib)]
    greeted += [dev(lax.rem(s + 2 * p - 1 + SEQ, SEQ), across)]
    greeted += [dev(lax.rem(s + d, SEQ), h) for d in (1, SEQ - 1)]
    for d in range(1, 16):
        lo, j = plane_peer(d)
        greeted.append(dev(z * 2 + lo, j * 2 + c))
    greeted += [dev(column_peer(d) * 2 + k_lo, h) for d in range(1, 8)]
    for device in greeted:
        pl.semaphore_signal(barrier, inc=1, device_id=device, device_id_type=MESH)

    locals_ = []

    def fetch(src, dst, k):
        copy = pltpu.make_async_copy(src, dst, local_sem.at[k])
        copy.start()
        return copy

    blocks = []
    for t, ref in enumerate((x_ref, g_ref)):
        blocks.append(fetch(ref.at[pl.ds(HALF, HALF)], buf.at[t, lane, 1 - p], t))
    for t, ref in enumerate((x_ref, g_ref)):

        @pl.when(p == 0)
        def _():
            fetch(ref.at[pl.ds(0, HALF)], buf.at[t, lane, 0], 2 + t)

    weights = [
        fetch(wq_ref.at[:, c], wqa, 4),
    ]
    for j in range(LANES):
        cols = pl.ds(pl.multiple_of((2 * j + c) * BLK, BLK), BLK)
        weights.append(fetch(kvt_ref.at[:, :, cols], wkv.at[j, pl.ds(0, 2), c], 5 + j))
    for j in range(LANES):
        cols = pl.ds(pl.multiple_of((2 * j + c) * BLK, BLK), BLK)
        weights.append(fetch(wo_ref.at[:, cols], woa.at[j], 13 + j))

    for acc in (acc_q0, acc_q1, acc_kd, acc_g0, acc_g1, acc_lg):
        acc[...] = jnp.zeros(acc.shape, F32)
    upb[:, 16:, :] = jnp.zeros((LANES, 112, BLK), BF16)
    kvf[...] = jnp.zeros(kvf.shape, BF16)
    qup_ref[...] = jnp.concatenate([qup_in[...], jnp.zeros((120, 256), BF16)], axis=0)
    od_ref[...] = jnp.concatenate([od_in[...], jnp.zeros((120, 256), BF16)], axis=0)
    up_ref[...] = jnp.concatenate([up_in[...], jnp.zeros((8, BLK), BF16)], axis=0)
    upb[lane, 0:16, :] = up_ref[...]
    for i in range(2):
        cos_ref[i] = jnp.concatenate([cos_in[i], cos_in[i]], axis=1)
        sin_ref[i] = jnp.concatenate([-sin_in[i], sin_in[i]], axis=1)
    source = lax.broadcasted_iota(jnp.int32, (64, 256), 0)
    target = lax.broadcasted_iota(jnp.int32, (64, 256), 1)
    goal = source + lax.rem(h, 4) * 32 + jnp.where(source < 32, 0, 96)
    goals = jnp.where(target == goal, 1.0, 0.0).astype(BF16)
    spread = dot(kvup_in[:, 0, :], goals[0:32]) + dot(kvup_in[:, 1, :], goals[32:64])
    column = lax.broadcasted_iota(jnp.int32, (8, 256), 1)
    none = jnp.zeros((8, 256), F32)
    kvup_ref[...] = jnp.concatenate(
        [none, jnp.where(column < 128, spread, 0.0), jnp.where(column < 128, 0.0, spread), none],
        axis=0,
    ).astype(BF16)
    wkv[:, 2:4] = jnp.zeros((LANES, 2, 2, 32, BLK), BF16)
    for j in range(LANES):
        cols = pl.ds(pl.multiple_of((2 * j + c) * BLK, BLK), BLK)
        wkv[j, 2, 0] = jnp.concatenate([down_ref[:, cols], jnp.zeros((8, BLK), BF16)], axis=0)

    pl.semaphore_wait(barrier, len(greeted))

    def send_own(t, slot):
        push(buf.at[t, lane, slot], buf.at[t, lane, slot], ag_send.at[t, 0, slot],
             ag_recv.at[t, 0, slot], dev(s, right))
        push(buf.at[t, lane, slot], buf.at[t, lane, slot], ag_send.at[t, 0, 2 + slot],
             ag_recv.at[t, 0, 2 + slot], dev(s, left))

    beyond = [dev(lax.rem(s + i - q + SEQ, SEQ), across) for i in range(2)]

    def cross(t, b, i, k):
        push(buf.at[t, b, i], buf.at[t, b, 1 - i], ag_send.at[t, 1, k + 1 - i],
             ag_recv.at[t, 1, k + 1 - i], beyond[i])

    def send_roll(t, ref):
        before = lax.rem(s + SEQ - 1, SEQ)

        def copy():
            return remote(ref.at[pl.ds(0, HALF)], buf.at[t, lane, 1], roll_send.at[t],
                          roll_recv.at[t], dev(before, h))

        rolled_sends.append(copy)

        @pl.when(p == 1)
        def _():
            copy().start()

    def send_across(t, ref):
        push(ref.at[pl.ds(0, HALF)], buf.at[t, lane, q], y_send.at[t, 0], y_recv.at[t, q],
             dev(lax.rem(s - q + SEQ, SEQ), across))
        push(ref.at[pl.ds(HALF, HALF)], buf.at[t, lane, p], y_send.at[t, 1], y_recv.at[t, p],
             dev(s, across))

    def own_local(t):
        blocks[t].wait()

        @pl.when(p == 0)
        def _():
            pltpu.make_async_copy(
                (x_ref, g_ref)[t].at[pl.ds(0, HALF)], buf.at[t, lane, 0], local_sem.at[2 + t]
            ).wait()

    def own_rolled(t):
        @pl.when(p == 1)
        def _():
            arrived(buf.at[t, lane, 1], roll_recv.at[t])

    send_roll(0, x_ref)
    own_local(0)
    send_own(0, 0)
    send_across(0, x_ref)
    own_rolled(0)
    send_own(0, 1)
    push(wq_ref.at[:, 1 - c], wqb, w_send.at[0], w_recv.at[0], dev(s, sib))
    for j in range(LANES):
        cols = pl.ds(pl.multiple_of((2 * j + 1 - c) * BLK, BLK), BLK)
        push(kvt_ref.at[:, :, cols], wkv.at[j, pl.ds(0, 2), c], w_send.at[22 + j],
             w_recv.at[22 + j], dev(s, sib))
    for j in range(LANES):
        cols = pl.ds(pl.multiple_of((2 * j + 1 - c) * BLK, BLK), BLK)
        push(wo_ref.at[:, cols], wob.at[j], w_send.at[2 + j], w_recv.at[2 + j], dev(s, sib))
    for d in range(1, LANES):
        push(up_ref, upb.at[lane, pl.ds(0, 16)], w_send.at[10 + d], w_recv.at[10 + d],
             dev(s, lax.rem(lane + d, LANES) * 2 + c))
    push(qup_ref.at[pl.ds(0, 16)], qups, w_send.at[18], w_recv.at[18], dev(s, sib))
    for k, peer in enumerate((sib, twin, twin_sib)):
        push(kvup_ref, kvur.at[k], w_send.at[19 + k], w_recv.at[19 + k], dev(s, peer))

    def multiply(t, b):
        def rows(i, carry):
            block = buf[t, b, i]
            if t == 0:
                acc_q0[i] += dot(block, wqa[b])
                acc_q1[i] += dot(block, wqb[b])
                acc_kd[i] += dot_nt(block, wkv[b].reshape(256, BLK))
            else:
                acc_g0[i] += dot_nt(block, woa[b])
                acc_g1[i] += dot_nt(block, wob[b])
                acc_lg[i] += dot_nt(block, upb[b])
            return carry

        lax.fori_loop(0, 2, rows, 0)

    def multiply_sides(t, r):
        def one(k, carry):
            multiply(t, lane_of(r, 1 + 2 * k))
            return carry

        lax.fori_loop(0, 2, one, 0)

    def forward(t, r):
        from_left, from_right = lane_of(r, -1), lane_of(r, 1)
        arrived(buf.at[t, from_left, 0], ag_recv.at[t, r, 0])
        push(buf.at[t, from_left, 0], buf.at[t, from_left, 0], ag_send.at[t, r, 4],
             ag_recv.at[t, r, 4], dev(s, right))
        arrived(buf.at[t, from_right, 1], ag_recv.at[t, r, 3])
        push(buf.at[t, from_right, 1], buf.at[t, from_right, 1], ag_send.at[t, r, 5],
             ag_recv.at[t, r, 5], dev(s, left))

    def sides_ready(t, r):
        from_left, from_right = lane_of(r, -1), lane_of(r, 1)
        arrived(buf.at[t, from_right, 0], ag_recv.at[t, r, 2])
        if r == 0:
            cross(t, from_right, 0, 2)
        arrived(buf.at[t, from_left, 1], ag_recv.at[t, r, 1])
        if r == 0:
            cross(t, from_left, 1, 0)

    def far_ready(t, r):
        far = lane_of(r, 2)
        arrived(buf.at[t, far, 0], ag_recv.at[t, r, 4])
        arrived(buf.at[t, far, 1], ag_recv.at[t, r, 5])

    def across_ready(t):
        b = lane_of(1, 0)
        for slot, device, k in ((0, left, 2), (1, right, 1)):
            arrived(buf.at[t, b, slot], y_recv.at[t, slot])
            push(buf.at[t, b, slot], buf.at[t, b, slot], ag_send.at[t, 1, k],
                 ag_recv.at[t, 1, k], dev(s, device))

    forward(0, 0)
    sides_ready(0, 0)
    across_ready(0)
    send_roll(1, g_ref)
    send_across(1, g_ref)
    for copy in weights[0:9]:
        copy.wait()
    arrived(wqb, w_recv.at[0])
    for j in range(LANES):
        arrived(wkv.at[j, pl.ds(0, 2), 1 - c], w_recv.at[22 + j])
    multiply(0, lane)
    own_local(1)
    send_own(1, 0)
    forward(0, 1)
    own_rolled(1)
    send_own(1, 1)
    multiply_sides(0, 0)
    multiply(0, lane_of(1, 0))
    far_ready(0, 0)
    multiply(0, lane_of(0, 2))
    sides_ready(0, 1)
    multiply_sides(0, 1)
    far_ready(0, 1)
    multiply(0, lane_of(1, 2))

    sq[...] = acc_q1[...].astype(BF16)
    kvp[...] = acc_kd[:, :, 0:128].astype(BF16)
    lip[...] = acc_kd[:, :, 128:256].astype(BF16)
    push(kvp, kvr.at[1], m_send.at[1], m_recv.at[1], dev(s, twin))
    push(kvp, kvr.at[0], m_send.at[0], m_recv.at[0], dev(s, sib))
    push(lip, lipr, m_send.at[3], m_recv.at[3], dev(s, sib))
    push(sq, sqr, m_send.at[4], m_recv.at[4], dev(s, sib))

    for copy in weights[9:]:
        copy.wait()
    for j in range(LANES):
        arrived(wob.at[j], w_recv.at[2 + j])
    for d in range(1, LANES):
        arrived(upb.at[lax.rem(lane - d + LANES, LANES), pl.ds(0, 16)], w_recv.at[10 + d])
    multiply(1, lane)
    forward(1, 0)
    sides_ready(1, 0)
    across_ready(1)

    for k in range(3):
        arrived(kvur.at[k], w_recv.at[19 + k])
    arrived(qups, w_recv.at[18])
    kvf[0:32, :] = kvup_ref[0:32, :] + kvur[0] + kvur[1] + kvur[2]
    arrived(kvr.at[1], m_recv.at[1])
    push(kvr.at[1], kvr.at[2], m_send.at[2], m_recv.at[2], dev(s, sib))
    arrived(kvr.at[0], m_recv.at[0])
    arrived(kvr.at[2], m_recv.at[2])
    arrived(lipr, m_recv.at[3])
    arrived(sqr, m_recv.at[4])

    def rotate(v, i):
        return v * cos_ref[i] + pltpu.roll(v, 64, 1) * sin_ref[i]

    def unrotate(v, i):
        return v * cos_ref[i] - pltpu.roll(v, 64, 1) * sin_ref[i]

    def project(i, carry):
        low_i = (acc_kd[i, :, 128:256] + lipr[i].astype(F32)).astype(BF16)
        low[i] = low_i
        q_i = (acc_q0[i] + sqr[i].astype(F32) + SCALE * dot(low_i, qup_ref[...])).astype(BF16)
        for hd in range(2):
            cols = slice(hd * 128, hd * 128 + 128)
            qs[hd, i] = rotate(q_i[:, cols].astype(F32), i).astype(BF16)
        own = acc_kd[i, :, 0:128] + kvr[0, i].astype(F32)
        other = kvr[1, i].astype(F32) + kvr[2, i].astype(F32)
        first = jnp.where(a == 0, own, other)
        second = jnp.where(a == 0, other, own)
        rank = SCALE * dot(low_i, kvf[...])
        k_i = jnp.concatenate([first[:, 0:64], second[:, 0:64]], axis=1) + rank[:, 0:128]
        v_i = jnp.concatenate([first[:, 64:128], second[:, 64:128]], axis=1) + rank[:, 128:256]
        start = pl.multiple_of(i * HALF, HALF)
        ks[pl.ds(start, HALF), :] = rotate(k_i.astype(BF16).astype(F32), i).astype(BF16)
        vs[pl.ds(start, HALF), :] = v_i.astype(BF16)
        return carry

    lax.fori_loop(0, 2, project, 0)

    for i in range(2):
        keys = (i + 1) * HALF

        def attend(hd, carry):
            scores = dot_nt(qs[hd, i], ks[0:keys, :]) * INV_ROOT
            row = lax.broadcasted_iota(jnp.int32, scores.shape, 0) + i * HALF
            col = lax.broadcasted_iota(jnp.int32, scores.shape, 1)
            e = jnp.where(col <= row, jnp.exp(scores), 0.0)
            full = e / jnp.sum(e, axis=-1, keepdims=True)
            probs[hd, i, :, 0:keys] = full
            att[hd, i] = dot(full.astype(BF16), vs[0:keys, :]).astype(BF16)
            return carry

        lax.fori_loop(0, 2, attend, 0)
    loti = jnp.concatenate(
        [
            dot_nt(od_ref[0:16, 0:128], att[0, i]) + dot_nt(od_ref[0:16, 128:256], att[1, i])
            for i in range(2)
        ],
        axis=1,
    )
    lot[...] = loti.astype(BF16)
    push(lot, lotr, m_send.at[7], m_recv.at[7], dev(s, sib))

    multiply_sides(1, 0)
    multiply(1, lane_of(1, 0))
    far_ready(1, 0)
    multiply(1, lane_of(0, 2))
    forward(1, 1)
    sides_ready(1, 1)
    multiply_sides(1, 1)
    far_ready(1, 1)
    multiply(1, lane_of(1, 2))
    sg[...] = acc_g1[...].astype(BF16)
    slg[...] = acc_lg[...].astype(BF16)
    push(slg, slgr, m_send.at[5], m_recv.at[5], dev(s, sib))
    push(sg, sgr, m_send.at[6], m_recv.at[6], dev(s, sib))

    arrived(slgr, m_recv.at[5])
    arrived(sgr, m_recv.at[6])

    def cotangent(i, carry):
        lg = (acc_lg[i] + slgr[i].astype(F32)).astype(BF16)
        lgs[i] = lg
        ga = (acc_g0[i] + sgr[i].astype(F32) + SCALE * dot(lg, od_ref[...])).astype(BF16)
        gas[0, i] = ga[:, 0:128]
        gas[1, i] = ga[:, 128:256]
        return carry

    lax.fori_loop(0, 2, cotangent, 0)
    dkacc[...] = jnp.zeros(dkacc.shape, F32)
    dvacc[...] = jnp.zeros(dvacc.shape, F32)

    def split_columns(kind, halves):
        for message, side in ((mown, a), (moth, 1 - a)):
            low_side = jnp.concatenate([half[:, 0:64] for half in halves], axis=1)
            high_side = jnp.concatenate([half[:, 64:128] for half in halves], axis=1)
            message[kind] = jnp.where(side == 0, low_side, high_side).astype(BF16)
        push(moth.at[kind], dkvr.at[1, kind], m_send.at[9 + 3 * kind], m_recv.at[9 + 3 * kind],
             dev(s, twin))
        push(mown.at[kind], dkvr.at[0, kind], m_send.at[11 + 3 * kind],
             m_recv.at[11 + 3 * kind], dev(s, sib))

    def pass_on(kind):
        arrived(dkvr.at[1, kind], m_recv.at[9 + 3 * kind])
        push(dkvr.at[1, kind], dkvr.at[2, kind], m_send.at[10 + 3 * kind],
             m_recv.at[10 + 3 * kind], dev(s, sib))

    for i in range(2):
        keys = (i + 1) * HALF
        for hd in range(2):
            dvacc[0:keys, :] += dot_tn(probs[hd, i, :, 0:keys].astype(BF16), gas[hd, i])
    split_columns(1, [dvacc[0:HALF, :], dvacc[HALF:ROWS, :]])
    for i in range(2):
        keys = (i + 1) * HALF
        for hd in range(2):
            full = probs[hd, i, :, 0:keys]
            grad = dot_nt(gas[hd, i], vs[0:keys, :])
            delta = jnp.sum(full * grad, axis=-1, keepdims=True)
            ds = (full * (grad - delta)).astype(BF16)
            dq = INV_ROOT * dot(ds, ks[0:keys, :])
            dq0[i, :, hd * 128 : hd * 128 + 128] = unrotate(dq, i).astype(BF16)
            dkacc[0:keys, :] += dot_tn(ds, qs[hd, i])
    push(dq0, dq1, m_send.at[8], m_recv.at[8], dev(s, sib))
    split_columns(
        0,
        [unrotate(INV_ROOT * dkacc[i * HALF : i * HALF + HALF, :], i) for i in range(2)],
    )
    pass_on(1)

    arrived(lotr, m_recv.at[7])
    low_out = (SCALE * (loti + lotr[...].astype(F32))).astype(BF16)

    def out_up(j, carry):
        total = jnp.zeros((16, BLK), F32)
        for i in range(2):
            total += dot(low_out[:, i * HALF : i * HALF + HALF], buf[1, j, i])
        ups[j] = total[0:8]
        return carry

    lax.fori_loop(0, LANES, out_up, 0)

    kv_rows = kvf[0:32, :].astype(F32)
    kv_low = jnp.concatenate([kv_rows[:, 0:64], kv_rows[:, 128:192]], axis=1)
    kv_high = jnp.concatenate([kv_rows[:, 64:128], kv_rows[:, 192:256]], axis=1)
    kv_chip = jnp.where(a == 0, kv_low, kv_high).astype(BF16)
    kv_chip = jnp.concatenate([kv_chip, jnp.zeros((96, 128), BF16)], axis=0)
    sib_up = jnp.concatenate([qups[...], jnp.zeros((112, 256), BF16)], axis=0)

    pass_on(0)
    arrived(dq1, m_recv.at[8])
    for kind in (1, 0):
        arrived(dkvr.at[2, kind], m_recv.at[10 + 3 * kind])
        arrived(dkvr.at[0, kind], m_recv.at[11 + 3 * kind])
    back_t = []
    for i in range(2):
        cols = slice(i * 64, i * 64 + 64)
        total = jnp.concatenate(
            [
                mown[kind].astype(F32)[:, cols] + dkvr[0, kind].astype(F32)[:, cols]
                + dkvr[1, kind].astype(F32)[:, cols] + dkvr[2, kind].astype(F32)[:, cols]
                for kind in range(2)
            ],
            axis=1,
        ).astype(BF16)
        back = SCALE * (
            dot_nt(dq0[i], qup_ref[...]) + dot_nt(dq1[i], sib_up) + dot_nt(total, kv_chip)
        )
        kb[i, :, 0:128] = total
        kb[i, :, 128:256] = back.astype(BF16)
        back_t.append(back.T[0:32, :])

    def dx_block(b, i):
        return dot_nt(dq0[i], wqa[b]) + dot_nt(dq1[i], wqb[b]) + dot(kb[i], wkv[b].reshape(256, BLK))

    def far_block(r):
        def one(i, carry):
            st[r, 0, i] = dx_block(lane_of(r, 2), i).astype(BF16)
            return carry

        lax.fori_loop(0, 2, one, 0)
        push(st.at[r, 0, 0], rsr.at[r, 0], rs_send.at[r, 0], rs_recv.at[r, 0], dev(s, right))
        push(st.at[r, 0, 1], rsr.at[r, 1], rs_send.at[r, 1], rs_recv.at[r, 1], dev(s, left))

    def side_cross(d, i, extra):
        k = 1 if d == 1 else 2
        total = dx_block(lane_of(1, d), i)
        arrived(rsr.at[1, extra], rs_recv.at[1, extra])
        total += rsr[1, extra].astype(F32)
        st[1, k, i] = total.astype(BF16)
        slot = 2 * k + 1 - i
        push(st.at[1, k, i], rsr.at[1, slot], rs_send.at[1, slot], rs_recv.at[1, slot], beyond[i])

    def side_next(d, i, slot):
        k = 1 if d == 1 else 2
        st[1, k, i] = dx_block(lane_of(1, d), i).astype(BF16)
        push(st.at[1, k, i], rsr.at[1, slot], rs_send.at[1, slot], rs_recv.at[1, slot],
             dev(s, right if d == 1 else left))

    def side_home(d, i, extra):
        k = 1 if d == 1 else 2
        slot = 2 * k + i
        total = dx_block(lane_of(0, d), i)
        if extra is not None:
            arrived(rsr.at[0, extra], rs_recv.at[0, extra])
            total += rsr[0, extra].astype(F32)
        else:
            arrived(rsr.at[1, slot], rs_recv.at[1, slot])
            total += rsr[1, slot].astype(F32)
        st[0, k, i] = total.astype(BF16)
        push(st.at[0, k, i], rsr.at[0, slot], rs_send.at[0, slot], rs_recv.at[0, slot],
             dev(s, right if d == 1 else left))

    far_block(1)

    back_full = jnp.concatenate(back_t, axis=1).astype(BF16)

    def adapters(j, carry):
        total = jnp.zeros((32, BLK), F32)
        for i in range(2):
            total += dot(back_full[:, i * HALF : i * HALF + HALF], buf[0, j, i])
        du[j, 0] = total[0:16].astype(BF16)
        du[j, 1] = jnp.concatenate([total[16:24], ups[j]], axis=0).astype(BF16)
        return carry

    lax.fori_loop(0, LANES, adapters, 0)
    for d in range(1, 16):
        lo, j = plane_peer(d)
        push(du.at[j, lo], r1buf.at[d - 1], s_send.at[0, d], s_recv.at[0, d],
             dev(z * 2 + lo, j * 2 + c))

    low_t = jnp.concatenate([low[i].astype(F32).T[0:32] for i in range(2)], axis=1).astype(BF16)
    lg_t = jnp.concatenate([lgs[i].astype(F32).T[0:16] for i in range(2)], axis=1).astype(BF16)
    query_up = jnp.zeros((32, 256), F32)
    kv_up = jnp.zeros((32, 128), F32)
    out_down = jnp.zeros((16, 256), F32)
    for i in range(2):
        cols = slice(i * HALF, i * HALF + HALF)
        query_up += dot(low_t[:, cols], dq0[i])
        kv_up += dot(low_t[:, cols], kb[i, :, 0:128])
        out_down += jnp.concatenate(
            [dot(lg_t[:, cols], att[0, i]), dot(lg_t[:, cols], att[1, i])], axis=1
        )
    lane_col = lax.broadcasted_iota(jnp.int32, (8, 128), 1)
    kv_grad = SCALE * jnp.where(lane_col < 64, kv_up[8:16], kv_up[16:24])
    alone = jnp.concatenate(
        [
            jnp.concatenate([SCALE * query_up[0:8], SCALE * out_down[0:8]], axis=1),
            jnp.concatenate([kv_grad, jnp.zeros((8, 384), F32)], axis=1),
        ],
        axis=0,
    ).astype(BF16)
    al[0] = alone[:, 0:256]
    al[1] = alone[:, 256:512]
    push(al.at[1 - k_lo], alr, s_send.at[4, 1], s_recv.at[4, 1], dev(z * 2 + 1 - k_lo, h))
    side_next(1, 1, 2)
    side_next(-1, 0, 5)
    far_block(0)
    side_cross(1, 0, 0)
    side_cross(-1, 1, 1)

    shared = du[lane, k_lo].astype(F32)
    for d in range(1, 16):
        arrived(r1buf.at[d - 1], s_recv.at[0, d])
        shared += r1buf[d - 1].astype(F32)
    arrived(alr, s_recv.at[4, 1])
    single = al[k_lo].astype(F32) + alr[...].astype(F32)
    for k in range(8):
        r, g = k // 4, k % 4
        pieces[k, 0] = shared[8 * r : 8 * r + 8, g * 128 : g * 128 + 128]
        r, g = k // 2, k % 2
        if k < 4:
            pieces[k, 1] = single[8 * r : 8 * r + 8, g * 128 : g * 128 + 128]
        else:
            pieces[k, 1] = jnp.zeros((8, 128), F32)
    for d in range(1, 8):
        owner = column_peer(d)
        push(pieces.at[owner], r2buf.at[d - 1], s_send.at[1, d], s_recv.at[1, d],
             dev(owner * 2 + k_lo, h))
    mine = pieces[z]
    for d in range(1, 8):
        arrived(r2buf.at[d - 1], s_recv.at[1, d])
        mine += r2buf[d - 1]
    tiles[place_in_plane] = mine[0]
    for d in range(1, 16):
        lo, j = plane_peer(d)
        push(tiles.at[place_in_plane], tiles.at[place_in_plane], s_send.at[2, d],
             s_recv.at[2, d], dev(z * 2 + lo, j * 2 + c))
    tiles[16 + k_lo] = mine[1]
    push(tiles.at[16 + k_lo], tiles.at[16 + k_lo], s_send.at[4, 2], s_recv.at[4, 2],
         dev(z * 2 + 1 - k_lo, h))

    for i, slot in ((0, 5), (1, 2)):
        total = dx_block(lane_of(1, 0), i)
        arrived(rsr.at[1, slot], rs_recv.at[1, slot])
        yst[i] = (total + rsr[1, slot].astype(F32)).astype(BF16)
        half = i + p - 2 * i * p
        push(yst.at[i], yrecv.at[half], y_send.at[2, i], y_recv.at[2, half],
             dev(lax.rem(s + i * p, SEQ), across))
    side_home(1, 0, 0)
    side_home(-1, 1, 1)
    for d in range(1, 16):
        m = lax.rem(place_in_plane - d + 16, 16)
        arrived(tiles.at[m], s_recv.at[2, d])
    arrived(tiles.at[17 - k_lo], s_recv.at[4, 2])
    for k in range(9):
        eb[c, z, k] = jnp.concatenate([tiles[2 * k], tiles[2 * k + 1]], axis=0).astype(BF16)
    for d in range(1, 8):
        push(eb.at[c, z], eb.at[c, z], s_send.at[3, d], s_recv.at[3, d],
             dev(column_peer(d) * 2 + k_lo, h))
    side_home(1, 1, None)
    side_home(-1, 0, None)
    after = lax.rem(s + 1, SEQ)

    def send_back():
        return remote(rollst, rollrecv, roll_send.at[2], roll_recv.at[2], dev(after, h))

    rolled_sends.append(send_back)
    for i in (1, 0):
        total = dx_block(lane, i)
        for k in (2, 4):
            arrived(rsr.at[0, k + i], rs_recv.at[0, k + i])
            total += rsr[0, k + i].astype(F32)
        rown[i] = total
        if i == 1:

            @pl.when(p == 1)
            def _():
                rollst[...] = rown[1].astype(BF16)
                send_back().start()

    for d in range(1, 8):
        arrived(eb.at[c, lax.rem(z - d + 8, 8)], s_recv.at[3, d])
    push(eb.at[c], eb.at[c], s_send.at[4, 0], s_recv.at[4, 0], dev(s, sib))
    for g in range(4):
        cols = slice(g * 128, g * 128 + 128)
        pair = eb[c, 4 + g, 4 + lane // 2].astype(F32)
        small_ref[0:8, cols] = jnp.where(lax.rem(lane, 2) == 0, pair[0:8], pair[8:16])
    for g in range(2):
        pair = eb[c, g, 8].astype(F32)
        small_ref[8:16, g * 128 : g * 128 + 128] = pair[0:8]
        small_ref[8:16, 256 + g * 128 : 384 + g * 128] = pair[8:16]
    kv_out = eb[c, 2, 8].astype(F32)[0:8]
    small_ref[16:24, :] = jnp.zeros((8, BLK), F32)
    small_ref[16:24, 0:64] = jnp.concatenate(
        [
            jnp.where(c == 0, kv_out[:, 0:32], kv_out[:, 32:64]),
            jnp.where(c == 0, kv_out[:, 64:96], kv_out[:, 96:128]),
        ],
        axis=1,
    )

    for half in range(2):
        arrived(yrecv.at[half], y_recv.at[2, half])

    @pl.when(p == 0)
    def _():
        for i in range(2):
            dx_ref[i * HALF : i * HALF + HALF, :] = (rown[i] + yrecv[i].astype(F32)).astype(BF16)

    @pl.when(p == 1)
    def _():
        arrived(rollrecv, roll_recv.at[2])
        dx_ref[HALF:ROWS, :] = (rown[0] + yrecv[1].astype(F32)).astype(BF16)
        dx_ref[0:HALF, :] = (rollrecv[...].astype(F32) + yrecv[0].astype(F32)).astype(BF16)

    arrived(eb.at[1 - c], s_recv.at[4, 0])

    def place(j, carry):
        for core in range(2):
            for g in range(4):
                cols = pl.ds(pl.multiple_of((2 * j + core) * BLK + g * 128, 128), 128)
                for r in range(3):
                    pair = eb[core, r % 2 * 4 + g, r // 2 * 4 + j // 2].astype(F32)
                    dgrad_ref[8 * r : 8 * r + 8, cols] = jnp.where(
                        lax.rem(j, 2) == 0, pair[0:8], pair[8:16]
                    )
        return carry

    lax.fori_loop(0, LANES, place, 0)

    for copy in sends:
        copy.wait_send()

    @pl.when(p == 1)
    def _():
        for copy in rolled_sends:
            copy().wait_send()


def finish(dx_ref, dgrad_ref, small_ref, out_dx, out_down, out_qg, out_kvg, out_odg, out_oug):
    out_dx[...] = dx_ref[...]
    for r in range(3):
        out_down[r] = dgrad_ref[r * RANK : (r + 1) * RANK, :]
    out_qg[...] = small_ref[8:16, 0:256]
    out_odg[...] = small_ref[8:16, 256:512]
    out_oug[...] = small_ref[0:8, :]
    out_kvg[:, 0, :] = small_ref[16:24, 0:32]
    out_kvg[:, 1, :] = small_ref[16:24, 32:64]


def body(normed, output_gradient, query_weight, key_value_weight, output_weight,
         adapter_down, query_up, key_value_up, output_down, output_up):
    h = lax.axis_index("head")
    s = lax.axis_index("seq")
    c = lax.rem(h, 2)
    p = h // 8
    width = adapter_down.shape[2]

    positions = lax.rem(
        s * ROWS + jnp.arange(ROWS, dtype=jnp.int32) + p * HALF, TOKENS
    ).astype(F32)
    half_dim = HEAD_SIZE // 2
    frequency = ROPE_BASE ** (-jnp.arange(half_dim, dtype=F32) * 2.0 / HEAD_SIZE)
    angles = positions[:, None] * frequency[None, :]
    cos, sin = jnp.cos(angles), jnp.sin(angles)
    cos = cos.reshape(2, HALF, half_dim)
    sin = sin.reshape(2, HALF, half_dim)

    kvt = key_value_weight.transpose(1, 2, 0)
    wq = query_weight.reshape(LANES, 2, BLK, 256)

    vm = lambda *shape: pltpu.VMEM(shape, BF16)
    vf = lambda *shape: pltpu.VMEM(shape, F32)
    dma = lambda *shape: pltpu.SemaphoreType.DMA(shape)
    out_shape = [
        jax.ShapeDtypeStruct((ROWS, BLK), BF16),
        jax.ShapeDtypeStruct((3 * RANK, width), F32),
        jax.ShapeDtypeStruct((3 * RANK, BLK), F32),
    ]
    hbm = pl.BlockSpec(memory_space=pl.ANY)
    vmem = pl.BlockSpec(memory_space=pltpu.VMEM)
    scratch = [
        vm(2, LANES, 2, HALF, BLK), vm(LANES, BLK, 256), vm(LANES, BLK, 256),
        vm(LANES, 4, 2, 32, BLK), vm(LANES, 256, BLK), vm(LANES, 256, BLK),
        vm(LANES, 128, BLK), vm(16, 256), vm(3, 32, 256), vm(128, 256),
        vm(128, 256), vm(32, 256), vm(128, 256), vm(16, BLK), vf(2, HALF, HEAD_SIZE),
        vf(2, HALF, HEAD_SIZE),
        vf(2, HALF, 256), vf(2, HALF, 256), vf(2, HALF, 256), vf(2, HALF, 256),
        vf(2, HALF, 256), vf(2, HALF, 128),
        vm(2, HALF, 256), vm(2, HALF, 256), vm(2, HALF, 128), vm(2, HALF, 128),
        vm(2, HALF, 128), vm(3, 2, HALF, 128), vm(2, HALF, 256), vm(2, HALF, 256),
        vm(2, HALF, 128), vm(2, HALF, 128),
        vf(2, 2, HALF, ROWS), vm(2, 2, HALF, 128), vm(ROWS, 128), vm(ROWS, 128),
        vm(2, 2, HALF, 128), vm(2, 2, HALF, 128), vm(2, HALF, 128), vm(2, HALF, 128),
        vf(ROWS, 128), vf(ROWS, 128),
        vm(2, HALF, 256), vm(2, HALF, 256), vm(2, HALF, 256), vm(16, ROWS), vm(16, ROWS),
        vm(2, HALF, 128), vm(2, HALF, 128), vm(3, 2, HALF, 128),
        vm(2, 3, 2, HALF, BLK), vm(2, 6, HALF, BLK), vf(2, HALF, BLK), vm(2, HALF, BLK),
        vm(2, HALF, BLK), vm(HALF, BLK), vm(HALF, BLK),
        vf(LANES, 8, BLK), vm(LANES, 2, 16, BLK), vm(15, 16, BLK), vm(2, 16, 256), vm(16, 256), vf(8, 2, 8, 128),
        vf(7, 2, 8, 128), vf(18, 8, 128), vm(2, 8, 9, 16, 128),
        dma(21), dma(30), dma(30), dma(2, 2, 6), dma(2, 2, 6), dma(3, 2), dma(3, 2),
        dma(3), dma(3), dma(15), dma(15), dma(2, 6), dma(2, 6), dma(5, 16), dma(5, 16),
    ]
    dx, dgrad, small = pl.pallas_call(
        kernel,
        out_shape=out_shape,
        in_specs=[hbm] * 5 + [vmem] * 7,
        out_specs=[vmem] * 3,
        scratch_shapes=scratch,
        compiler_params=pltpu.CompilerParams(
            collective_id=0, has_side_effects=True, vmem_limit_bytes=56 * 1024 * 1024
        ),
        cost_estimate=pl.CostEstimate(
            flops=9_000_000_000, bytes_accessed=20_000_000, transcendentals=400_000
        ),
    )(
        normed, output_gradient, wq, kvt, output_weight, adapter_down.reshape(3 * RANK, width),
        query_up, key_value_up, output_down, output_up, cos, sin,
    )
    return tuple(
        pl.pallas_call(
            finish,
            out_shape=[
                jax.ShapeDtypeStruct((ROWS, BLK), BF16),
                jax.ShapeDtypeStruct((3, RANK, width), F32),
                jax.ShapeDtypeStruct((RANK, 256), F32),
                jax.ShapeDtypeStruct((RANK, 2, 32), F32),
                jax.ShapeDtypeStruct((RANK, 256), F32),
                jax.ShapeDtypeStruct((RANK, BLK), F32),
            ],
            in_specs=[vmem] * 3,
            out_specs=[vmem] * 6,
        )(dx, dgrad, small)
    )


def solution(mesh):
    return jax.shard_map(
        body,
        mesh=mesh,
        in_specs=(
            P("seq", "head"), P("seq", "head"), P(None, "head"), P(None, None, "head"),
            P("head", None), P(), P(None, "head"), P(None, None, "head"),
            P(None, "head"), P(None, "head"),
        ),
        out_specs=(
            P("seq", "head"), P(), P(None, "head"), P(None, None, "head"),
            P(None, "head"), P(None, "head"),
        ),
        check_vma=False,
    )
```

```python
import math

import jax
import jax.numpy as jnp
from jax import lax
from jax.experimental import pallas as pl
from jax.experimental.pallas import tpu as pltpu
from jax.sharding import PartitionSpec as P

MESH = pl.DeviceIdType.MESH
F32 = jnp.float32
BF16 = jnp.bfloat16

HEAD_SIZE = 128
RANK = 8
SCALE = 2.0
ROPE_BASE = 10000.0
ROWS = 512
HALF = 256
BLK = 512
SEQ = 16
LANES = 8
TOKENS = 8192
INV_ROOT = 1.0 / math.sqrt(HEAD_SIZE)


def dot(a, b):
    return lax.dot_general(a, b, (((1,), (0,)), ((), ())), preferred_element_type=F32)


def dot_nt(a, b):
    return lax.dot_general(a, b, (((1,), (1,)), ((), ())), preferred_element_type=F32)


def dot_tn(a, b):
    return lax.dot_general(a, b, (((0,), (0,)), ((), ())), preferred_element_type=F32)


def kernel(
    x_ref, g_ref, wq_ref, kvt_ref, wo_ref, down_ref, qup_in, kvup_in, od_in, up_in, cos_in, sin_in,
    dx_ref, dgrad_ref, small_ref,
    buf, wqa, wqb, wkv, woa, wob, upb, qups, kvur, kvf, qup_ref, kvup_ref, od_ref, up_ref, cos_ref, sin_ref,
    acc_q0, acc_q1, acc_kd, acc_g0, acc_g1, acc_lg,
    sq, sqr, lip, lipr, kvp, kvr, sg, sgr, slg, slgr,
    probs, qs, ks, vs, att, gas, low, lgs, dkacc, dvacc,
    dq0, dq1, kb, lot, lotr, mown, moth, dkvr,
    st, rsr, rown, yst, yrecv, rollst, rollrecv,
    ups, du, r1buf, al, alr, pieces, r2buf, tiles, eb,
    local_sem, w_send, w_recv, ag_send, ag_recv, y_send, y_recv, roll_send, roll_recv,
    m_send, m_recv, rs_send, rs_recv, s_send, s_recv,
):
    s = lax.axis_index("seq")
    h = lax.axis_index("head")
    c = lax.rem(h, 2)
    lane = h // 2
    p = lane // 4
    xi = lax.rem(lane, 4)
    a = lax.rem(xi, 2)
    q = 1 - p
    right = p * 8 + lax.rem(xi + 1, 4) * 2 + c
    left = p * 8 + lax.rem(xi + 3, 4) * 2 + c
    sib = h + 1 - 2 * c
    twin = h + 2 - 4 * a
    twin_sib = twin + 1 - 2 * c
    across = h + 8 - 16 * p
    z = s // 2
    k_lo = lax.rem(s, 2)
    place_in_plane = k_lo * 8 + lane

    def dev(seq, head):
        return (seq, head)

    def lane_of(r, d):
        plane = p if r == 0 else q
        return plane * 4 + lax.rem(xi + d + 4, 4)

    sends = []
    rolled_sends = []

    def remote(src, dst, ssem, rsem, device):
        return pltpu.make_async_remote_copy(
            src_ref=src, dst_ref=dst, send_sem=ssem, recv_sem=rsem,
            device_id=device, device_id_type=MESH,
        )

    def push(*ends):
        copy = remote(*ends)
        copy.start()
        sends.append(copy)

    def arrived(dst, rsem):
        pltpu.make_async_remote_copy(
            src_ref=dst, dst_ref=dst, send_sem=w_send.at[0], recv_sem=rsem,
            device_id=dev(s, sib), device_id_type=MESH,
        ).wait_recv()

    barrier = pltpu.get_barrier_semaphore()
    def plane_peer(d):
        m = lax.rem(place_in_plane + d, 16)
        return m // 8, lax.rem(m, 8)

    def column_peer(d):
        return lax.rem(z + d, 8)

    greeted = [dev(s, sib), dev(s, twin_sib)]
    greeted += [dev(lax.rem(s + 2 * p - 1 + SEQ, SEQ), across)]
    greeted += [dev(lax.rem(s + d, SEQ), h) for d in (1, SEQ - 1)]
    for d in range(1, 16):
        lo, j = plane_peer(d)
        greeted.append(dev(z * 2 + lo, j * 2 + c))
    greeted += [dev(column_peer(d) * 2 + k_lo, h) for d in range(1, 8)]
    for device in greeted:
        pl.semaphore_signal(barrier, inc=1, device_id=device, device_id_type=MESH)

    locals_ = []

    def fetch(src, dst, k):
        copy = pltpu.make_async_copy(src, dst, local_sem.at[k])
        copy.start()
        return copy

    blocks = []
    for t, ref in enumerate((x_ref, g_ref)):
        blocks.append(fetch(ref.at[pl.ds(HALF, HALF)], buf.at[t, lane, 1 - p], t))
    for t, ref in enumerate((x_ref, g_ref)):

        @pl.when(p == 0)
        def _():
            fetch(ref.at[pl.ds(0, HALF)], buf.at[t, lane, 0], 2 + t)

    weights = [
        fetch(wq_ref.at[:, c], wqa, 4),
    ]
    for j in range(LANES):
        cols = pl.ds(pl.multiple_of((2 * j + c) * BLK, BLK), BLK)
        weights.append(fetch(kvt_ref.at[:, :, cols], wkv.at[j, pl.ds(0, 2), c], 5 + j))
    for j in range(LANES):
        cols = pl.ds(pl.multiple_of((2 * j + c) * BLK, BLK), BLK)
        weights.append(fetch(wo_ref.at[:, cols], woa.at[j], 13 + j))

    for acc in (acc_q0, acc_q1, acc_kd, acc_g0, acc_g1, acc_lg):
        acc[...] = jnp.zeros(acc.shape, F32)
    upb[:, 16:, :] = jnp.zeros((LANES, 112, BLK), BF16)
    kvf[...] = jnp.zeros(kvf.shape, BF16)
    qup_ref[...] = jnp.concatenate([qup_in[...], jnp.zeros((120, 256), BF16)], axis=0)
    od_ref[...] = jnp.concatenate([od_in[...], jnp.zeros((120, 256), BF16)], axis=0)
    up_ref[...] = jnp.concatenate([up_in[...], jnp.zeros((8, BLK), BF16)], axis=0)
    upb[lane, 0:16, :] = up_ref[...]
    for i in range(2):
        cos_ref[i] = jnp.concatenate([cos_in[i], cos_in[i]], axis=1)
        sin_ref[i] = jnp.concatenate([-sin_in[i], sin_in[i]], axis=1)
    source = lax.broadcasted_iota(jnp.int32, (64, 256), 0)
    target = lax.broadcasted_iota(jnp.int32, (64, 256), 1)
    goal = source + lax.rem(h, 4) * 32 + jnp.where(source < 32, 0, 96)
    goals = jnp.where(target == goal, 1.0, 0.0).astype(BF16)
    spread = dot(kvup_in[:, 0, :], goals[0:32]) + dot(kvup_in[:, 1, :], goals[32:64])
    column = lax.broadcasted_iota(jnp.int32, (8, 256), 1)
    none = jnp.zeros((8, 256), F32)
    kvup_ref[...] = jnp.concatenate(
        [none, jnp.where(column < 128, spread, 0.0), jnp.where(column < 128, 0.0, spread), none],
        axis=0,
    ).astype(BF16)
    wkv[:, 2:4] = jnp.zeros((LANES, 2, 2, 32, BLK), BF16)
    for j in range(LANES):
        cols = pl.ds(pl.multiple_of((2 * j + c) * BLK, BLK), BLK)
        wkv[j, 2, 0] = jnp.concatenate([down_ref[:, cols], jnp.zeros((8, BLK), BF16)], axis=0)

    pl.semaphore_wait(barrier, len(greeted))

    def send_own(t, slot):
        push(buf.at[t, lane, slot], buf.at[t, lane, slot], ag_send.at[t, 0, slot],
             ag_recv.at[t, 0, slot], dev(s, right))
        push(buf.at[t, lane, slot], buf.at[t, lane, slot], ag_send.at[t, 0, 2 + slot],
             ag_recv.at[t, 0, 2 + slot], dev(s, left))

    beyond = [dev(lax.rem(s + i - q + SEQ, SEQ), across) for i in range(2)]

    def cross(t, b, i, k):
        push(buf.at[t, b, i], buf.at[t, b, 1 - i], ag_send.at[t, 1, k + 1 - i],
             ag_recv.at[t, 1, k + 1 - i], beyond[i])

    def send_roll(t, ref):
        before = lax.rem(s + SEQ - 1, SEQ)

        def copy():
            return remote(ref.at[pl.ds(0, HALF)], buf.at[t, lane, 1], roll_send.at[t],
                          roll_recv.at[t], dev(before, h))

        rolled_sends.append(copy)

        @pl.when(p == 1)
        def _():
            copy().start()

    def send_across(t, ref):
        push(ref.at[pl.ds(0, HALF)], buf.at[t, lane, q], y_send.at[t, 0], y_recv.at[t, q],
             dev(lax.rem(s - q + SEQ, SEQ), across))
        push(ref.at[pl.ds(HALF, HALF)], buf.at[t, lane, p], y_send.at[t, 1], y_recv.at[t, p],
             dev(s, across))

    def own_local(t):
        blocks[t].wait()

        @pl.when(p == 0)
        def _():
            pltpu.make_async_copy(
                (x_ref, g_ref)[t].at[pl.ds(0, HALF)], buf.at[t, lane, 0], local_sem.at[2 + t]
            ).wait()

    def own_rolled(t):
        @pl.when(p == 1)
        def _():
            arrived(buf.at[t, lane, 1], roll_recv.at[t])

    send_roll(0, x_ref)
    own_local(0)
    send_own(0, 0)
    send_across(0, x_ref)
    own_rolled(0)
    send_own(0, 1)
    push(wq_ref.at[:, 1 - c], wqb, w_send.at[0], w_recv.at[0], dev(s, sib))
    for j in range(LANES):
        cols = pl.ds(pl.multiple_of((2 * j + 1 - c) * BLK, BLK), BLK)
        push(kvt_ref.at[:, :, cols], wkv.at[j, pl.ds(0, 2), c], w_send.at[22 + j],
             w_recv.at[22 + j], dev(s, sib))
    for j in range(LANES):
        cols = pl.ds(pl.multiple_of((2 * j + 1 - c) * BLK, BLK), BLK)
        push(wo_ref.at[:, cols], wob.at[j], w_send.at[2 + j], w_recv.at[2 + j], dev(s, sib))
    for d in range(1, LANES):
        push(up_ref, upb.at[lane, pl.ds(0, 16)], w_send.at[10 + d], w_recv.at[10 + d],
             dev(s, lax.rem(lane + d, LANES) * 2 + c))
    push(qup_ref.at[pl.ds(0, 16)], qups, w_send.at[18], w_recv.at[18], dev(s, sib))
    for k, peer in enumerate((sib, twin, twin_sib)):
        push(kvup_ref, kvur.at[k], w_send.at[19 + k], w_recv.at[19 + k], dev(s, peer))

    def multiply(t, b):
        def rows(i, carry):
            block = buf[t, b, i]
            if t == 0:
                acc_q0[i] += dot(block, wqa[b])
                acc_q1[i] += dot(block, wqb[b])
                acc_kd[i] += dot_nt(block, wkv[b].reshape(256, BLK))
            else:
                acc_g0[i] += dot_nt(block, woa[b])
                acc_g1[i] += dot_nt(block, wob[b])
                acc_lg[i] += dot_nt(block, upb[b])
            return carry

        lax.fori_loop(0, 2, rows, 0)

    def multiply_sides(t, r):
        def one(k, carry):
            multiply(t, lane_of(r, 1 + 2 * k))
            return carry

        lax.fori_loop(0, 2, one, 0)

    def forward(t, r):
        from_left, from_right = lane_of(r, -1), lane_of(r, 1)
        arrived(buf.at[t, from_left, 0], ag_recv.at[t, r, 0])
        push(buf.at[t, from_left, 0], buf.at[t, from_left, 0], ag_send.at[t, r, 4],
             ag_recv.at[t, r, 4], dev(s, right))
        arrived(buf.at[t, from_right, 1], ag_recv.at[t, r, 3])
        push(buf.at[t, from_right, 1], buf.at[t, from_right, 1], ag_send.at[t, r, 5],
             ag_recv.at[t, r, 5], dev(s, left))

    def sides_ready(t, r):
        from_left, from_right = lane_of(r, -1), lane_of(r, 1)
        arrived(buf.at[t, from_right, 0], ag_recv.at[t, r, 2])
        if r == 0:
            cross(t, from_right, 0, 2)
        arrived(buf.at[t, from_left, 1], ag_recv.at[t, r, 1])
        if r == 0:
            cross(t, from_left, 1, 0)

    def far_ready(t, r):
        far = lane_of(r, 2)
        arrived(buf.at[t, far, 0], ag_recv.at[t, r, 4])
        arrived(buf.at[t, far, 1], ag_recv.at[t, r, 5])

    def across_ready(t):
        b = lane_of(1, 0)
        for slot, device, k in ((0, left, 2), (1, right, 1)):
            arrived(buf.at[t, b, slot], y_recv.at[t, slot])
            push(buf.at[t, b, slot], buf.at[t, b, slot], ag_send.at[t, 1, k],
                 ag_recv.at[t, 1, k], dev(s, device))

    forward(0, 0)
    sides_ready(0, 0)
    across_ready(0)
    send_roll(1, g_ref)
    send_across(1, g_ref)
    for copy in weights[0:9]:
        copy.wait()
    arrived(wqb, w_recv.at[0])
    for j in range(LANES):
        arrived(wkv.at[j, pl.ds(0, 2), 1 - c], w_recv.at[22 + j])
    multiply(0, lane)
    own_local(1)
    send_own(1, 0)
    forward(0, 1)
    own_rolled(1)
    send_own(1, 1)
    multiply_sides(0, 0)
    multiply(0, lane_of(1, 0))
    far_ready(0, 0)
    multiply(0, lane_of(0, 2))
    sides_ready(0, 1)
    multiply_sides(0, 1)
    far_ready(0, 1)
    multiply(0, lane_of(1, 2))

    sq[...] = acc_q1[...].astype(BF16)
    kvp[...] = acc_kd[:, :, 0:128].astype(BF16)
    lip[...] = acc_kd[:, :, 128:256].astype(BF16)
    push(kvp, kvr.at[1], m_send.at[1], m_recv.at[1], dev(s, twin))
    push(kvp, kvr.at[0], m_send.at[0], m_recv.at[0], dev(s, sib))
    push(lip, lipr, m_send.at[3], m_recv.at[3], dev(s, sib))
    push(sq, sqr, m_send.at[4], m_recv.at[4], dev(s, sib))

    for copy in weights[9:]:
        copy.wait()
    for j in range(LANES):
        arrived(wob.at[j], w_recv.at[2 + j])
    for d in range(1, LANES):
        arrived(upb.at[lax.rem(lane - d + LANES, LANES), pl.ds(0, 16)], w_recv.at[10 + d])
    multiply(1, lane)
    forward(1, 0)
    sides_ready(1, 0)
    across_ready(1)

    for k in range(3):
        arrived(kvur.at[k], w_recv.at[19 + k])
    arrived(qups, w_recv.at[18])
    kvf[0:32, :] = kvup_ref[0:32, :] + kvur[0] + kvur[1] + kvur[2]
    arrived(kvr.at[1], m_recv.at[1])
    push(kvr.at[1], kvr.at[2], m_send.at[2], m_recv.at[2], dev(s, sib))
    arrived(kvr.at[0], m_recv.at[0])
    arrived(kvr.at[2], m_recv.at[2])
    arrived(lipr, m_recv.at[3])
    arrived(sqr, m_recv.at[4])

    def rotate(v, i):
        return v * cos_ref[i] + pltpu.roll(v, 64, 1) * sin_ref[i]

    def unrotate(v, i):
        return v * cos_ref[i] - pltpu.roll(v, 64, 1) * sin_ref[i]

    def project(i, carry):
        low_i = (acc_kd[i, :, 128:256] + lipr[i].astype(F32)).astype(BF16)
        low[i] = low_i
        q_i = (acc_q0[i] + sqr[i].astype(F32) + SCALE * dot(low_i, qup_ref[...])).astype(BF16)
        for hd in range(2):
            cols = slice(hd * 128, hd * 128 + 128)
            qs[hd, i] = rotate(q_i[:, cols].astype(F32), i).astype(BF16)
        own = acc_kd[i, :, 0:128] + kvr[0, i].astype(F32)
        other = kvr[1, i].astype(F32) + kvr[2, i].astype(F32)
        first = jnp.where(a == 0, own, other)
        second = jnp.where(a == 0, other, own)
        rank = SCALE * dot(low_i, kvf[...])
        k_i = jnp.concatenate([first[:, 0:64], second[:, 0:64]], axis=1) + rank[:, 0:128]
        v_i = jnp.concatenate([first[:, 64:128], second[:, 64:128]], axis=1) + rank[:, 128:256]
        start = pl.multiple_of(i * HALF, HALF)
        ks[pl.ds(start, HALF), :] = rotate(k_i.astype(BF16).astype(F32), i).astype(BF16)
        vs[pl.ds(start, HALF), :] = v_i.astype(BF16)
        return carry

    lax.fori_loop(0, 2, project, 0)

    for i in range(2):
        keys = (i + 1) * HALF

        def attend(hd, carry):
            scores = dot_nt(qs[hd, i], ks[0:keys, :]) * INV_ROOT
            row = lax.broadcasted_iota(jnp.int32, scores.shape, 0) + i * HALF
            col = lax.broadcasted_iota(jnp.int32, scores.shape, 1)
            e = jnp.where(col <= row, jnp.exp(scores), 0.0)
            full = e / jnp.sum(e, axis=-1, keepdims=True)
            probs[hd, i, :, 0:keys] = full
            att[hd, i] = dot(full.astype(BF16), vs[0:keys, :]).astype(BF16)
            return carry

        lax.fori_loop(0, 2, attend, 0)
    loti = jnp.concatenate(
        [
            dot_nt(od_ref[0:16, 0:128], att[0, i]) + dot_nt(od_ref[0:16, 128:256], att[1, i])
            for i in range(2)
        ],
        axis=1,
    )
    lot[...] = loti.astype(BF16)
    push(lot, lotr, m_send.at[7], m_recv.at[7], dev(s, sib))

    multiply_sides(1, 0)
    multiply(1, lane_of(1, 0))
    far_ready(1, 0)
    multiply(1, lane_of(0, 2))
    forward(1, 1)
    sides_ready(1, 1)
    multiply_sides(1, 1)
    far_ready(1, 1)
    multiply(1, lane_of(1, 2))
    sg[...] = acc_g1[...].astype(BF16)
    slg[...] = acc_lg[...].astype(BF16)
    push(slg, slgr, m_send.at[5], m_recv.at[5], dev(s, sib))
    push(sg, sgr, m_send.at[6], m_recv.at[6], dev(s, sib))

    arrived(slgr, m_recv.at[5])
    arrived(sgr, m_recv.at[6])

    def cotangent(i, carry):
        lg = (acc_lg[i] + slgr[i].astype(F32)).astype(BF16)
        lgs[i] = lg
        ga = (acc_g0[i] + sgr[i].astype(F32) + SCALE * dot(lg, od_ref[...])).astype(BF16)
        gas[0, i] = ga[:, 0:128]
        gas[1, i] = ga[:, 128:256]
        return carry

    lax.fori_loop(0, 2, cotangent, 0)
    dkacc[...] = jnp.zeros(dkacc.shape, F32)
    dvacc[...] = jnp.zeros(dvacc.shape, F32)

    def split_columns(kind, halves):
        for message, side in ((mown, a), (moth, 1 - a)):
            low_side = jnp.concatenate([half[:, 0:64] for half in halves], axis=1)
            high_side = jnp.concatenate([half[:, 64:128] for half in halves], axis=1)
            message[kind] = jnp.where(side == 0, low_side, high_side).astype(BF16)
        push(moth.at[kind], dkvr.at[1, kind], m_send.at[9 + 3 * kind], m_recv.at[9 + 3 * kind],
             dev(s, twin))
        push(mown.at[kind], dkvr.at[0, kind], m_send.at[11 + 3 * kind],
             m_recv.at[11 + 3 * kind], dev(s, sib))

    def pass_on(kind):
        arrived(dkvr.at[1, kind], m_recv.at[9 + 3 * kind])
        push(dkvr.at[1, kind], dkvr.at[2, kind], m_send.at[10 + 3 * kind],
             m_recv.at[10 + 3 * kind], dev(s, sib))

    for i in range(2):
        keys = (i + 1) * HALF
        for hd in range(2):
            dvacc[0:keys, :] += dot_tn(probs[hd, i, :, 0:keys].astype(BF16), gas[hd, i])
    split_columns(1, [dvacc[0:HALF, :], dvacc[HALF:ROWS, :]])
    for i in range(2):
        keys = (i + 1) * HALF
        for hd in range(2):
            full = probs[hd, i, :, 0:keys]
            grad = dot_nt(gas[hd, i], vs[0:keys, :])
            delta = jnp.sum(full * grad, axis=-1, keepdims=True)
            ds = (full * (grad - delta)).astype(BF16)
            dq = INV_ROOT * dot(ds, ks[0:keys, :])
            dq0[i, :, hd * 128 : hd * 128 + 128] = unrotate(dq, i).astype(BF16)
            dkacc[0:keys, :] += dot_tn(ds, qs[hd, i])
    push(dq0, dq1, m_send.at[8], m_recv.at[8], dev(s, sib))
    split_columns(
        0,
        [unrotate(INV_ROOT * dkacc[i * HALF : i * HALF + HALF, :], i) for i in range(2)],
    )
    pass_on(1)

    arrived(lotr, m_recv.at[7])
    low_out = (SCALE * (loti + lotr[...].astype(F32))).astype(BF16)

    def out_up(j, carry):
        total = jnp.zeros((16, BLK), F32)
        for i in range(2):
            total += dot(low_out[:, i * HALF : i * HALF + HALF], buf[1, j, i])
        ups[j] = total[0:8]
        return carry

    lax.fori_loop(0, LANES, out_up, 0)

    kv_rows = kvf[0:32, :].astype(F32)
    kv_low = jnp.concatenate([kv_rows[:, 0:64], kv_rows[:, 128:192]], axis=1)
    kv_high = jnp.concatenate([kv_rows[:, 64:128], kv_rows[:, 192:256]], axis=1)
    kv_chip = jnp.where(a == 0, kv_low, kv_high).astype(BF16)
    kv_chip = jnp.concatenate([kv_chip, jnp.zeros((96, 128), BF16)], axis=0)
    sib_up = jnp.concatenate([qups[...], jnp.zeros((112, 256), BF16)], axis=0)

    pass_on(0)
    arrived(dq1, m_recv.at[8])
    for kind in (1, 0):
        arrived(dkvr.at[2, kind], m_recv.at[10 + 3 * kind])
        arrived(dkvr.at[0, kind], m_recv.at[11 + 3 * kind])
    back_t = []
    for i in range(2):
        cols = slice(i * 64, i * 64 + 64)
        total = jnp.concatenate(
            [
                mown[kind].astype(F32)[:, cols] + dkvr[0, kind].astype(F32)[:, cols]
                + dkvr[1, kind].astype(F32)[:, cols] + dkvr[2, kind].astype(F32)[:, cols]
                for kind in range(2)
            ],
            axis=1,
        ).astype(BF16)
        back = SCALE * (
            dot_nt(dq0[i], qup_ref[...]) + dot_nt(dq1[i], sib_up) + dot_nt(total, kv_chip)
        )
        kb[i, :, 0:128] = total
        kb[i, :, 128:256] = back.astype(BF16)
        back_t.append(back.T[0:32, :])

    def dx_block(b, i):
        return dot_nt(dq0[i], wqa[b]) + dot_nt(dq1[i], wqb[b]) + dot(kb[i], wkv[b].reshape(256, BLK))

    def far_block(r):
        def one(i, carry):
            st[r, 0, i] = dx_block(lane_of(r, 2), i).astype(BF16)
            return carry

        lax.fori_loop(0, 2, one, 0)
        push(st.at[r, 0, 0], rsr.at[r, 0], rs_send.at[r, 0], rs_recv.at[r, 0], dev(s, right))
        push(st.at[r, 0, 1], rsr.at[r, 1], rs_send.at[r, 1], rs_recv.at[r, 1], dev(s, left))

    def side_cross(d, i, extra):
        k = 1 if d == 1 else 2
        total = dx_block(lane_of(1, d), i)
        arrived(rsr.at[1, extra], rs_recv.at[1, extra])
        total += rsr[1, extra].astype(F32)
        st[1, k, i] = total.astype(BF16)
        slot = 2 * k + 1 - i
        push(st.at[1, k, i], rsr.at[1, slot], rs_send.at[1, slot], rs_recv.at[1, slot], beyond[i])

    def side_next(d, i, slot):
        k = 1 if d == 1 else 2
        st[1, k, i] = dx_block(lane_of(1, d), i).astype(BF16)
        push(st.at[1, k, i], rsr.at[1, slot], rs_send.at[1, slot], rs_recv.at[1, slot],
             dev(s, right if d == 1 else left))

    def side_home(d, i, extra):
        k = 1 if d == 1 else 2
        slot = 2 * k + i
        total = dx_block(lane_of(0, d), i)
        if extra is not None:
            arrived(rsr.at[0, extra], rs_recv.at[0, extra])
            total += rsr[0, extra].astype(F32)
        else:
            arrived(rsr.at[1, slot], rs_recv.at[1, slot])
            total += rsr[1, slot].astype(F32)
        st[0, k, i] = total.astype(BF16)
        push(st.at[0, k, i], rsr.at[0, slot], rs_send.at[0, slot], rs_recv.at[0, slot],
             dev(s, right if d == 1 else left))

    far_block(1)

    back_full = jnp.concatenate(back_t, axis=1).astype(BF16)

    def adapters(j, carry):
        total = jnp.zeros((32, BLK), F32)
        for i in range(2):
            total += dot(back_full[:, i * HALF : i * HALF + HALF], buf[0, j, i])
        du[j, 0] = total[0:16].astype(BF16)
        du[j, 1] = jnp.concatenate([total[16:24], ups[j]], axis=0).astype(BF16)
        return carry

    lax.fori_loop(0, LANES, adapters, 0)
    for d in range(1, 16):
        lo, j = plane_peer(d)
        push(du.at[j, lo], r1buf.at[d - 1], s_send.at[0, d], s_recv.at[0, d],
             dev(z * 2 + lo, j * 2 + c))

    low_t = jnp.concatenate([low[i].astype(F32).T[0:32] for i in range(2)], axis=1).astype(BF16)
    lg_t = jnp.concatenate([lgs[i].astype(F32).T[0:16] for i in range(2)], axis=1).astype(BF16)
    query_up = jnp.zeros((32, 256), F32)
    kv_up = jnp.zeros((32, 128), F32)
    out_down = jnp.zeros((16, 256), F32)
    for i in range(2):
        cols = slice(i * HALF, i * HALF + HALF)
        query_up += dot(low_t[:, cols], dq0[i])
        kv_up += dot(low_t[:, cols], kb[i, :, 0:128])
        out_down += jnp.concatenate(
            [dot(lg_t[:, cols], att[0, i]), dot(lg_t[:, cols], att[1, i])], axis=1
        )
    lane_col = lax.broadcasted_iota(jnp.int32, (8, 128), 1)
    kv_grad = SCALE * jnp.where(lane_col < 64, kv_up[8:16], kv_up[16:24])
    alone = jnp.concatenate(
        [
            jnp.concatenate([SCALE * query_up[0:8], SCALE * out_down[0:8]], axis=1),
            jnp.concatenate([kv_grad, jnp.zeros((8, 384), F32)], axis=1),
        ],
        axis=0,
    ).astype(BF16)
    al[0] = alone[:, 0:256]
    al[1] = alone[:, 256:512]
    push(al.at[1 - k_lo], alr, s_send.at[4, 1], s_recv.at[4, 1], dev(z * 2 + 1 - k_lo, h))
    side_next(1, 1, 2)
    side_next(-1, 0, 5)
    far_block(0)
    side_cross(1, 0, 0)
    side_cross(-1, 1, 1)

    shared = du[lane, k_lo].astype(F32)
    for d in range(1, 16):
        arrived(r1buf.at[d - 1], s_recv.at[0, d])
        shared += r1buf[d - 1].astype(F32)
    arrived(alr, s_recv.at[4, 1])
    single = al[k_lo].astype(F32) + alr[...].astype(F32)
    for k in range(8):
        r, g = k // 4, k % 4
        pieces[k, 0] = shared[8 * r : 8 * r + 8, g * 128 : g * 128 + 128]
        r, g = k // 2, k % 2
        if k < 4:
            pieces[k, 1] = single[8 * r : 8 * r + 8, g * 128 : g * 128 + 128]
        else:
            pieces[k, 1] = jnp.zeros((8, 128), F32)
    for d in range(1, 8):
        owner = column_peer(d)
        push(pieces.at[owner], r2buf.at[d - 1], s_send.at[1, d], s_recv.at[1, d],
             dev(owner * 2 + k_lo, h))
    mine = pieces[z]
    for d in range(1, 8):
        arrived(r2buf.at[d - 1], s_recv.at[1, d])
        mine += r2buf[d - 1]
    tiles[place_in_plane] = mine[0]
    for d in range(1, 16):
        lo, j = plane_peer(d)
        push(tiles.at[place_in_plane], tiles.at[place_in_plane], s_send.at[2, d],
             s_recv.at[2, d], dev(z * 2 + lo, j * 2 + c))
    tiles[16 + k_lo] = mine[1]
    push(tiles.at[16 + k_lo], tiles.at[16 + k_lo], s_send.at[4, 2], s_recv.at[4, 2],
         dev(z * 2 + 1 - k_lo, h))

    for i, slot in ((0, 5), (1, 2)):
        total = dx_block(lane_of(1, 0), i)
        arrived(rsr.at[1, slot], rs_recv.at[1, slot])
        yst[i] = (total + rsr[1, slot].astype(F32)).astype(BF16)
        push(yst.at[i], yrecv.at[1 - i], y_send.at[2, i], y_recv.at[2, 1 - i], beyond[i])
    side_home(-1, 1, 1)
    side_home(1, 1, None)
    for d in range(1, 16):
        m = lax.rem(place_in_plane - d + 16, 16)
        arrived(tiles.at[m], s_recv.at[2, d])
    arrived(tiles.at[17 - k_lo], s_recv.at[4, 2])
    for k in range(9):
        eb[c, z, k] = jnp.concatenate([tiles[2 * k], tiles[2 * k + 1]], axis=0).astype(BF16)
    for d in range(1, 8):
        push(eb.at[c, z], eb.at[c, z], s_send.at[3, d], s_recv.at[3, d],
             dev(column_peer(d) * 2 + k_lo, h))
    side_home(1, 0, 0)
    side_home(-1, 0, None)
    after = lax.rem(s + 1, SEQ)

    def send_back():
        return remote(rollst, rollrecv, roll_send.at[2], roll_recv.at[2], dev(after, h))

    rolled_sends.append(send_back)
    for i in (1, 0):
        total = dx_block(lane, i)
        for k in (2, 4):
            arrived(rsr.at[0, k + i], rs_recv.at[0, k + i])
            total += rsr[0, k + i].astype(F32)
        arrived(yrecv.at[i], y_recv.at[2, i])
        rown[i] = total + yrecv[i].astype(F32)
        if i == 1:

            @pl.when(p == 1)
            def _():
                rollst[...] = rown[1].astype(BF16)
                send_back().start()

    for d in range(1, 8):
        arrived(eb.at[c, lax.rem(z - d + 8, 8)], s_recv.at[3, d])
    push(eb.at[c], eb.at[c], s_send.at[4, 0], s_recv.at[4, 0], dev(s, sib))
    for g in range(4):
        cols = slice(g * 128, g * 128 + 128)
        pair = eb[c, 4 + g, 4 + lane // 2].astype(F32)
        small_ref[0:8, cols] = jnp.where(lax.rem(lane, 2) == 0, pair[0:8], pair[8:16])
    for g in range(2):
        pair = eb[c, g, 8].astype(F32)
        small_ref[8:16, g * 128 : g * 128 + 128] = pair[0:8]
        small_ref[8:16, 256 + g * 128 : 384 + g * 128] = pair[8:16]
    kv_out = eb[c, 2, 8].astype(F32)[0:8]
    small_ref[16:24, :] = jnp.zeros((8, BLK), F32)
    small_ref[16:24, 0:64] = jnp.concatenate(
        [
            jnp.where(c == 0, kv_out[:, 0:32], kv_out[:, 32:64]),
            jnp.where(c == 0, kv_out[:, 64:96], kv_out[:, 96:128]),
        ],
        axis=1,
    )

    @pl.when(p == 0)
    def _():
        for i in range(2):
            dx_ref[i * HALF : i * HALF + HALF, :] = rown[i].astype(BF16)

    @pl.when(p == 1)
    def _():
        dx_ref[HALF:ROWS, :] = rown[0].astype(BF16)
        arrived(rollrecv, roll_recv.at[2])
        dx_ref[0:HALF, :] = rollrecv[...]

    arrived(eb.at[1 - c], s_recv.at[4, 0])

    def place(j, carry):
        for core in range(2):
            for g in range(4):
                cols = pl.ds(pl.multiple_of((2 * j + core) * BLK + g * 128, 128), 128)
                for r in range(3):
                    pair = eb[core, r % 2 * 4 + g, r // 2 * 4 + j // 2].astype(F32)
                    dgrad_ref[8 * r : 8 * r + 8, cols] = jnp.where(
                        lax.rem(j, 2) == 0, pair[0:8], pair[8:16]
                    )
        return carry

    lax.fori_loop(0, LANES, place, 0)

    for copy in sends:
        copy.wait_send()

    @pl.when(p == 1)
    def _():
        for copy in rolled_sends:
            copy().wait_send()


def finish(dx_ref, dgrad_ref, small_ref, out_dx, out_down, out_qg, out_kvg, out_odg, out_oug):
    out_dx[...] = dx_ref[...]
    for r in range(3):
        out_down[r] = dgrad_ref[r * RANK : (r + 1) * RANK, :]
    out_qg[...] = small_ref[8:16, 0:256]
    out_odg[...] = small_ref[8:16, 256:512]
    out_oug[...] = small_ref[0:8, :]
    out_kvg[:, 0, :] = small_ref[16:24, 0:32]
    out_kvg[:, 1, :] = small_ref[16:24, 32:64]


def body(normed, output_gradient, query_weight, key_value_weight, output_weight,
         adapter_down, query_up, key_value_up, output_down, output_up):
    h = lax.axis_index("head")
    s = lax.axis_index("seq")
    c = lax.rem(h, 2)
    p = h // 8
    width = adapter_down.shape[2]

    positions = lax.rem(
        s * ROWS + jnp.arange(ROWS, dtype=jnp.int32) + p * HALF, TOKENS
    ).astype(F32)
    half_dim = HEAD_SIZE // 2
    frequency = ROPE_BASE ** (-jnp.arange(half_dim, dtype=F32) * 2.0 / HEAD_SIZE)
    angles = positions[:, None] * frequency[None, :]
    cos, sin = jnp.cos(angles), jnp.sin(angles)
    cos = cos.reshape(2, HALF, half_dim)
    sin = sin.reshape(2, HALF, half_dim)

    kvt = key_value_weight.transpose(1, 2, 0)
    wq = query_weight.reshape(LANES, 2, BLK, 256)

    vm = lambda *shape: pltpu.VMEM(shape, BF16)
    vf = lambda *shape: pltpu.VMEM(shape, F32)
    dma = lambda *shape: pltpu.SemaphoreType.DMA(shape)
    out_shape = [
        jax.ShapeDtypeStruct((ROWS, BLK), BF16),
        jax.ShapeDtypeStruct((3 * RANK, width), F32),
        jax.ShapeDtypeStruct((3 * RANK, BLK), F32),
    ]
    hbm = pl.BlockSpec(memory_space=pl.ANY)
    vmem = pl.BlockSpec(memory_space=pltpu.VMEM)
    scratch = [
        vm(2, LANES, 2, HALF, BLK), vm(LANES, BLK, 256), vm(LANES, BLK, 256),
        vm(LANES, 4, 2, 32, BLK), vm(LANES, 256, BLK), vm(LANES, 256, BLK),
        vm(LANES, 128, BLK), vm(16, 256), vm(3, 32, 256), vm(128, 256),
        vm(128, 256), vm(32, 256), vm(128, 256), vm(16, BLK), vf(2, HALF, HEAD_SIZE),
        vf(2, HALF, HEAD_SIZE),
        vf(2, HALF, 256), vf(2, HALF, 256), vf(2, HALF, 256), vf(2, HALF, 256),
        vf(2, HALF, 256), vf(2, HALF, 128),
        vm(2, HALF, 256), vm(2, HALF, 256), vm(2, HALF, 128), vm(2, HALF, 128),
        vm(2, HALF, 128), vm(3, 2, HALF, 128), vm(2, HALF, 256), vm(2, HALF, 256),
        vm(2, HALF, 128), vm(2, HALF, 128),
        vf(2, 2, HALF, ROWS), vm(2, 2, HALF, 128), vm(ROWS, 128), vm(ROWS, 128),
        vm(2, 2, HALF, 128), vm(2, 2, HALF, 128), vm(2, HALF, 128), vm(2, HALF, 128),
        vf(ROWS, 128), vf(ROWS, 128),
        vm(2, HALF, 256), vm(2, HALF, 256), vm(2, HALF, 256), vm(16, ROWS), vm(16, ROWS),
        vm(2, HALF, 128), vm(2, HALF, 128), vm(3, 2, HALF, 128),
        vm(2, 3, 2, HALF, BLK), vm(2, 6, HALF, BLK), vf(2, HALF, BLK), vm(2, HALF, BLK),
        vm(2, HALF, BLK), vm(HALF, BLK), vm(HALF, BLK),
        vf(LANES, 8, BLK), vm(LANES, 2, 16, BLK), vm(15, 16, BLK), vm(2, 16, 256), vm(16, 256), vf(8, 2, 8, 128),
        vf(7, 2, 8, 128), vf(18, 8, 128), vm(2, 8, 9, 16, 128),
        dma(21), dma(30), dma(30), dma(2, 2, 6), dma(2, 2, 6), dma(3, 2), dma(3, 2),
        dma(3), dma(3), dma(15), dma(15), dma(2, 6), dma(2, 6), dma(5, 16), dma(5, 16),
    ]
    dx, dgrad, small = pl.pallas_call(
        kernel,
        out_shape=out_shape,
        in_specs=[hbm] * 5 + [vmem] * 7,
        out_specs=[vmem] * 3,
        scratch_shapes=scratch,
        compiler_params=pltpu.CompilerParams(
            collective_id=0, has_side_effects=True, vmem_limit_bytes=56 * 1024 * 1024
        ),
        cost_estimate=pl.CostEstimate(
            flops=9_000_000_000, bytes_accessed=20_000_000, transcendentals=400_000
        ),
    )(
        normed, output_gradient, wq, kvt, output_weight, adapter_down.reshape(3 * RANK, width),
        query_up, key_value_up, output_down, output_up, cos, sin,
    )
    return tuple(
        pl.pallas_call(
            finish,
            out_shape=[
                jax.ShapeDtypeStruct((ROWS, BLK), BF16),
                jax.ShapeDtypeStruct((3, RANK, width), F32),
                jax.ShapeDtypeStruct((RANK, 256), F32),
                jax.ShapeDtypeStruct((RANK, 2, 32), F32),
                jax.ShapeDtypeStruct((RANK, 256), F32),
                jax.ShapeDtypeStruct((RANK, BLK), F32),
            ],
            in_specs=[vmem] * 3,
            out_specs=[vmem] * 6,
        )(dx, dgrad, small)
    )


def solution(mesh):
    return jax.shard_map(
        body,
        mesh=mesh,
        in_specs=(
            P("seq", "head"), P("seq", "head"), P(None, "head"), P(None, None, "head"),
            P("head", None), P(), P(None, "head"), P(None, None, "head"),
            P(None, "head"), P(None, "head"),
        ),
        out_specs=(
            P("seq", "head"), P(), P(None, "head"), P(None, None, "head"),
            P(None, "head"), P(None, "head"),
        ),
        check_vma=False,
    )
```

```python
import math

import jax
import jax.numpy as jnp
from jax import lax
from jax.experimental import pallas as pl
from jax.experimental.pallas import tpu as pltpu
from jax.sharding import PartitionSpec as P

MESH = pl.DeviceIdType.MESH
F32 = jnp.float32
BF16 = jnp.bfloat16

HEAD_SIZE = 128
RANK = 8
SCALE = 2.0
ROPE_BASE = 10000.0
ROWS = 512
HALF = 256
BLK = 512
SEQ = 16
LANES = 8
TOKENS = 8192
INV_ROOT = 1.0 / math.sqrt(HEAD_SIZE)


def dot(a, b):
    return lax.dot_general(a, b, (((1,), (0,)), ((), ())), preferred_element_type=F32)


def dot_nt(a, b):
    return lax.dot_general(a, b, (((1,), (1,)), ((), ())), preferred_element_type=F32)


def dot_tn(a, b):
    return lax.dot_general(a, b, (((0,), (0,)), ((), ())), preferred_element_type=F32)


def kernel(
    x_ref, g_ref, wq_ref, kvt_ref, wo_ref, down_ref, qup_in, kvup_in, od_in, up_in, cos_in, sin_in,
    dx_ref, dgrad_ref, small_ref,
    buf, wqa, wqb, wkv, woa, wob, upb, qups, kvur, kvf, qup_ref, kvup_ref, od_ref, up_ref, cos_ref, sin_ref,
    acc_q0, acc_q1, acc_kd, acc_g0, acc_g1, acc_lg,
    sq, sqr, lip, lipr, kvp, kvr, sg, sgr, slg, slgr,
    probs, qs, ks, vs, att, gas, low, lgs, dkacc, dvacc,
    dq0, dq1, kb, lot, lotr, mown, moth, dkvr,
    st, rsr, rown, yst, yrecv, rollst, rollrecv,
    ups, du, r1buf, al, alr, pieces, r2buf, tiles, eb,
    local_sem, w_send, w_recv, ag_send, ag_recv, y_send, y_recv, roll_send, roll_recv,
    m_send, m_recv, rs_send, rs_recv, s_send, s_recv,
):
    s = lax.axis_index("seq")
    h = lax.axis_index("head")
    c = lax.rem(h, 2)
    lane = h // 2
    p = lane // 4
    xi = lax.rem(lane, 4)
    a = lax.rem(xi, 2)
    q = 1 - p
    right = p * 8 + lax.rem(xi + 1, 4) * 2 + c
    left = p * 8 + lax.rem(xi + 3, 4) * 2 + c
    sib = h + 1 - 2 * c
    twin = h + 2 - 4 * a
    twin_sib = twin + 1 - 2 * c
    across = h + 8 - 16 * p
    z = s // 2
    k_lo = lax.rem(s, 2)
    place_in_plane = k_lo * 8 + lane

    def dev(seq, head):
        return (seq, head)

    def lane_of(r, d):
        plane = p if r == 0 else q
        return plane * 4 + lax.rem(xi + d + 4, 4)

    sends = []
    rolled_sends = []

    def remote(src, dst, ssem, rsem, device):
        return pltpu.make_async_remote_copy(
            src_ref=src, dst_ref=dst, send_sem=ssem, recv_sem=rsem,
            device_id=device, device_id_type=MESH,
        )

    def push(*ends):
        copy = remote(*ends)
        copy.start()
        sends.append(copy)

    def arrived(dst, rsem):
        pltpu.make_async_remote_copy(
            src_ref=dst, dst_ref=dst, send_sem=w_send.at[0], recv_sem=rsem,
            device_id=dev(s, sib), device_id_type=MESH,
        ).wait_recv()

    barrier = pltpu.get_barrier_semaphore()
    def plane_peer(d):
        m = lax.rem(place_in_plane + d, 16)
        return m // 8, lax.rem(m, 8)

    def column_peer(d):
        return lax.rem(z + d, 8)

    greeted = [dev(s, sib), dev(s, twin_sib)]
    greeted += [dev(lax.rem(s + 2 * p - 1 + SEQ, SEQ), across)]
    greeted += [dev(lax.rem(s + d, SEQ), h) for d in (1, SEQ - 1)]
    for d in range(1, 16):
        lo, j = plane_peer(d)
        greeted.append(dev(z * 2 + lo, j * 2 + c))
    greeted += [dev(column_peer(d) * 2 + k_lo, h) for d in range(1, 8)]
    for device in greeted:
        pl.semaphore_signal(barrier, inc=1, device_id=device, device_id_type=MESH)

    locals_ = []

    def fetch(src, dst, k):
        copy = pltpu.make_async_copy(src, dst, local_sem.at[k])
        copy.start()
        return copy

    blocks = []
    for t, ref in enumerate((x_ref, g_ref)):
        blocks.append(fetch(ref.at[pl.ds(HALF, HALF)], buf.at[t, lane, 1 - p], t))
    for t, ref in enumerate((x_ref, g_ref)):

        @pl.when(p == 0)
        def _():
            fetch(ref.at[pl.ds(0, HALF)], buf.at[t, lane, 0], 2 + t)

    weights = [
        fetch(wq_ref.at[:, c], wqa, 4),
    ]
    for j in range(LANES):
        cols = pl.ds(pl.multiple_of((2 * j + c) * BLK, BLK), BLK)
        weights.append(fetch(kvt_ref.at[:, :, cols], wkv.at[j, pl.ds(0, 2), c], 5 + j))
    for j in range(LANES):
        cols = pl.ds(pl.multiple_of((2 * j + c) * BLK, BLK), BLK)
        weights.append(fetch(wo_ref.at[:, cols], woa.at[j], 13 + j))

    for acc in (acc_q0, acc_q1, acc_kd, acc_g0, acc_g1, acc_lg):
        acc[...] = jnp.zeros(acc.shape, F32)
    upb[:, 16:, :] = jnp.zeros((LANES, 112, BLK), BF16)
    kvf[...] = jnp.zeros(kvf.shape, BF16)
    qup_ref[...] = jnp.concatenate([qup_in[...], jnp.zeros((120, 256), BF16)], axis=0)
    od_ref[...] = jnp.concatenate([od_in[...], jnp.zeros((120, 256), BF16)], axis=0)
    up_ref[...] = jnp.concatenate([up_in[...], jnp.zeros((8, BLK), BF16)], axis=0)
    upb[lane, 0:16, :] = up_ref[...]
    for i in range(2):
        cos_ref[i] = jnp.concatenate([cos_in[i], cos_in[i]], axis=1)
        sin_ref[i] = jnp.concatenate([-sin_in[i], sin_in[i]], axis=1)
    source = lax.broadcasted_iota(jnp.int32, (64, 256), 0)
    target = lax.broadcasted_iota(jnp.int32, (64, 256), 1)
    goal = source + lax.rem(h, 4) * 32 + jnp.where(source < 32, 0, 96)
    goals = jnp.where(target == goal, 1.0, 0.0).astype(BF16)
    spread = dot(kvup_in[:, 0, :], goals[0:32]) + dot(kvup_in[:, 1, :], goals[32:64])
    column = lax.broadcasted_iota(jnp.int32, (8, 256), 1)
    none = jnp.zeros((8, 256), F32)
    kvup_ref[...] = jnp.concatenate(
        [none, jnp.where(column < 128, spread, 0.0), jnp.where(column < 128, 0.0, spread), none],
        axis=0,
    ).astype(BF16)
    wkv[:, 2:4] = jnp.zeros((LANES, 2, 2, 32, BLK), BF16)
    for j in range(LANES):
        cols = pl.ds(pl.multiple_of((2 * j + c) * BLK, BLK), BLK)
        wkv[j, 2, 0] = jnp.concatenate([down_ref[:, cols], jnp.zeros((8, BLK), BF16)], axis=0)

    pl.semaphore_wait(barrier, len(greeted))

    def send_own(t, slot):
        push(buf.at[t, lane, slot], buf.at[t, lane, slot], ag_send.at[t, 0, slot],
             ag_recv.at[t, 0, slot], dev(s, right))
        push(buf.at[t, lane, slot], buf.at[t, lane, slot], ag_send.at[t, 0, 2 + slot],
             ag_recv.at[t, 0, 2 + slot], dev(s, left))

    beyond = [dev(lax.rem(s + i - q + SEQ, SEQ), across) for i in range(2)]

    def cross(t, b, i, k):
        push(buf.at[t, b, i], buf.at[t, b, 1 - i], ag_send.at[t, 1, k + 1 - i],
             ag_recv.at[t, 1, k + 1 - i], beyond[i])

    def send_roll(t, ref):
        before = lax.rem(s + SEQ - 1, SEQ)

        def copy():
            return remote(ref.at[pl.ds(0, HALF)], buf.at[t, lane, 1], roll_send.at[t],
                          roll_recv.at[t], dev(before, h))

        rolled_sends.append(copy)

        @pl.when(p == 1)
        def _():
            copy().start()

    def send_across(t, ref):
        push(ref.at[pl.ds(0, HALF)], buf.at[t, lane, q], y_send.at[t, 0], y_recv.at[t, q],
             dev(lax.rem(s - q + SEQ, SEQ), across))
        push(ref.at[pl.ds(HALF, HALF)], buf.at[t, lane, p], y_send.at[t, 1], y_recv.at[t, p],
             dev(s, across))

    def own_local(t):
        blocks[t].wait()

        @pl.when(p == 0)
        def _():
            pltpu.make_async_copy(
                (x_ref, g_ref)[t].at[pl.ds(0, HALF)], buf.at[t, lane, 0], local_sem.at[2 + t]
            ).wait()

    def own_rolled(t):
        @pl.when(p == 1)
        def _():
            arrived(buf.at[t, lane, 1], roll_recv.at[t])

    send_roll(0, x_ref)
    own_local(0)
    send_own(0, 0)
    send_across(0, x_ref)
    own_rolled(0)
    send_own(0, 1)
    push(wq_ref.at[:, 1 - c], wqb, w_send.at[0], w_recv.at[0], dev(s, sib))
    for j in range(LANES):
        cols = pl.ds(pl.multiple_of((2 * j + 1 - c) * BLK, BLK), BLK)
        push(kvt_ref.at[:, :, cols], wkv.at[j, pl.ds(0, 2), c], w_send.at[22 + j],
             w_recv.at[22 + j], dev(s, sib))
    for j in range(LANES):
        cols = pl.ds(pl.multiple_of((2 * j + 1 - c) * BLK, BLK), BLK)
        push(wo_ref.at[:, cols], wob.at[j], w_send.at[2 + j], w_recv.at[2 + j], dev(s, sib))
    for d in range(1, LANES):
        push(up_ref, upb.at[lane, pl.ds(0, 16)], w_send.at[10 + d], w_recv.at[10 + d],
             dev(s, lax.rem(lane + d, LANES) * 2 + c))
    push(qup_ref.at[pl.ds(0, 16)], qups, w_send.at[18], w_recv.at[18], dev(s, sib))
    for k, peer in enumerate((sib, twin, twin_sib)):
        push(kvup_ref, kvur.at[k], w_send.at[19 + k], w_recv.at[19 + k], dev(s, peer))

    def multiply(t, b):
        def rows(i, carry):
            block = buf[t, b, i]
            if t == 0:
                acc_q0[i] += dot(block, wqa[b])
                acc_q1[i] += dot(block, wqb[b])
                acc_kd[i] += dot_nt(block, wkv[b].reshape(256, BLK))
            else:
                acc_g0[i] += dot_nt(block, woa[b])
                acc_g1[i] += dot_nt(block, wob[b])
                acc_lg[i] += dot_nt(block, upb[b])
            return carry

        lax.fori_loop(0, 2, rows, 0)

    def multiply_sides(t, r):
        def one(k, carry):
            multiply(t, lane_of(r, 1 + 2 * k))
            return carry

        lax.fori_loop(0, 2, one, 0)

    def forward(t, r):
        from_left, from_right = lane_of(r, -1), lane_of(r, 1)
        arrived(buf.at[t, from_left, 0], ag_recv.at[t, r, 0])
        push(buf.at[t, from_left, 0], buf.at[t, from_left, 0], ag_send.at[t, r, 4],
             ag_recv.at[t, r, 4], dev(s, right))
        arrived(buf.at[t, from_right, 1], ag_recv.at[t, r, 3])
        push(buf.at[t, from_right, 1], buf.at[t, from_right, 1], ag_send.at[t, r, 5],
             ag_recv.at[t, r, 5], dev(s, left))

    def sides_ready(t, r):
        from_left, from_right = lane_of(r, -1), lane_of(r, 1)
        arrived(buf.at[t, from_right, 0], ag_recv.at[t, r, 2])
        if r == 0:
            cross(t, from_right, 0, 2)
        arrived(buf.at[t, from_left, 1], ag_recv.at[t, r, 1])
        if r == 0:
            cross(t, from_left, 1, 0)

    def far_ready(t, r):
        far = lane_of(r, 2)
        arrived(buf.at[t, far, 0], ag_recv.at[t, r, 4])
        arrived(buf.at[t, far, 1], ag_recv.at[t, r, 5])

    def across_ready(t):
        b = lane_of(1, 0)
        for slot, device, k in ((0, left, 2), (1, right, 1)):
            arrived(buf.at[t, b, slot], y_recv.at[t, slot])
            push(buf.at[t, b, slot], buf.at[t, b, slot], ag_send.at[t, 1, k],
                 ag_recv.at[t, 1, k], dev(s, device))

    forward(0, 0)
    sides_ready(0, 0)
    across_ready(0)
    send_roll(1, g_ref)
    send_across(1, g_ref)
    for copy in weights[0:9]:
        copy.wait()
    arrived(wqb, w_recv.at[0])
    for j in range(LANES):
        arrived(wkv.at[j, pl.ds(0, 2), 1 - c], w_recv.at[22 + j])
    multiply(0, lane)
    own_local(1)
    send_own(1, 0)
    forward(0, 1)
    own_rolled(1)
    send_own(1, 1)
    multiply_sides(0, 0)
    multiply(0, lane_of(1, 0))
    far_ready(0, 0)
    multiply(0, lane_of(0, 2))
    sides_ready(0, 1)
    multiply_sides(0, 1)
    far_ready(0, 1)
    multiply(0, lane_of(1, 2))

    sq[...] = acc_q1[...].astype(BF16)
    kvp[...] = acc_kd[:, :, 0:128].astype(BF16)
    lip[...] = acc_kd[:, :, 128:256].astype(BF16)
    push(kvp, kvr.at[1], m_send.at[1], m_recv.at[1], dev(s, twin))
    push(kvp, kvr.at[0], m_send.at[0], m_recv.at[0], dev(s, sib))
    push(lip, lipr, m_send.at[3], m_recv.at[3], dev(s, sib))
    push(sq, sqr, m_send.at[4], m_recv.at[4], dev(s, sib))

    for copy in weights[9:]:
        copy.wait()
    for j in range(LANES):
        arrived(wob.at[j], w_recv.at[2 + j])
    for d in range(1, LANES):
        arrived(upb.at[lax.rem(lane - d + LANES, LANES), pl.ds(0, 16)], w_recv.at[10 + d])
    multiply(1, lane)
    forward(1, 0)
    sides_ready(1, 0)
    across_ready(1)

    for k in range(3):
        arrived(kvur.at[k], w_recv.at[19 + k])
    arrived(qups, w_recv.at[18])
    kvf[0:32, :] = kvup_ref[0:32, :] + kvur[0] + kvur[1] + kvur[2]
    arrived(kvr.at[1], m_recv.at[1])
    push(kvr.at[1], kvr.at[2], m_send.at[2], m_recv.at[2], dev(s, sib))
    arrived(kvr.at[0], m_recv.at[0])
    arrived(kvr.at[2], m_recv.at[2])
    arrived(lipr, m_recv.at[3])
    arrived(sqr, m_recv.at[4])

    def rotate(v, i):
        return v * cos_ref[i] + pltpu.roll(v, 64, 1) * sin_ref[i]

    def unrotate(v, i):
        return v * cos_ref[i] - pltpu.roll(v, 64, 1) * sin_ref[i]

    def project(i, carry):
        low_i = (acc_kd[i, :, 128:256] + lipr[i].astype(F32)).astype(BF16)
        low[i] = low_i
        q_i = (acc_q0[i] + sqr[i].astype(F32) + SCALE * dot(low_i, qup_ref[...])).astype(BF16)
        for hd in range(2):
            cols = slice(hd * 128, hd * 128 + 128)
            qs[hd, i] = rotate(q_i[:, cols].astype(F32), i).astype(BF16)
        own = acc_kd[i, :, 0:128] + kvr[0, i].astype(F32)
        other = kvr[1, i].astype(F32) + kvr[2, i].astype(F32)
        first = jnp.where(a == 0, own, other)
        second = jnp.where(a == 0, other, own)
        rank = SCALE * dot(low_i, kvf[...])
        k_i = jnp.concatenate([first[:, 0:64], second[:, 0:64]], axis=1) + rank[:, 0:128]
        v_i = jnp.concatenate([first[:, 64:128], second[:, 64:128]], axis=1) + rank[:, 128:256]
        start = pl.multiple_of(i * HALF, HALF)
        ks[pl.ds(start, HALF), :] = rotate(k_i.astype(BF16).astype(F32), i).astype(BF16)
        vs[pl.ds(start, HALF), :] = v_i.astype(BF16)
        return carry

    lax.fori_loop(0, 2, project, 0)

    for i in range(2):
        keys = (i + 1) * HALF

        def attend(hd, carry):
            scores = dot_nt(qs[hd, i], ks[0:keys, :]) * INV_ROOT
            row = lax.broadcasted_iota(jnp.int32, scores.shape, 0) + i * HALF
            col = lax.broadcasted_iota(jnp.int32, scores.shape, 1)
            e = jnp.where(col <= row, jnp.exp(scores), 0.0)
            full = e / jnp.sum(e, axis=-1, keepdims=True)
            probs[hd, i, :, 0:keys] = full
            att[hd, i] = dot(full.astype(BF16), vs[0:keys, :]).astype(BF16)
            return carry

        lax.fori_loop(0, 2, attend, 0)
    loti = jnp.concatenate(
        [
            dot_nt(od_ref[0:16, 0:128], att[0, i]) + dot_nt(od_ref[0:16, 128:256], att[1, i])
            for i in range(2)
        ],
        axis=1,
    )
    lot[...] = loti.astype(BF16)
    push(lot, lotr, m_send.at[7], m_recv.at[7], dev(s, sib))

    multiply_sides(1, 0)
    multiply(1, lane_of(1, 0))
    far_ready(1, 0)
    multiply(1, lane_of(0, 2))
    forward(1, 1)
    sides_ready(1, 1)
    multiply_sides(1, 1)
    far_ready(1, 1)
    multiply(1, lane_of(1, 2))
    sg[...] = acc_g1[...].astype(BF16)
    slg[...] = acc_lg[...].astype(BF16)
    push(slg, slgr, m_send.at[5], m_recv.at[5], dev(s, sib))
    push(sg, sgr, m_send.at[6], m_recv.at[6], dev(s, sib))

    arrived(slgr, m_recv.at[5])
    arrived(sgr, m_recv.at[6])

    def cotangent(i, carry):
        lg = (acc_lg[i] + slgr[i].astype(F32)).astype(BF16)
        lgs[i] = lg
        ga = (acc_g0[i] + sgr[i].astype(F32) + SCALE * dot(lg, od_ref[...])).astype(BF16)
        gas[0, i] = ga[:, 0:128]
        gas[1, i] = ga[:, 128:256]
        return carry

    lax.fori_loop(0, 2, cotangent, 0)
    dkacc[...] = jnp.zeros(dkacc.shape, F32)
    dvacc[...] = jnp.zeros(dvacc.shape, F32)

    def split_columns(kind, halves):
        for message, side in ((mown, a), (moth, 1 - a)):
            low_side = jnp.concatenate([half[:, 0:64] for half in halves], axis=1)
            high_side = jnp.concatenate([half[:, 64:128] for half in halves], axis=1)
            message[kind] = jnp.where(side == 0, low_side, high_side).astype(BF16)
        push(moth.at[kind], dkvr.at[1, kind], m_send.at[9 + 3 * kind], m_recv.at[9 + 3 * kind],
             dev(s, twin))
        push(mown.at[kind], dkvr.at[0, kind], m_send.at[11 + 3 * kind],
             m_recv.at[11 + 3 * kind], dev(s, sib))

    def pass_on(kind):
        arrived(dkvr.at[1, kind], m_recv.at[9 + 3 * kind])
        push(dkvr.at[1, kind], dkvr.at[2, kind], m_send.at[10 + 3 * kind],
             m_recv.at[10 + 3 * kind], dev(s, sib))

    for i in range(2):
        keys = (i + 1) * HALF
        for hd in range(2):
            dvacc[0:keys, :] += dot_tn(probs[hd, i, :, 0:keys].astype(BF16), gas[hd, i])
    split_columns(1, [dvacc[0:HALF, :], dvacc[HALF:ROWS, :]])
    for i in range(2):
        keys = (i + 1) * HALF
        for hd in range(2):
            full = probs[hd, i, :, 0:keys]
            grad = dot_nt(gas[hd, i], vs[0:keys, :])
            delta = jnp.sum(full * grad, axis=-1, keepdims=True)
            ds = (full * (grad - delta)).astype(BF16)
            dq = INV_ROOT * dot(ds, ks[0:keys, :])
            dq0[i, :, hd * 128 : hd * 128 + 128] = unrotate(dq, i).astype(BF16)
            dkacc[0:keys, :] += dot_tn(ds, qs[hd, i])
    push(dq0, dq1, m_send.at[8], m_recv.at[8], dev(s, sib))
    split_columns(
        0,
        [unrotate(INV_ROOT * dkacc[i * HALF : i * HALF + HALF, :], i) for i in range(2)],
    )
    pass_on(1)

    arrived(lotr, m_recv.at[7])
    low_out = (SCALE * (loti + lotr[...].astype(F32))).astype(BF16)

    def out_up(j, carry):
        total = jnp.zeros((16, BLK), F32)
        for i in range(2):
            total += dot(low_out[:, i * HALF : i * HALF + HALF], buf[1, j, i])
        ups[j] = total[0:8]
        return carry

    lax.fori_loop(0, LANES // 2, out_up, 0)

    kv_rows = kvf[0:32, :].astype(F32)
    kv_low = jnp.concatenate([kv_rows[:, 0:64], kv_rows[:, 128:192]], axis=1)
    kv_high = jnp.concatenate([kv_rows[:, 64:128], kv_rows[:, 192:256]], axis=1)
    kv_chip = jnp.where(a == 0, kv_low, kv_high).astype(BF16)
    kv_chip = jnp.concatenate([kv_chip, jnp.zeros((96, 128), BF16)], axis=0)
    sib_up = jnp.concatenate([qups[...], jnp.zeros((112, 256), BF16)], axis=0)

    pass_on(0)
    lax.fori_loop(LANES // 2, LANES, out_up, 0)
    arrived(dq1, m_recv.at[8])
    for kind in (1, 0):
        arrived(dkvr.at[2, kind], m_recv.at[10 + 3 * kind])
        arrived(dkvr.at[0, kind], m_recv.at[11 + 3 * kind])
    back_t = []
    for i in range(2):
        cols = slice(i * 64, i * 64 + 64)
        total = jnp.concatenate(
            [
                mown[kind].astype(F32)[:, cols] + dkvr[0, kind].astype(F32)[:, cols]
                + dkvr[1, kind].astype(F32)[:, cols] + dkvr[2, kind].astype(F32)[:, cols]
                for kind in range(2)
            ],
            axis=1,
        ).astype(BF16)
        back = SCALE * (
            dot_nt(dq0[i], qup_ref[...]) + dot_nt(dq1[i], sib_up) + dot_nt(total, kv_chip)
        )
        kb[i, :, 0:128] = total
        kb[i, :, 128:256] = back.astype(BF16)
        back_t.append(back.T[0:32, :])

    def dx_block(b, i):
        return dot_nt(dq0[i], wqa[b]) + dot_nt(dq1[i], wqb[b]) + dot(kb[i], wkv[b].reshape(256, BLK))

    def far_block(r):
        def one(i, carry):
            st[r, 0, i] = dx_block(lane_of(r, 2), i).astype(BF16)
            return carry

        lax.fori_loop(0, 2, one, 0)
        push(st.at[r, 0, 0], rsr.at[r, 0], rs_send.at[r, 0], rs_recv.at[r, 0], dev(s, right))
        push(st.at[r, 0, 1], rsr.at[r, 1], rs_send.at[r, 1], rs_recv.at[r, 1], dev(s, left))

    def side_cross(d, i, extra):
        k = 1 if d == 1 else 2
        total = dx_block(lane_of(1, d), i)
        arrived(rsr.at[1, extra], rs_recv.at[1, extra])
        total += rsr[1, extra].astype(F32)
        st[1, k, i] = total.astype(BF16)
        slot = 2 * k + 1 - i
        push(st.at[1, k, i], rsr.at[1, slot], rs_send.at[1, slot], rs_recv.at[1, slot], beyond[i])

    def side_next(d, i, slot):
        k = 1 if d == 1 else 2
        st[1, k, i] = dx_block(lane_of(1, d), i).astype(BF16)
        push(st.at[1, k, i], rsr.at[1, slot], rs_send.at[1, slot], rs_recv.at[1, slot],
             dev(s, right if d == 1 else left))

    def side_home(d, i, extra):
        k = 1 if d == 1 else 2
        slot = 2 * k + i
        total = dx_block(lane_of(0, d), i)
        if extra is not None:
            arrived(rsr.at[0, extra], rs_recv.at[0, extra])
            total += rsr[0, extra].astype(F32)
        else:
            arrived(rsr.at[1, slot], rs_recv.at[1, slot])
            total += rsr[1, slot].astype(F32)
        st[0, k, i] = total.astype(BF16)
        push(st.at[0, k, i], rsr.at[0, slot], rs_send.at[0, slot], rs_recv.at[0, slot],
             dev(s, right if d == 1 else left))

    far_block(1)

    back_full = jnp.concatenate(back_t, axis=1).astype(BF16)

    def adapters(j, carry):
        total = jnp.zeros((32, BLK), F32)
        for i in range(2):
            total += dot(back_full[:, i * HALF : i * HALF + HALF], buf[0, j, i])
        du[j, 0] = total[0:16].astype(BF16)
        du[j, 1] = jnp.concatenate([total[16:24], ups[j]], axis=0).astype(BF16)
        return carry

    lax.fori_loop(0, LANES, adapters, 0)
    for d in range(1, 16):
        lo, j = plane_peer(d)
        push(du.at[j, lo], r1buf.at[d - 1], s_send.at[0, d], s_recv.at[0, d],
             dev(z * 2 + lo, j * 2 + c))

    low_t = jnp.concatenate([low[i].astype(F32).T[0:32] for i in range(2)], axis=1).astype(BF16)
    lg_t = jnp.concatenate([lgs[i].astype(F32).T[0:16] for i in range(2)], axis=1).astype(BF16)
    query_up = jnp.zeros((32, 256), F32)
    kv_up = jnp.zeros((32, 128), F32)
    out_down = jnp.zeros((16, 256), F32)
    for i in range(2):
        cols = slice(i * HALF, i * HALF + HALF)
        query_up += dot(low_t[:, cols], dq0[i])
        kv_up += dot(low_t[:, cols], kb[i, :, 0:128])
        out_down += jnp.concatenate(
            [dot(lg_t[:, cols], att[0, i]), dot(lg_t[:, cols], att[1, i])], axis=1
        )
    lane_col = lax.broadcasted_iota(jnp.int32, (8, 128), 1)
    kv_grad = SCALE * jnp.where(lane_col < 64, kv_up[8:16], kv_up[16:24])
    alone = jnp.concatenate(
        [
            jnp.concatenate([SCALE * query_up[0:8], SCALE * out_down[0:8]], axis=1),
            jnp.concatenate([kv_grad, jnp.zeros((8, 384), F32)], axis=1),
        ],
        axis=0,
    ).astype(BF16)
    al[0] = alone[:, 0:256]
    al[1] = alone[:, 256:512]
    push(al.at[1 - k_lo], alr, s_send.at[4, 1], s_recv.at[4, 1], dev(z * 2 + 1 - k_lo, h))
    side_next(1, 1, 2)
    side_next(-1, 0, 5)
    far_block(0)
    side_cross(1, 0, 0)
    side_cross(-1, 1, 1)

    shared = du[lane, k_lo].astype(F32)
    for d in range(1, 16):
        arrived(r1buf.at[d - 1], s_recv.at[0, d])
        shared += r1buf[d - 1].astype(F32)
    arrived(alr, s_recv.at[4, 1])
    single = al[k_lo].astype(F32) + alr[...].astype(F32)
    for k in range(8):
        r, g = k // 4, k % 4
        pieces[k, 0] = shared[8 * r : 8 * r + 8, g * 128 : g * 128 + 128]
        r, g = k // 2, k % 2
        if k < 4:
            pieces[k, 1] = single[8 * r : 8 * r + 8, g * 128 : g * 128 + 128]
        else:
            pieces[k, 1] = jnp.zeros((8, 128), F32)
    for d in range(1, 8):
        owner = column_peer(d)
        push(pieces.at[owner], r2buf.at[d - 1], s_send.at[1, d], s_recv.at[1, d],
             dev(owner * 2 + k_lo, h))
    mine = pieces[z]
    for d in range(1, 8):
        arrived(r2buf.at[d - 1], s_recv.at[1, d])
        mine += r2buf[d - 1]
    tiles[place_in_plane] = mine[0]
    for d in range(1, 16):
        lo, j = plane_peer(d)
        push(tiles.at[place_in_plane], tiles.at[place_in_plane], s_send.at[2, d],
             s_recv.at[2, d], dev(z * 2 + lo, j * 2 + c))
    tiles[16 + k_lo] = mine[1]
    push(tiles.at[16 + k_lo], tiles.at[16 + k_lo], s_send.at[4, 2], s_recv.at[4, 2],
         dev(z * 2 + 1 - k_lo, h))

    for i, slot in ((0, 5), (1, 2)):
        total = dx_block(lane_of(1, 0), i)
        arrived(rsr.at[1, slot], rs_recv.at[1, slot])
        yst[i] = (total + rsr[1, slot].astype(F32)).astype(BF16)
        push(yst.at[i], yrecv.at[1 - i], y_send.at[2, i], y_recv.at[2, 1 - i], beyond[i])
    side_home(-1, 1, 1)
    side_home(1, 1, None)
    for d in range(1, 16):
        m = lax.rem(place_in_plane - d + 16, 16)
        arrived(tiles.at[m], s_recv.at[2, d])
    arrived(tiles.at[17 - k_lo], s_recv.at[4, 2])
    for k in range(9):
        eb[c, z, k] = jnp.concatenate([tiles[2 * k], tiles[2 * k + 1]], axis=0).astype(BF16)
    for d in range(1, 8):
        push(eb.at[c, z], eb.at[c, z], s_send.at[3, d], s_recv.at[3, d],
             dev(column_peer(d) * 2 + k_lo, h))
    side_home(1, 0, 0)
    side_home(-1, 0, None)
    after = lax.rem(s + 1, SEQ)

    def send_back():
        return remote(rollst, rollrecv, roll_send.at[2], roll_recv.at[2], dev(after, h))

    rolled_sends.append(send_back)
    for i in (1, 0):
        total = dx_block(lane, i)
        for k in (2, 4):
            arrived(rsr.at[0, k + i], rs_recv.at[0, k + i])
            total += rsr[0, k + i].astype(F32)
        arrived(yrecv.at[i], y_recv.at[2, i])
        rown[i] = total + yrecv[i].astype(F32)
        if i == 1:

            @pl.when(p == 1)
            def _():
                rollst[...] = rown[1].astype(BF16)
                send_back().start()

    for d in range(1, 8):
        arrived(eb.at[c, lax.rem(z - d + 8, 8)], s_recv.at[3, d])
    push(eb.at[c], eb.at[c], s_send.at[4, 0], s_recv.at[4, 0], dev(s, sib))
    for g in range(4):
        cols = slice(g * 128, g * 128 + 128)
        pair = eb[c, 4 + g, 4 + lane // 2].astype(F32)
        small_ref[0:8, cols] = jnp.where(lax.rem(lane, 2) == 0, pair[0:8], pair[8:16])
    for g in range(2):
        pair = eb[c, g, 8].astype(F32)
        small_ref[8:16, g * 128 : g * 128 + 128] = pair[0:8]
        small_ref[8:16, 256 + g * 128 : 384 + g * 128] = pair[8:16]
    kv_out = eb[c, 2, 8].astype(F32)[0:8]
    small_ref[16:24, :] = jnp.zeros((8, BLK), F32)
    small_ref[16:24, 0:64] = jnp.concatenate(
        [
            jnp.where(c == 0, kv_out[:, 0:32], kv_out[:, 32:64]),
            jnp.where(c == 0, kv_out[:, 64:96], kv_out[:, 96:128]),
        ],
        axis=1,
    )

    @pl.when(p == 0)
    def _():
        for i in range(2):
            dx_ref[i * HALF : i * HALF + HALF, :] = rown[i].astype(BF16)

    @pl.when(p == 1)
    def _():
        dx_ref[HALF:ROWS, :] = rown[0].astype(BF16)
        arrived(rollrecv, roll_recv.at[2])
        dx_ref[0:HALF, :] = rollrecv[...]

    arrived(eb.at[1 - c], s_recv.at[4, 0])

    def place(j, carry):
        for core in range(2):
            for g in range(4):
                cols = pl.ds(pl.multiple_of((2 * j + core) * BLK + g * 128, 128), 128)
                for r in range(3):
                    pair = eb[core, r % 2 * 4 + g, r // 2 * 4 + j // 2].astype(F32)
                    dgrad_ref[8 * r : 8 * r + 8, cols] = jnp.where(
                        lax.rem(j, 2) == 0, pair[0:8], pair[8:16]
                    )
        return carry

    lax.fori_loop(0, LANES, place, 0)

    for copy in sends:
        copy.wait_send()

    @pl.when(p == 1)
    def _():
        for copy in rolled_sends:
            copy().wait_send()


def finish(dx_ref, dgrad_ref, small_ref, out_dx, out_down, out_qg, out_kvg, out_odg, out_oug):
    out_dx[...] = dx_ref[...]
    for r in range(3):
        out_down[r] = dgrad_ref[r * RANK : (r + 1) * RANK, :]
    out_qg[...] = small_ref[8:16, 0:256]
    out_odg[...] = small_ref[8:16, 256:512]
    out_oug[...] = small_ref[0:8, :]
    out_kvg[:, 0, :] = small_ref[16:24, 0:32]
    out_kvg[:, 1, :] = small_ref[16:24, 32:64]


def body(normed, output_gradient, query_weight, key_value_weight, output_weight,
         adapter_down, query_up, key_value_up, output_down, output_up):
    h = lax.axis_index("head")
    s = lax.axis_index("seq")
    c = lax.rem(h, 2)
    p = h // 8
    width = adapter_down.shape[2]

    positions = lax.rem(
        s * ROWS + jnp.arange(ROWS, dtype=jnp.int32) + p * HALF, TOKENS
    ).astype(F32)
    half_dim = HEAD_SIZE // 2
    frequency = ROPE_BASE ** (-jnp.arange(half_dim, dtype=F32) * 2.0 / HEAD_SIZE)
    angles = positions[:, None] * frequency[None, :]
    cos, sin = jnp.cos(angles), jnp.sin(angles)
    cos = cos.reshape(2, HALF, half_dim)
    sin = sin.reshape(2, HALF, half_dim)

    kvt = key_value_weight.transpose(1, 2, 0)
    wq = query_weight.reshape(LANES, 2, BLK, 256)

    vm = lambda *shape: pltpu.VMEM(shape, BF16)
    vf = lambda *shape: pltpu.VMEM(shape, F32)
    dma = lambda *shape: pltpu.SemaphoreType.DMA(shape)
    out_shape = [
        jax.ShapeDtypeStruct((ROWS, BLK), BF16),
        jax.ShapeDtypeStruct((3 * RANK, width), F32),
        jax.ShapeDtypeStruct((3 * RANK, BLK), F32),
    ]
    hbm = pl.BlockSpec(memory_space=pl.ANY)
    vmem = pl.BlockSpec(memory_space=pltpu.VMEM)
    scratch = [
        vm(2, LANES, 2, HALF, BLK), vm(LANES, BLK, 256), vm(LANES, BLK, 256),
        vm(LANES, 4, 2, 32, BLK), vm(LANES, 256, BLK), vm(LANES, 256, BLK),
        vm(LANES, 128, BLK), vm(16, 256), vm(3, 32, 256), vm(128, 256),
        vm(128, 256), vm(32, 256), vm(128, 256), vm(16, BLK), vf(2, HALF, HEAD_SIZE),
        vf(2, HALF, HEAD_SIZE),
        vf(2, HALF, 256), vf(2, HALF, 256), vf(2, HALF, 256), vf(2, HALF, 256),
        vf(2, HALF, 256), vf(2, HALF, 128),
        vm(2, HALF, 256), vm(2, HALF, 256), vm(2, HALF, 128), vm(2, HALF, 128),
        vm(2, HALF, 128), vm(3, 2, HALF, 128), vm(2, HALF, 256), vm(2, HALF, 256),
        vm(2, HALF, 128), vm(2, HALF, 128),
        vf(2, 2, HALF, ROWS), vm(2, 2, HALF, 128), vm(ROWS, 128), vm(ROWS, 128),
        vm(2, 2, HALF, 128), vm(2, 2, HALF, 128), vm(2, HALF, 128), vm(2, HALF, 128),
        vf(ROWS, 128), vf(ROWS, 128),
        vm(2, HALF, 256), vm(2, HALF, 256), vm(2, HALF, 256), vm(16, ROWS), vm(16, ROWS),
        vm(2, HALF, 128), vm(2, HALF, 128), vm(3, 2, HALF, 128),
        vm(2, 3, 2, HALF, BLK), vm(2, 6, HALF, BLK), vf(2, HALF, BLK), vm(2, HALF, BLK),
        vm(2, HALF, BLK), vm(HALF, BLK), vm(HALF, BLK),
        vf(LANES, 8, BLK), vm(LANES, 2, 16, BLK), vm(15, 16, BLK), vm(2, 16, 256), vm(16, 256), vf(8, 2, 8, 128),
        vf(7, 2, 8, 128), vf(18, 8, 128), vm(2, 8, 9, 16, 128),
        dma(21), dma(30), dma(30), dma(2, 2, 6), dma(2, 2, 6), dma(3, 2), dma(3, 2),
        dma(3), dma(3), dma(15), dma(15), dma(2, 6), dma(2, 6), dma(5, 16), dma(5, 16),
    ]
    dx, dgrad, small = pl.pallas_call(
        kernel,
        out_shape=out_shape,
        in_specs=[hbm] * 5 + [vmem] * 7,
        out_specs=[vmem] * 3,
        scratch_shapes=scratch,
        compiler_params=pltpu.CompilerParams(
            collective_id=0, has_side_effects=True, vmem_limit_bytes=56 * 1024 * 1024
        ),
        cost_estimate=pl.CostEstimate(
            flops=9_000_000_000, bytes_accessed=20_000_000, transcendentals=400_000
        ),
    )(
        normed, output_gradient, wq, kvt, output_weight, adapter_down.reshape(3 * RANK, width),
        query_up, key_value_up, output_down, output_up, cos, sin,
    )
    return tuple(
        pl.pallas_call(
            finish,
            out_shape=[
                jax.ShapeDtypeStruct((ROWS, BLK), BF16),
                jax.ShapeDtypeStruct((3, RANK, width), F32),
                jax.ShapeDtypeStruct((RANK, 256), F32),
                jax.ShapeDtypeStruct((RANK, 2, 32), F32),
                jax.ShapeDtypeStruct((RANK, 256), F32),
                jax.ShapeDtypeStruct((RANK, BLK), F32),
            ],
            in_specs=[vmem] * 3,
            out_specs=[vmem] * 6,
        )(dx, dgrad, small)
    )


def solution(mesh):
    return jax.shard_map(
        body,
        mesh=mesh,
        in_specs=(
            P("seq", "head"), P("seq", "head"), P(None, "head"), P(None, None, "head"),
            P("head", None), P(), P(None, "head"), P(None, None, "head"),
            P(None, "head"), P(None, "head"),
        ),
        out_specs=(
            P("seq", "head"), P(), P(None, "head"), P(None, None, "head"),
            P(None, "head"), P(None, "head"),
        ),
        check_vma=False,
    )
```
